32 devices in a mesh: own: 8 (over y, x, core), dp: 4 (over z).
Axes of the slice: x: 2, y: 2, z: 4, core: 2. Of those that a mesh axis runs over, the one named last changes fastest.
Arguments:
- tokens: bfloat16 [8192, 640], P(('dp', 'own')), may hold values from -6 to 6
- cotangent: bfloat16 [8192, 640], P(('dp', 'own')), may hold values from -6 to 6
- lengths: int32 [4, 4], P('dp'), may hold values from 1 to 1024, 2048 in all within a row
- row_packed_slot: int32 [4, 2048], P('dp'), may hold values from 0 to 2047, as said below
- shared_attention_matrix: bfloat16 [640, 1536], P('own'), may hold values from -0.25 to 0.25
- shared_output_matrix: bfloat16 [1024, 640], P('own'), may hold values from -0.1875 to 0.1875
- shared_gate_up_matrix: bfloat16 [640, 4096], P('own'), may hold values from -0.25 to 0.25
- shared_down_matrix: bfloat16 [2048, 640], P('own'), may hold values from -0.125 to 0.125
- norm_gain_table: bfloat16 [4, 640], P(None, 'own'), may hold values from 0.25 to 1.75
- query_key_gains: bfloat16 [2, 256], P(None, 'own'), may hold values from 0.25 to 1.75
- adapter_attention_first: bfloat16 [2, 640, 768], P(None, 'own'), may hold values from -0.25 to 0.25
- adapter_query_second: bfloat16 [2, 256, 1024], P(None, 'own'), may hold values from -0.1875 to 0.1875
- adapter_key_value_second: bfloat16 [2, 2, 256, 256], P(None, None, 'own'), may hold values from -0.1875 to 0.1875
- adapter_output_first: bfloat16 [2, 1024, 256], P(None, 'own'), may hold values from -0.1875 to 0.1875
- adapter_output_second: bfloat16 [2, 256, 640], P(None, 'own'), may hold values from -0.1875 to 0.1875
- adapter_gate_first: bfloat16 [2, 640, 512], P(None, 'own'), may hold values from -0.25 to 0.25
- adapter_gate_second: bfloat16 [2, 2, 256, 2048], P(None, None, 'own'), may hold values from -0.1875 to 0.1875
- adapter_down_first: bfloat16 [2, 2048, 256], P(None, 'own'), may hold values from -0.125 to 0.125
- adapter_down_second: bfloat16 [2, 256, 640], P(None, 'own'), may hold values from -0.1875 to 0.1875
Outputs:
- mixed: bfloat16 [8192, 640], P(('dp', 'own'))
- tokens_grad: bfloat16 [8192, 640], P(('dp', 'own'))
- qkv_weight_grad: float32 [640, 1536], P('own')
- out_weight_grad: float32 [1024, 640], P('own')
- gate_up_weight_grad: float32 [640, 4096], P('own')
- down_weight_grad: float32 [2048, 640], P('own')
- norm_gains_grad: float32 [4, 640], P(None, 'own')
- qk_gains_grad: float32 [2, 256], P(None, 'own')
- lora_a_qkv_grad: float32 [2, 640, 768], P(None, 'own')
- lora_b_q_grad: float32 [2, 256, 1024], P(None, 'own')
- lora_b_kv_grad: float32 [2, 2, 256, 256], P(None, None, 'own')
- lora_a_out_grad: float32 [2, 1024, 256], P(None, 'own')
- lora_b_out_grad: float32 [2, 256, 640], P(None, 'own')
- lora_a_gu_grad: float32 [2, 640, 512], P(None, 'own')
- lora_b_gu_grad: float32 [2, 2, 256, 2048], P(None, None, 'own')
- lora_a_down_grad: float32 [2, 2048, 256], P(None, 'own')
- lora_b_down_grad: float32 [2, 256, 640], P(None, 'own')
The draws below stay inside these ranges and needn't reach their ends.
Inputs may be any that keep to these rules, and one draw needn't show every extreme that they name: The lengths of a group sum to 2048; its sequences fill slots 0 to 2047 in order. Each slot of a group appears once in its row of row_packed_slot. Rows 256 * j to 256 * j + 255 of a group lie on index j of own, and their slots all leave the same remainder when divided by 8.
All inputs are finite; a program needn't handle non-finite values.
Results may differ from the reference program's by a relative error of at most 0.029.
Values may be sent and summed in bfloat16 or wider, within the bound.
No kernel may reach another device: no remote copies, remote signals or barrier semaphores. Data moves between devices by JAX's collectives and lax.ppermute only.
A program may use at most 192 MiB of HBM per device.

```python
import math
import jax
import jax.numpy as jnp
import numpy as np
from jax import lax

MODEL_WIDTH = 640
QUERY_HEADS = 4
HEAD_SIZE = 256
FEEDFWD_HIDDEN = 2048
ADAPTER_RANK = 256
SEQS = 4
TOK_DEV = 256
GROUPS = 4
GROUP = 2048
TOKENS = 8192


def draw_row_packed_slot(key, part):
    key = jax.random.fold_in(key, 11)
    inner_key, outer_key = jax.random.split(key)
    owners = GROUP // TOK_DEV
    within = jax.vmap(lambda subkey: jax.random.permutation(subkey, TOK_DEV))(jax.random.split(inner_key, GROUPS * owners))
    residue = jax.vmap(lambda subkey: jax.random.permutation(subkey, owners))(jax.random.split(outer_key, GROUPS))
    slots = owners * within.reshape(GROUPS, owners, TOK_DEV) + residue[:, :, None]
    return slots.reshape(GROUPS, owners * TOK_DEV).astype(jnp.int32)


def levels(stream_key, dims, shards, low, top_value):
    loudness = 1.0
    for axis_at, blocks in shards:
        draws = jax.random.uniform(jax.random.fold_in(jax.random.fold_in(stream_key, 6), axis_at), (blocks,), jnp.float32, low / len(shards), top_value / len(shards))
        loudness = loudness * jnp.repeat(jnp.exp(draws), dims[axis_at] // blocks).reshape((-1,) + (1,) * (len(dims) - 1 - axis_at))
    return loudness


def length_profile(amount, total, reach, skew):
    portions = [(1 << 20) // math.isqrt(standing ** skew) + 1 for standing in range(2, amount + 1)]
    spare, holding = total - reach - (amount - 1), [1] * (amount - 1)
    while spare > 0:
        movable = [i for i in range(amount - 1) if holding[i] < reach]
        mass, left = sum([portions[i] for i in movable]), spare
        for i in movable:
            addition = min(reach - holding[i], max(1, left * portions[i] // mass), spare)
            holding[i] = holding[i] + addition
            spare = spare - addition
    return np.array([reach] + holding)


def uneven_parts(stream_key, amount, total, most, skew):
    if amount == 2:
        one = jax.random.randint(stream_key, (), max(1, total - most), min(most, total - 1) + 1)
        return jnp.stack([one, total - one])
    sizes = jnp.asarray(length_profile(amount, total, most, skew), jnp.int32)
    pairs = (amount - 1) // 2
    source_of, receiver = sizes[1:1 + 2 * pairs:2], sizes[2:2 + 2 * pairs:2]
    room = jnp.minimum(source_of - 1, most - receiver)
    moved = jax.random.randint(jax.random.fold_in(stream_key, 1), (pairs,), 0, 1 << 20) % (room + 1)
    sizes = sizes.at[1:1 + 2 * pairs:2].set(source_of - moved).at[2:2 + 2 * pairs:2].set(receiver + moved)
    return sizes[jax.random.permutation(jax.random.fold_in(stream_key, 2), amount)]


def bell_draw(rng, dims, spread, limit, shards=(), kind=jnp.bfloat16):
    values = jax.random.normal(rng, dims, jnp.float32) * spread
    if len(shards) > 0:
        values = levels(rng, dims, shards, -0.22, 0.18) * values
    return jnp.clip(values, min=-limit, max=limit).astype(kind)


def setup_inputs(seed: int = 0) -> dict:
    keys = jax.random.split(jax.random.key(seed), 20)
    return {
        "tokens": bell_draw(keys[0], (TOKENS, MODEL_WIDTH), 1.0, 6.0, ((0, 32),)),
        "cotangent": bell_draw(keys[1], (TOKENS, MODEL_WIDTH), 1.0, 6.0, ((0, 32),)),
        "lengths": jax.vmap(lambda own: uneven_parts(own, SEQS, GROUP, GROUP // 2, 2))(jax.random.split(keys[2], GROUPS)).reshape((GROUPS, SEQS)).astype(jnp.int32),
        "row_packed_slot": draw_row_packed_slot(jax.random.fold_in(keys[19], 71), 0),
        "shared_attention_matrix": bell_draw(keys[4], (MODEL_WIDTH, QUERY_HEADS * HEAD_SIZE + 2 * HEAD_SIZE), MODEL_WIDTH ** -0.5, 0.25, ((0, 8),)),
        "shared_output_matrix": bell_draw(keys[5], (QUERY_HEADS * HEAD_SIZE, MODEL_WIDTH), (QUERY_HEADS * HEAD_SIZE) ** -0.5, 0.1875, ((0, 8),)),
        "shared_gate_up_matrix": bell_draw(keys[6], (MODEL_WIDTH, 2 * FEEDFWD_HIDDEN), MODEL_WIDTH ** -0.5, 0.25, ((0, 8),)),
        "shared_down_matrix": bell_draw(keys[7], (FEEDFWD_HIDDEN, MODEL_WIDTH), FEEDFWD_HIDDEN ** -0.5, 0.125, ((0, 8),)),
        "norm_gain_table": jnp.clip(1.0 + 0.15 * jax.random.normal(keys[8], (4, MODEL_WIDTH), jnp.float32), 0.25, 1.75).astype(jnp.bfloat16),
        "query_key_gains": jnp.clip(1.0 + 0.15 * jax.random.normal(keys[9], (2, HEAD_SIZE), jnp.float32), 0.25, 1.75).astype(jnp.bfloat16),
        "adapter_attention_first": bell_draw(keys[10], (2, MODEL_WIDTH, 3 * ADAPTER_RANK), MODEL_WIDTH ** -0.5, 0.25, ((1, 8),)),
        "adapter_query_second": bell_draw(keys[11], (2, ADAPTER_RANK, QUERY_HEADS * HEAD_SIZE), (4 * ADAPTER_RANK) ** -0.5, 0.1875, ((1, 8),)),
        "adapter_key_value_second": bell_draw(keys[12], (2, 2, ADAPTER_RANK, HEAD_SIZE), (4 * ADAPTER_RANK) ** -0.5, 0.1875, ((2, 8),)),
        "adapter_output_first": bell_draw(keys[13], (2, QUERY_HEADS * HEAD_SIZE, ADAPTER_RANK), (QUERY_HEADS * HEAD_SIZE) ** -0.5, 0.1875, ((1, 8),)),
        "adapter_output_second": bell_draw(keys[14], (2, ADAPTER_RANK, MODEL_WIDTH), (4 * ADAPTER_RANK) ** -0.5, 0.1875, ((1, 8),)),
        "adapter_gate_first": bell_draw(keys[15], (2, MODEL_WIDTH, 2 * ADAPTER_RANK), MODEL_WIDTH ** -0.5, 0.25, ((1, 8),)),
        "adapter_gate_second": bell_draw(keys[16], (2, 2, ADAPTER_RANK, FEEDFWD_HIDDEN), (4 * ADAPTER_RANK) ** -0.5, 0.1875, ((2, 8),)),
        "adapter_down_first": bell_draw(keys[17], (2, FEEDFWD_HIDDEN, ADAPTER_RANK), FEEDFWD_HIDDEN ** -0.5, 0.125, ((1, 8),)),
        "adapter_down_second": bell_draw(keys[18], (2, ADAPTER_RANK, MODEL_WIDTH), (4 * ADAPTER_RANK) ** -0.5, 0.1875, ((1, 8),)),
    }


EPS = 1e-06
THETA = 1000000.0
MASKED = -1e+30
HIGH = lax.Precision.HIGHEST

@jax.custom_vjp
def low(v):
    return lax.optimization_barrier(v.astype(jnp.bfloat16)).astype(jnp.float32)

@jax.custom_vjp
def lowrank_backward(v):
    return v

def low_keep(v):
    return (low(v), None)

def low_pass(kept, grad):
    return (grad,)

def back_keep(v):
    return (v, None)

def back_low(kept, grad):
    return (low(grad),)
low.defvjp(low_keep, low_pass)
lowrank_backward.defvjp(back_keep, back_low)

def precise_product(left, right):
    return jnp.dot(left, right, precision=HIGH)

def rms_gain(values, gain):
    return values * lax.rsqrt(lax.optimization_barrier(jnp.mean(values * values, axis=-1, keepdims=True)) + EPS) * gain

def gated_gelu(gate_up_output):
    half_width = gate_up_output.shape[-1] // 2
    return jax.nn.gelu(gate_up_output[..., :half_width], approximate=True) * gate_up_output[..., half_width:]

def locate(slots, seq_lengths):
    ends = jnp.cumsum(seq_lengths).astype(jnp.int32)
    starts = ends - seq_lengths
    segment = lax.optimization_barrier(jnp.sum((slots[:, None] >= ends[None, :]).astype(jnp.int32), axis=1)).astype(jnp.int32)
    tree_member = segment[:, None] == jnp.arange(seq_lengths.shape[0], dtype=jnp.int32)[None, :]
    position = slots - lax.optimization_barrier(jnp.sum(jnp.where(tree_member, starts[None, :], 0), axis=1)).astype(jnp.int32)
    return (segment, position.astype(jnp.int32))

def rotary(position, head_extent):
    inverse = THETA ** (-jnp.arange(head_extent // 2, dtype=jnp.float32) * 2.0 / head_extent)
    angles = position.astype(jnp.float32)[:, None] * inverse[None, :]
    return (jnp.cos(angles), jnp.sin(angles))

def rotate(values, cos_table, sin_table):
    half_width = values.shape[-1] // 2
    leading = values[..., :half_width]
    trailing = values[..., half_width:]
    return jnp.concatenate([leading * cos_table - trailing * sin_table, trailing * cos_table + leading * sin_table], axis=-1)

def split_heads(attention_projected, qk_gain, cos_table, sin_table):
    head_extent = qk_gain.shape[1]
    query_span_width = attention_projected.shape[1] - 2 * head_extent
    query = attention_projected[:, :query_span_width].reshape(attention_projected.shape[0], query_span_width // head_extent, head_extent)
    key_rows = attention_projected[:, query_span_width:query_span_width + head_extent]
    value_rows = attention_projected[:, query_span_width + head_extent:]
    query = rotate(rms_gain(query, qk_gain[0]), cos_table[:, None, :], sin_table[:, None, :])
    key_rows = rotate(rms_gain(key_rows, qk_gain[1]), cos_table, sin_table)
    return (query, key_rows, value_rows)

def group_attention(query, key_rows, value_rows, segment, position):
    group_rows, head_count, head_extent = query.shape
    block_rows = math.gcd(group_rows, 512)
    softmax_scale = head_extent ** (-0.5)

    def one_block(pieces):
        query_block, seg_block, pos_block = pieces
        scores = lowrank_backward(jnp.einsum('thd,kd->thk', query_block, key_rows, precision=HIGH) * softmax_scale)
        allowed = ((seg_block[:, None] == segment[None, :]) & (position[None, :] <= pos_block[:, None]))[:, None, :]
        scores = jnp.where(allowed, scores, MASKED)
        highest = lax.optimization_barrier(jnp.max(scores, axis=-1, keepdims=True))
        totals = lax.optimization_barrier(jnp.sum(jnp.where(allowed, jnp.exp(scores - highest), 0.0), axis=-1, keepdims=True))
        probs = jnp.where(allowed, jnp.exp(scores - highest - jnp.log(totals)), 0.0)
        return jnp.einsum('thk,kd->thd', low(probs), value_rows, precision=HIGH)
    blocks = group_rows // block_rows
    result = lax.map(jax.checkpoint(one_block), (query.reshape(blocks, block_rows, head_count, head_extent), segment.reshape(blocks, block_rows), position.reshape(blocks, block_rows)))
    return result.reshape(group_rows, head_count * head_extent)

def block(stream_in, params, segment, position, cos_table, sin_table):
    attention_matrix, out_w, gate_up_matrix, down_w, norm_gain, qk_gain, qkv_a, query_up_factor, key_value_factor, out_a, out_b, gate_a, gate_up_factor, down_a, down_b = params
    adapter_rank = query_up_factor.shape[0]
    attention_input = low(rms_gain(stream_in, norm_gain[0]))
    attention_middle_part = low(lowrank_backward(precise_product(attention_input, qkv_a)))
    attention_projected = lowrank_backward(precise_product(attention_input, attention_matrix) + jnp.concatenate([precise_product(attention_middle_part[:, :adapter_rank], query_up_factor), precise_product(attention_middle_part[:, adapter_rank:2 * adapter_rank], key_value_factor[0]), precise_product(attention_middle_part[:, 2 * adapter_rank:], key_value_factor[1])], axis=1))
    query, key_rows, value_rows = split_heads(attention_projected, qk_gain, cos_table, sin_table)
    query, key_rows, value_rows = (low(query), low(key_rows), low(value_rows))
    pieces = []
    for group_index in range(GROUPS):
        window = slice(group_index * GROUP, (group_index + 1) * GROUP)
        pieces.append(group_attention(query[window], key_rows[window], value_rows[window], segment[group_index], position[group_index]))
    heads_out = lowrank_backward(low(jnp.concatenate(pieces, axis=0)))
    out_mid = low(lowrank_backward(precise_product(heads_out, out_a)))
    branch = lowrank_backward(precise_product(heads_out, out_w) + precise_product(out_mid, out_b))
    middle = stream_in + rms_gain(branch, norm_gain[1])
    feedforward_input = low(rms_gain(middle, norm_gain[2]))
    gate_middle_part = low(lowrank_backward(precise_product(feedforward_input, gate_a)))
    gate_up_output = lowrank_backward(precise_product(feedforward_input, gate_up_matrix) + jnp.concatenate([precise_product(gate_middle_part[:, :adapter_rank], gate_up_factor[0]), precise_product(gate_middle_part[:, adapter_rank:], gate_up_factor[1])], axis=1))
    hidden = low(gated_gelu(gate_up_output))
    down_mid = low(lowrank_backward(precise_product(hidden, down_a)))
    ffn_out = lowrank_backward(precise_product(hidden, down_w) + precise_product(down_mid, down_b))
    return middle + rms_gain(ffn_out, norm_gain[3])

def reference(tokens, cotangent, lengths, row_packed_slot, shared_attention_matrix, shared_output_matrix, shared_gate_up_matrix, shared_down_matrix, norm_gain_table, query_key_gains, adapter_attention_first, adapter_query_second, adapter_key_value_second, adapter_output_first, adapter_output_second, adapter_gate_first, adapter_gate_second, adapter_down_first, adapter_down_second):
    segments = []
    positions = []
    for group_index in range(GROUPS):
        segment, position = locate(row_packed_slot[group_index], lengths[group_index])
        segments.append(segment)
        positions.append(position)
    segment = jnp.stack(segments)
    position = jnp.stack(positions)
    cos_table, sin_table = rotary(position.reshape(-1), HEAD_SIZE)
    weight_collection = tuple((tree_member.astype(jnp.float32) for tree_member in (shared_attention_matrix, shared_output_matrix, shared_gate_up_matrix, shared_down_matrix, norm_gain_table, query_key_gains, adapter_attention_first, adapter_query_second, adapter_key_value_second, adapter_output_first, adapter_output_second, adapter_gate_first, adapter_gate_second, adapter_down_first, adapter_down_second)))

    def forward(stream_in, *params):
        shared = params[:6]
        middle = block(stream_in, shared + tuple((tree_member[0] for tree_member in params[6:])), segment, position, cos_table, sin_table)
        return block(middle, shared + tuple((tree_member[1] for tree_member in params[6:])), segment, position, cos_table, sin_table)
    stream_out, pull_back = jax.vjp(forward, tokens.astype(jnp.float32), *weight_collection)
    gradients = pull_back(cotangent.astype(jnp.float32))
    return (stream_out.astype(jnp.bfloat16), gradients[0].astype(jnp.bfloat16), gradients[1], gradients[2], gradients[3], gradients[4], gradients[5], gradients[6], gradients[7], gradients[8], gradients[9], gradients[10], gradients[11], gradients[12], gradients[13], gradients[14], gradients[15])
```

```python
import math

import jax
import jax.numpy as jnp
from jax import lax
from jax.experimental import pallas as pl
from jax.experimental.pallas import tpu as pltpu
from jax.sharding import PartitionSpec as P

BF = jnp.bfloat16
F32 = jnp.float32
EPS = 1e-06
THETA = 1000000.0
LANES = 128
LOG2E = 1.4426950408889634
VMEM_LIMIT = 60 * 2**20
PEAK = 1e6
CORE, XBIT, YBIT = 1, 2, 4


def dot(a, b):
    return jnp.dot(a, b, preferred_element_type=F32)


def dot_nt(a, b):
    return lax.dot_general(a, b, (((1,), (1,)), ((), ())), preferred_element_type=F32)


def dot_tn(a, b):
    return lax.dot_general(a, b, (((0,), (0,)), ((), ())), preferred_element_type=F32)


def side_by_side(parts):
    return parts[0] if len(parts) == 1 else jnp.concatenate(parts, axis=1)


def stacked(parts):
    return parts[0] if len(parts) == 1 else jnp.concatenate(parts, axis=0)


class Name(str):
    def __call__(self, *more):
        return Name(self + str().join(str(m) for m in more))


class Names:
    def __getattr__(self, name):
        return Name(name)


N = Names()


class Sizes:
    pass


class Layout:
    def __init__(self, sizes, names, gains=False):
        self.at = {}
        total = 0
        for name in names:
            rows, blocks = sizes.shard[name]
            self.at[name] = (total, rows, blocks)
            total += rows * blocks
        self.gains = None
        if gains:
            self.gains = total
            total += 16
        self.total = total


class Chunk:
    def __init__(self, layout, pieces, ids):
        self.layout, self.pieces, self.ids, self.mine = layout, pieces, ids, pieces[0]


class Env:
    def __init__(self):
        self.refs = {}
        self.pending = {}

    def __getitem__(self, name):
        return self.refs[name]

    def w(self, name):
        if name in self.pending:
            sem = self.pending.pop(name)
            ref = self.refs[N.w(name)]
            pltpu.make_async_copy(ref, ref, sem).wait()
        return self.refs[N.w(name)]


def run_kernel(sizes, name, stages, ins, outs, scratch=(), weights=(), smem=(), micros=0):
    chunks = []
    for _, chunk in weights:
        if chunk not in chunks:
            chunks.append(chunk)
    smem = dict(smem)
    for number, chunk in enumerate(chunks):
        smem[N.ids(number)] = chunk.ids
    scratch = dict(scratch)
    names_in = list(ins)
    names_smem = list(smem)
    pieces = [piece for chunk in chunks for piece in chunk.pieces]
    names_out = list(outs)
    names_scratch = list(scratch)
    shapes = []
    for wname, chunk in weights:
        if wname == N.gains:
            shapes.append(((sizes.slots, 16, LANES), BF))
        else:
            _, rows, blocks = chunk.layout.at[wname]
            shapes.append(((blocks, rows * sizes.slots, LANES), BF))

    def kernel(*refs):
        env = Env()
        position = 0
        for key in names_smem + names_in:
            env.refs[key] = refs[position]
            position += 1
        piece_refs = refs[position : position + len(pieces)]
        position += len(pieces)
        for key in names_out + names_scratch:
            env.refs[key] = refs[position]
            position += 1
        of_chunk = {}
        start = 0
        for number, chunk in enumerate(chunks):
            of_chunk[number] = piece_refs[start : start + len(chunk.pieces)]
            start += len(chunk.pieces)
        for number, (wname, chunk) in enumerate(weights):
            buffer = refs[position]
            position += 1
            env.refs[N.w(wname)] = buffer
        for number, (wname, chunk) in enumerate(weights):
            sem = refs[position]
            position += 1
            buffer = env.refs[N.w(wname)]
            which = chunks.index(chunk)
            for slot in range(sizes.slots):
                piece = of_chunk[which][0 if len(chunk.pieces) == 1 else slot]
                offset = slot * chunk.layout.total if len(chunk.pieces) == 1 else 0
                if wname == N.gains:
                    source = piece.at[pl.ds(offset + chunk.layout.gains, 16), :]
                    target = buffer.at[slot]
                else:
                    first, rows, blocks = chunk.layout.at[wname]
                    first = offset + first
                    source = piece.at[pl.ds(first, blocks * rows), :].reshape(blocks, rows, LANES)
                    if sizes.slots == 1:
                        target = buffer
                    else:
                        row = pl.multiple_of(env[N.ids(which)][slot] * rows, 16)
                        target = buffer.at[:, pl.ds(row, rows), :]
                pltpu.make_async_copy(source, target, sem).start()
            env.pending[wname] = sem
        env.ids = lambda chunk: env[N.ids(chunks.index(chunk))]
        for stage in stages:
            stage(env)
        for wname, _ in weights:
            env.w(wname)

    any_space = pl.BlockSpec(memory_space=pl.ANY)
    vmem = pl.BlockSpec(memory_space=pltpu.VMEM)
    nbytes = sum(math.prod(a.shape) * a.dtype.itemsize for a in list(ins.values()) + pieces)
    nbytes += sum(math.prod(s) * jnp.dtype(d).itemsize for s, d in outs.values())
    results = pl.pallas_call(
        kernel,
        name=name,
        out_shape=[jax.ShapeDtypeStruct(*outs[key]) for key in names_out],
        in_specs=[pl.BlockSpec(memory_space=pltpu.SMEM)] * len(names_smem)
        + [vmem] * len(names_in)
        + [any_space] * len(pieces),
        out_specs=[vmem] * len(names_out),
        scratch_shapes=[pltpu.VMEM(*scratch[key]) for key in names_scratch]
        + [pltpu.VMEM(*shape) for shape in shapes]
        + [pltpu.SemaphoreType.DMA] * len(weights),
        compiler_params=pltpu.CompilerParams(vmem_limit_bytes=VMEM_LIMIT),
        cost_estimate=pl.CostEstimate(flops=int(micros * PEAK), bytes_accessed=0, transcendentals=0),
    )(*smem.values(), *ins.values(), *pieces)
    return dict(zip(names_out, results))


def columns(weight, first, count, rows=None):
    if rows is None:
        return side_by_side([weight[first + i] for i in range(count)])
    return side_by_side([weight[first + i, rows] for i in range(count)])


def root(values):
    return lax.rsqrt(jnp.mean(values * values, axis=-1, keepdims=True) + EPS)


def rms_back(values, gain, grad):
    r = root(values)
    scaled = grad * gain
    back = r * scaled - values * (r * r * r * jnp.mean(values * scaled, axis=-1, keepdims=True))
    return back, jnp.sum(values * r * grad, axis=0, keepdims=True)


def rotate(values, cos, sin):
    half = values.shape[-1] // 2
    p, q = values[:, :half], values[:, half:]
    return jnp.concatenate([p * cos - q * sin, q * cos + p * sin], axis=1)


def rotate_back(grad, cos, sin):
    half = grad.shape[-1] // 2
    a, b = grad[:, :half], grad[:, half:]
    return jnp.concatenate([a * cos + b * sin, b * cos - a * sin], axis=1)


GELU_A = math.sqrt(2.0 / math.pi)
GELU_B = 0.044715


def gelu_parts(v):
    t = jnp.tanh(GELU_A * (v + GELU_B * v * v * v))
    return 0.5 * v * (1.0 + t), t


def gelu_slope(v, t):
    return 0.5 * (1.0 + t) + 0.5 * v * (1.0 - t * t) * (GELU_A * (1.0 + 3.0 * GELU_B * v * v))


def stage_gains(sizes, chunk):
    def stage(env):
        blocks = env.w(N.gains)
        ids = env.ids(chunk)
        norm = jnp.zeros((16, sizes.D), F32)
        heads = jnp.zeros((16, sizes.HD), F32)
        width, head_width = sizes.D // sizes.slots, sizes.HD // sizes.slots

        def pick(total, each, index):
            a = lax.broadcasted_iota(jnp.int32, (LANES, total), 0)
            b = lax.broadcasted_iota(jnp.int32, (LANES, total), 1)
            return jnp.where((b == a + index * each) & (a < each), 1.0, 0.0).astype(BF)

        for m in range(sizes.slots):
            norm = norm + dot(blocks[m], pick(sizes.D, width, ids[m]))
            heads = heads + dot(blocks[m], pick(sizes.HD, head_width, ids[m]))
        env[N.norm][...] = norm
        env[N.qkg][...] = heads

    return stage


def stage_qkv(sizes, l, stream):
    def stage(env):
        x = env[stream][...]
        attn_in = (x * root(x) * env[N.norm][0:1, :]).astype(BF)
        env[N.attn_in(l)][...] = attn_in
        first = env.w(N.aqkv)
        mids = []
        for j in range(3):
            mid = dot(attn_in, columns(first, sizes.RB * j, sizes.RB)).astype(BF)
            env[N.mid(l)][j] = mid
            mids.append(mid)
        qkv, hb = env.w(N.qkv), sizes.HB
        cos, sin = env[N.cos][...], env[N.sin][...]
        gq, gk = env[N.qkg][4:5, :], env[N.qkg][5:6, :]
        bk, bv, bq = env.w(N.bk), env.w(N.bv), env.w(N.bq)
        raw = dot(attn_in, columns(qkv, hb * sizes.H, hb)) + dot(mids[1], columns(bk, 0, hb))
        env[N.raw(l)][sizes.H] = raw
        env[N.kv(l)][:, : sizes.HD] = rotate(raw * root(raw) * gk, cos, sin).astype(BF)
        raw = dot(attn_in, columns(qkv, hb * (sizes.H + 1), hb)) + dot(mids[2], columns(bv, 0, hb))
        env[N.kv(l)][:, sizes.HD :] = raw.astype(BF)
        for h in range(sizes.H):
            raw = dot(attn_in, columns(qkv, hb * h, hb)) + dot(mids[0], columns(bq, hb * h, hb))
            env[N.raw(l)][h] = raw
            env[N.q(l)][h] = rotate(raw * root(raw) * gq, cos, sin).astype(BF)

    return stage


def key_block(sizes, pieces, b, value):
    lanes = slice(sizes.HD, 2 * sizes.HD) if value else slice(0, sizes.HD)
    rows = pl.ds(pl.multiple_of(b * sizes.IB, 16), sizes.IB)
    parts = []
    for piece in pieces:
        if len(piece.shape) == 3:
            parts += [piece[g, rows, lanes] for g in range(piece.shape[0])]
        else:
            parts.append(piece[rows, lanes])
    return stacked(parts)


def query_limits(sizes, env, qb):
    rows = slice(qb * sizes.QB, (qb + 1) * sizes.QB)
    slot = jnp.concatenate([env[N.qslot][rows, :]] * sizes.H, axis=0)
    low = jnp.concatenate([env[N.qstart][rows, :]] * sizes.H, axis=0)
    last = (qb + 1) * sizes.QB // sizes.IB
    return rows, slot, low, last


def stage_attend(sizes, l):
    scale = sizes.HD ** (-0.5) * LOG2E
    M = sizes.H * sizes.QB

    def stage(env):
        pieces = [env[N.kvp(l, i)] for i in range(sizes.kv_pieces)]
        for qb in range(sizes.T // sizes.QB):
            rows, slot, low, last = query_limits(sizes, env, qb)
            query = env[N.q(l)][:, rows, :].reshape(M, sizes.HD)
            env[N.o_acc][...] = jnp.zeros((M, sizes.HD), F32)
            env[N.l_acc][...] = jnp.zeros((M, LANES), F32)

            def body(b, carry):
                keys = env[N.kslot][b]
                scores = dot_nt(query, key_block(sizes, pieces, b, False))
                allowed = (keys <= slot) & (keys >= low)
                probs = jnp.where(allowed, jnp.exp2(scores * scale), 0.0)
                part = probs[:, :LANES]
                for i in range(1, probs.shape[1] // LANES):
                    part = part + probs[:, i * LANES : (i + 1) * LANES]
                env[N.l_acc][...] += part
                env[N.o_acc][...] += dot(probs.astype(BF), key_block(sizes, pieces, b, True))
                return carry

            lax.fori_loop(env[N.first_block][qb], last, body, 0)
            total = jnp.sum(env[N.l_acc][...], axis=1, keepdims=True)
            env[N.att(l)][:, rows, :] = (env[N.o_acc][...] / total).reshape(sizes.H, sizes.QB, sizes.HD)
            env[N.lse(l)][:, rows, :] = jnp.broadcast_to(jnp.log2(total), (M, LANES)).reshape(
                sizes.H, sizes.QB, LANES
            )

    return stage


def stage_out(sizes, l, stream):
    def stage(env):
        outa, outw, outb = env.w(N.outa), env.w(N.outw), env.w(N.outb)
        mid = jnp.zeros((sizes.T, sizes.R), F32)
        branch = jnp.zeros((sizes.T, sizes.D), F32)
        for h in range(sizes.H):
            heads = env[N.att(l)][h].astype(BF)
            env[N.ho(l)][h] = heads
            rows = slice(h * sizes.HD, (h + 1) * sizes.HD)
            mid = mid + dot(heads, columns(outa, 0, sizes.RB, rows))
            branch = branch + dot(heads, columns(outw, 0, sizes.DB, rows))
        mid = mid.astype(BF)
        env[N.omid(l)][...] = mid
        branch = branch + dot(mid, columns(outb, 0, sizes.DB))
        env[N.branch(l)][...] = branch
        middle = env[stream][...] + branch * root(branch) * env[N.norm][1:2, :]
        env[N.middle(l)][...] = middle
        env[N.ffn_in(l)][...] = (middle * root(middle) * env[N.norm][2:3, :]).astype(BF)

    return stage


def stage_ffn(sizes, l):
    def stage(env):
        x = env[N.ffn_in(l)][...]
        agu = env.w(N.agu)
        mids = []
        for j in range(2):
            mid = dot(x, columns(agu, sizes.RB * j, sizes.RB)).astype(BF)
            env[N.gmid(l)][j] = mid
            mids.append(mid)
        bg, bu, gu = env.w(N.bg), env.w(N.bu), env.w(N.gu)
        dnw, dna = env.w(N.dnw), env.w(N.dna)
        blocks = sizes.F // 256
        out = jnp.zeros((sizes.T, sizes.D), F32)
        down = jnp.zeros((sizes.T, sizes.R), F32)
        for b in range(blocks):
            gate = dot(x, columns(gu, 2 * b, 2)) + dot(mids[0], columns(bg, 2 * b, 2))
            up = dot(x, columns(gu, 2 * (blocks + b), 2)) + dot(mids[1], columns(bu, 2 * b, 2))
            env[N.gu(l)][b, :, :256] = gate
            env[N.gu(l)][b, :, 256:] = up
            hidden = (gelu_parts(gate)[0] * up).astype(BF)
            env[N.hidden(l)][b] = hidden
            rows = slice(b * 256, (b + 1) * 256)
            out = out + dot(hidden, columns(dnw, 0, sizes.DB, rows))
            down = down + dot(hidden, columns(dna, 0, sizes.RB, rows))
        down = down.astype(BF)
        env[N.dmid(l)][...] = down
        out = out + dot(down, columns(env.w(N.dnb), 0, sizes.DB))
        env[N.ffn_out(l)][...] = out
        env[N.stream(l + 1)][...] = env[N.middle(l)][...] + out * root(out) * env[N.norm][3:4, :]

    return stage


def stage_ffn_back(sizes, l, grad):
    def stage(env):
        out_grad = env[grad][...]
        back, gain = rms_back(env[N.ffn_out(l)][...], env[N.norm][3:4, :], out_grad)
        env[N.dnorm(l, 3)][...] = gain
        low = back.astype(BF)
        env[N.ffn_low(l)][...] = low
        dmg = dot_nt(low, columns(env.w(N.dnb), 0, sizes.DB)).astype(BF)
        env[N.dmg(l)][...] = dmg
        dnw, dna, bg, bu, gu = env.w(N.dnw), env.w(N.dna), env.w(N.bg), env.w(N.bu), env.w(N.gu)
        blocks = sizes.F // 256
        gate_mid = jnp.zeros((sizes.T, sizes.R), F32)
        up_mid = jnp.zeros((sizes.T, sizes.R), F32)
        total = jnp.zeros((sizes.T, sizes.D), F32)
        for b in range(blocks):
            rows = slice(b * 256, (b + 1) * 256)
            hidden_grad = dot_nt(low, columns(dnw, 0, sizes.DB, rows)) + dot_nt(
                dmg, columns(dna, 0, sizes.RB, rows)
            )
            gate, up = env[N.gu(l)][b, :, :256], env[N.gu(l)][b, :, 256:]
            value, t = gelu_parts(gate)
            gate_grad = (hidden_grad * up * gelu_slope(gate, t)).astype(BF)
            up_grad = (hidden_grad * value).astype(BF)
            env[N.gug(l)][b] = gate_grad
            env[N.gug(l)][blocks + b] = up_grad
            gate_mid = gate_mid + dot_nt(gate_grad, columns(bg, 2 * b, 2))
            up_mid = up_mid + dot_nt(up_grad, columns(bu, 2 * b, 2))
            total = total + dot_nt(gate_grad, columns(gu, 2 * b, 2))
            total = total + dot_nt(up_grad, columns(gu, 2 * (blocks + b), 2))
        agu = env.w(N.agu)
        for j, mid in enumerate((gate_mid, up_mid)):
            mid = mid.astype(BF)
            env[N.gmg(l)][j] = mid
            total = total + dot_nt(mid, columns(agu, sizes.RB * j, sizes.RB))
        back, gain = rms_back(env[N.middle(l)][...], env[N.norm][2:3, :], total)
        env[N.dnorm(l, 2)][...] = gain
        env[N.mgrad(l)][...] = out_grad + back

    return stage


def stage_out_back(sizes, l):
    def stage(env):
        back, gain = rms_back(env[N.branch(l)][...], env[N.norm][1:2, :], env[N.mgrad(l)][...])
        env[N.dnorm(l, 1)][...] = gain
        low = back.astype(BF)
        env[N.blow(l)][...] = low
        omg = dot_nt(low, columns(env.w(N.outb), 0, sizes.DB)).astype(BF)
        env[N.omg(l)][...] = omg
        outw, outa = env.w(N.outw), env.w(N.outa)
        for h in range(sizes.H):
            rows = slice(h * sizes.HD, (h + 1) * sizes.HD)
            grad = dot_nt(low, columns(outw, 0, sizes.DB, rows)) + dot_nt(omg, columns(outa, 0, sizes.RB, rows))
            env[N.hgrad(l)][h] = grad.astype(BF)

    return stage


def stage_attend_back(sizes, l):
    factor = sizes.HD ** (-0.5)
    scale = factor * LOG2E
    M = sizes.H * sizes.QB
    HD = sizes.HD

    def stage(env):
        pieces = [env[N.kvp(l, i)] for i in range(sizes.kv_pieces)]
        total_blocks = sizes.T // sizes.IB
        for b in range(total_blocks):
            env[N.dkv_acc][b] = jnp.zeros((sizes.n * sizes.IB, 2 * HD), F32)
        for qb in range(sizes.T // sizes.QB):
            rows, slot, low, last = query_limits(sizes, env, qb)
            query = env[N.q(l)][:, rows, :].reshape(M, HD)
            grad = env[N.hgrad(l)][:, rows, :].reshape(M, HD)
            attended = env[N.att(l)][:, rows, :].reshape(M, HD)
            row_dot = jnp.sum(grad.astype(F32) * attended, axis=1, keepdims=True)
            lse = env[N.lse(l)][:, rows, :].reshape(M, LANES)[:, 0:1]
            env[N.o_acc][...] = jnp.zeros((M, HD), F32)

            def body(b, carry):
                keys = env[N.kslot][b]
                k = key_block(sizes, pieces, b, False)
                v = key_block(sizes, pieces, b, True)
                allowed = (keys <= slot) & (keys >= low)
                probs = jnp.where(allowed, jnp.exp2(dot_nt(query, k) * scale - lse), 0.0)
                scores_grad = (probs * (dot_nt(grad, v) - row_dot)).astype(BF)
                env[N.o_acc][...] += dot(scores_grad, k)
                env[N.dkv_acc][b, :, :HD] += dot_tn(scores_grad, query)
                env[N.dkv_acc][b, :, HD:] += dot_tn(probs.astype(BF), grad)
                return carry

            lax.fori_loop(env[N.first_block][qb], last, body, 0)
            env[N.dq(l)][:, rows, :] = (env[N.o_acc][...] * factor).reshape(sizes.H, sizes.QB, HD)
        IB = sizes.IB
        for m in range(sizes.n):
            if sizes.slots > 1:
                where = (N.dkvkeep if m < sizes.n // 2 else N.dkvsend, m % (sizes.n // 2))
            else:
                where = (N.dkvkeep, m)
            for b in range(total_blocks):
                for j, by in enumerate((factor, 1.0)):
                    lanes = slice(j * HD, (j + 1) * HD)
                    part = env[N.dkv_acc][b, m * IB : (m + 1) * IB, lanes]
                    env[where[0](l)][where[1], b * IB : (b + 1) * IB, lanes] = (part * by).astype(BF)

    return stage


def stage_q_back(sizes, l):
    def stage(env):
        cos, sin = env[N.cos][...], env[N.sin][...]
        gq = env[N.qkg][4:5, :]
        hb = sizes.HB
        qkv, bq, aqkv = env.w(N.qkv), env.w(N.bq), env.w(N.aqkv)
        gains = jnp.zeros((1, sizes.HD), F32)
        mid = jnp.zeros((sizes.T, sizes.R), F32)
        total = jnp.zeros((sizes.T, sizes.D), F32)
        for h in range(sizes.H):
            turned = rotate_back(env[N.dq(l)][h], cos, sin)
            back, gain = rms_back(env[N.raw(l)][h], gq, turned)
            gains = gains + gain
            low = back.astype(BF)
            env[N.rawq_low(l)][h] = low
            mid = mid + dot_nt(low, columns(bq, hb * h, hb))
            total = total + dot_nt(low, columns(qkv, hb * h, hb))
        mid = mid.astype(BF)
        env[N.midgq(l)][...] = mid
        total = total + dot_nt(mid, columns(aqkv, 0, sizes.RB))
        env[N.agrad(l)][...] = total
        env[N.dqg(l)][...] = gains

    return stage


def stage_kv_back(sizes, l, stream, result):
    def stage(env):
        cos, sin = env[N.cos][...], env[N.sin][...]
        hb = sizes.HB
        qkv, aqkv = env.w(N.qkv), env.w(N.aqkv)
        turned = rotate_back(env[N.dkv][:, : sizes.HD].astype(F32), cos, sin)
        back, gain = rms_back(env[N.raw(l)][sizes.H], env[N.qkg][5:6, :], turned)
        env[N.dkg(l)][...] = gain
        total = env[N.agrad(l)][...]
        for j, (low, second) in enumerate(((back.astype(BF), N.bk), (env[N.dkv][:, sizes.HD :], N.bv))):
            env[N.rawkv_low(l)][j] = low
            mid = dot_nt(low, columns(env.w(second), 0, hb)).astype(BF)
            env[N.midgkv(l)][j] = mid
            total = total + dot_nt(low, columns(qkv, hb * (sizes.H + j), hb))
            total = total + dot_nt(mid, columns(aqkv, sizes.RB * (j + 1), sizes.RB))
        back, gain = rms_back(env[stream][...], env[N.norm][0:1, :], total)
        env[N.dnorm(l, 0)][...] = gain
        env[result][...] = env[N.mgrad(l)][...] + back

    return stage


def put(sizes, env, layout, prefix, name, block, value, first_row=0):
    first, rows, _ = layout.at[name]
    count = value.shape[1] // LANES
    keep = env[N.keep(prefix)]
    if sizes.slots == 1:
        value = value.astype(BF)
        for i in range(count):
            at = first + (block + i) * rows + first_row
            keep[0, at : at + value.shape[0], :] = value[:, i * LANES : (i + 1) * LANES]
        return
    send = env[N.send(prefix)]
    core, chip = env[N.place][0], env[N.place][1]
    even_stays = core == 0
    for pair in range(value.shape[0] // (2 * rows)):
        a = value[2 * pair * rows : (2 * pair + 1) * rows]
        b = value[(2 * pair + 1) * rows : (2 * pair + 2) * rows]
        stays = jnp.where(even_stays, a, b).astype(BF)
        goes = jnp.where(even_stays, b, a).astype(BF)
        slot = jnp.bitwise_xor(first_row // (2 * rows) + pair, chip)
        for i in range(count):
            at = first + (block + i) * rows
            keep[slot, at : at + rows, :] = stays[:, i * LANES : (i + 1) * LANES]
            send[slot, at : at + rows, :] = goes[:, i * LANES : (i + 1) * LANES]


def grad_product(sizes, env, layout, prefix, name, lefts, rights, first_block=0, first_row=0):
    left = stacked([a.T if len(lefts) == 1 else a.T for a in lefts]) if len(lefts) == 1 else side_by_side(
        [a.T for a in lefts]
    )
    for block, right in rights:
        value = dot(left, stacked(right))
        put(sizes, env, layout, prefix, name, first_block + block, value, first_row)


def wide(ref, width, step=256):
    out = []
    at = 0
    while at < width:
        size = min(step, width - at)
        out.append((at // LANES, slice(at, at + size)))
        at += size
    return out


def grads_ffn_wide(sizes, env, layout, prefix, names, loops, pl_l):
    blocks = sizes.F // 256
    for j, name in enumerate((N.gug, N.guu)):
        if name in names:
            left = [env[N.ffn_in(l)][...] for l in loops]
            rights = [(2 * b, [env[N.gug(l)][j * blocks + b] for l in loops]) for b in range(blocks)]
            grad_product(sizes, env, layout, prefix, name, left, rights)
    if N.agu in names:
        rights = [(sizes.RB * j, [env[N.gmg(pl_l)][j]]) for j in range(2)]
        grad_product(sizes, env, layout, prefix, N.agu, [env[N.ffn_in(pl_l)][...]], rights)
    for j, name in enumerate((N.bg, N.bu)):
        if name in names:
            rights = [(2 * b, [env[N.gug(pl_l)][j * blocks + b]]) for b in range(blocks)]
            grad_product(sizes, env, layout, prefix, name, [env[N.gmid(pl_l)][j]], rights)


def grads_ffn_down(sizes, env, layout, prefix, names, loops, pl_l):
    blocks = sizes.F // 256
    step = 512
    for b in range(0, blocks, 2):
        row = b * 256
        if N.dnw in names:
            left = [side_by_side([env[N.hidden(l)][b], env[N.hidden(l)][b + 1]]) for l in loops]
            rights = [(i, [env[N.ffn_low(l)][:, s] for l in loops]) for i, s in wide(None, sizes.D, 640)]
            grad_product(sizes, env, layout, prefix, N.dnw, left, rights, 0, row)
        if N.dna in names:
            left = [side_by_side([env[N.hidden(pl_l)][b], env[N.hidden(pl_l)][b + 1]])]
            grad_product(sizes, env, layout, prefix, N.dna, left, [(0, [env[N.dmg(pl_l)][...]])], 0, row)
    if N.dnb in names:
        grad_product(
            sizes, env, layout, prefix, N.dnb, [env[N.dmid(pl_l)][...]], [(0, [env[N.ffn_low(pl_l)][...]])]
        )


def grads_out(sizes, env, layout, prefix, names, loops, pl_l):
    for h in range(0, sizes.H, 2):
        row = h * sizes.HD
        if N.outw in names:
            left = [side_by_side([env[N.ho(l)][h], env[N.ho(l)][h + 1]]) for l in loops]
            grad_product(
                sizes, env, layout, prefix, N.outw, left, [(0, [env[N.blow(l)][...] for l in loops])], 0, row
            )
        if N.outa in names:
            left = [side_by_side([env[N.ho(pl_l)][h], env[N.ho(pl_l)][h + 1]])]
            grad_product(sizes, env, layout, prefix, N.outa, left, [(0, [env[N.omg(pl_l)][...]])], 0, row)
    if N.outb in names:
        grad_product(
            sizes, env, layout, prefix, N.outb, [env[N.omid(pl_l)][...]], [(0, [env[N.blow(pl_l)][...]])]
        )


def grads_qkv(sizes, env, layout, prefix, names, loops, pl_l):
    hb = sizes.HB
    left = [env[N.attn_in(l)][...] for l in loops] if {N.qkvq, N.qkvkv} & set(names) else None
    if N.qkvq in names:
        rights = [(hb * h, [env[N.rawq_low(l)][h] for l in loops]) for h in range(sizes.H)]
        grad_product(sizes, env, layout, prefix, N.qkvq, left, rights)
    if N.qkvkv in names:
        rights = [(hb * j, [env[N.rawkv_low(l)][j] for l in loops]) for j in range(2)]
        grad_product(sizes, env, layout, prefix, N.qkvkv, left, rights)
    first = ([(0, N.midgq(pl_l), None)] if {N.aqkv, N.aqkvq} & set(names) else []) + (
        [(sizes.RB * j, N.midgkv(pl_l), j) for j in range(2)] if {N.aqkv, N.aqkvkv} & set(names) else []
    )
    for name in (N.aqkv, N.aqkvq, N.aqkvkv):
        if name in names:
            rights = [
                (at + (sizes.RB if name == N.aqkv and j is not None else 0), [env[ref][...] if j is None else env[ref][j]])
                for at, ref, j in first
            ]
            grad_product(sizes, env, layout, prefix, name, [env[N.attn_in(pl_l)][...]], rights)
    if N.bq in names:
        rights = [(hb * h, [env[N.rawq_low(pl_l)][h]]) for h in range(sizes.H)]
        grad_product(sizes, env, layout, prefix, N.bq, [env[N.mid(pl_l)][0]], rights)
    for j, name in enumerate((N.bk, N.bv)):
        if name in names:
            grad_product(
                sizes, env, layout, prefix, name, [env[N.mid(pl_l)][j + 1]], [(0, [env[N.rawkv_low(pl_l)][j]])]
            )


def stage_grads(sizes, parts):
    def stage(env):
        for prefix, layout, names, loops, pl_l in parts:
            for build in (grads_ffn_wide, grads_ffn_down, grads_out, grads_qkv):
                build(sizes, env, layout, prefix, names, loops, pl_l)

    return stage


def stage_gain_grads(sizes, prefix, layout):
    def stage(env):
        norm = stacked(
            [env[N.dnorm(0, i)][...] + env[N.dnorm(1, i)][...] for i in range(4)] + [jnp.zeros((12, sizes.D), F32)]
        )
        heads = stacked(
            [jnp.zeros((4, sizes.HD), F32)]
            + [env[kind(0)][...] + env[kind(1)][...] for kind in (N.dqg, N.dkg)]
            + [jnp.zeros((10, sizes.HD), F32)]
        )
        if sizes.slots == 1:
            env[N.gain_norm][...] = norm
            env[N.gain_heads][...] = heads
            return
        norm, heads = norm.astype(BF), heads.astype(BF)
        width, head_width = sizes.D // sizes.slots, sizes.HD // sizes.slots

        def pick(total, each, index):
            a = lax.broadcasted_iota(jnp.int32, (total, LANES), 0)
            b = lax.broadcasted_iota(jnp.int32, (total, LANES), 1)
            return jnp.where((a == b + index * each) & (b < each), 1.0, 0.0).astype(BF)

        at = layout.gains
        chip, core = env[N.place][1], env[N.place][0]
        for k in range(sizes.slots // 2):
            for name, flip in ((N.keep, core), (N.send, 1 - core)):
                index = 2 * jnp.bitwise_xor(k, chip) + flip
                block = dot(norm, pick(sizes.D, width, index)) + dot(heads, pick(sizes.HD, head_width, index))
                env[name(prefix)][k, at : at + 16, :] = block.astype(BF)

    return stage


def pack(sizes, layout, arrays, gains=None):
    names = list(layout.at)
    unique = []
    for name in names:
        if not any(arrays[name][0] is u for u in unique):
            unique.append(arrays[name][0])
    extra = [] if layout.gains is None else [gains]

    def kernel(*refs):
        out = refs[-1]
        for name in names:
            array, lead = arrays[name]
            source = refs[[array is u for u in unique].index(True)]
            first, rows, blocks = layout.at[name]
            for b in range(blocks):
                out[first + b * rows : first + (b + 1) * rows, :] = source[
                    lead + (slice(None), slice(b * LANES, (b + 1) * LANES))
                ]
        if layout.gains is not None:
            out[layout.gains : layout.gains + 16, :] = refs[len(unique)][...]

    return pl.pallas_call(
        kernel,
        name=N.pack,
        out_shape=jax.ShapeDtypeStruct((layout.total, LANES), BF),
        compiler_params=pltpu.CompilerParams(vmem_limit_bytes=VMEM_LIMIT),
        cost_estimate=pl.CostEstimate(flops=0, bytes_accessed=4 * layout.total * LANES, transcendentals=0),
    )(*unique, *extra)


def sort_rows(sizes, rank, *arrays):
    def kernel(rank_ref, *refs):
        count = len(refs) // 2
        place = lax.broadcasted_iota(jnp.int32, (sizes.T, sizes.T), 0)
        matrix = jnp.where(place == rank_ref[...], 1.0, 0.0).astype(BF)
        for source, target in zip(refs[:count], refs[count:]):
            target[...] = dot(matrix, source[...])

    return pl.pallas_call(
        kernel,
        name=N.sort_rows,
        out_shape=[jax.ShapeDtypeStruct(a.shape, F32) for a in arrays],
        compiler_params=pltpu.CompilerParams(vmem_limit_bytes=VMEM_LIMIT),
        cost_estimate=pl.CostEstimate(flops=0, bytes_accessed=2**21, transcendentals=0),
    )(rank, *arrays)


def unsort_rows(sizes, rank, value):
    def kernel(rank_ref, source, target):
        place = lax.broadcasted_iota(jnp.int32, (sizes.T, sizes.T), 0)
        matrix = jnp.where(place == rank_ref[...], 1.0, 0.0).astype(BF)
        target[...] = dot_tn(matrix, source[...].astype(BF)).astype(BF)

    return pl.pallas_call(
        kernel,
        name=N.unsort_rows,
        out_shape=jax.ShapeDtypeStruct(value.shape, BF),
        compiler_params=pltpu.CompilerParams(vmem_limit_bytes=VMEM_LIMIT),
        cost_estimate=pl.CostEstimate(flops=0, bytes_accessed=2**20, transcendentals=0),
    )(rank, value)


def unpack(sizes, targets, sources):
    names = list(sources)
    shapes = [jax.ShapeDtypeStruct(shape, F32) for shape, _ in targets]

    def kernel(*refs):
        ins = {name: refs[2 * i : 2 * i + 2] for i, name in enumerate(names)}
        outs = refs[2 * len(names) :]

        def rows_of(prefix, first, count):
            low, high = ins[prefix]
            half = low.shape[0]
            if first + count <= half:
                return low[first : first + count, :].astype(F32)
            if first >= half:
                return high[first - half : first + count - half, :].astype(F32)
            return jnp.concatenate(
                [low[first:half, :].astype(F32), high[: first + count - half, :].astype(F32)], axis=0
            )

        for out, (_, parts) in zip(outs, targets):
            for lead, prefix, name, column in parts:
                layout = sources[prefix][2]
                if name == N.norm:
                    out[...] = rows_of(prefix, layout.gains, 16)
                    continue
                first, rows, blocks = layout.at[name]
                for b in range(blocks):
                    out[lead + (slice(None), slice((column + b) * LANES, (column + b + 1) * LANES))] = rows_of(
                        prefix, first + b * rows, rows
                    )

    return pl.pallas_call(
        kernel,
        name=N.unpack,
        out_shape=shapes,
        compiler_params=pltpu.CompilerParams(vmem_limit_bytes=VMEM_LIMIT),
        cost_estimate=pl.CostEstimate(flops=0, bytes_accessed=2**22, transcendentals=0),
    )(*[half for name in names for half in sources[name][:2]])


def swap(sizes, value, bit):
    return lax.ppermute(value, "own", [(i, i ^ bit) for i in range(sizes.n)])


def along(value, pairs):
    return lax.ppermute(value, "dp", pairs)


def after_all(values, others):
    others = [o for o in others if not any(o is value for value in values)]
    count = len(values)

    def kernel(*refs):
        pass

    space = pl.BlockSpec(memory_space=pl.ANY)
    return pl.pallas_call(
        kernel,
        name=N.after,
        out_shape=[jax.ShapeDtypeStruct(value.shape, value.dtype) for value in values],
        in_specs=[space] * (count + len(others)),
        out_specs=[space] * count,
        input_output_aliases={i: i for i in range(count)},
        cost_estimate=pl.CostEstimate(flops=0, bytes_accessed=0, transcendentals=0),
    )(*values, *others)


def after(value, *others):
    return after_all([value], others)[0]


def gather_plain(sizes, mine, x_first, others=()):
    px, py = swap(sizes, mine, XBIT), swap(sizes, mine, YBIT)
    px = after(px, *others) if others else px
    pd = swap(sizes, px, YBIT) if x_first else swap(sizes, py, XBIT)
    here = [mine, px, py, pd]
    return here + [swap(sizes, piece, CORE) for piece in here]


def gather_direct(sizes, mine):
    here = [mine] + [swap(sizes, mine, bit) for bit in (XBIT, YBIT, XBIT | YBIT)]
    return here + [swap(sizes, piece, CORE) for piece in here]


PIECES = (0, XBIT, YBIT, XBIT | YBIT, CORE, CORE | XBIT, CORE | YBIT, CORE | XBIT | YBIT)


def gather_paired(sizes, mine, odd, others=()):
    px = swap(sizes, mine, XBIT)
    chosen = jnp.where(odd, px, mine)
    py = swap(sizes, after(chosen, *others) if others else chosen, YBIT)
    pz = along(py, [(0, 1), (1, 0), (2, 3), (3, 2)])
    here = [mine, px, py, pz]
    return here + [swap(sizes, piece, CORE) for piece in here]


def add(first, *others):
    total = first.astype(F32)
    for other in others:
        total = total + other.astype(F32)
    return total.astype(BF)


class Sum:
    def __init__(self, sizes, keep, send, mode, odd=None):
        self.sizes, self.keep, self.mode, self.odd = sizes, keep, mode, odd
        self.payload, self.done = [send], []
        self.steps = [self.core] + ([self.direct] if mode == N.direct else [self.near, self.far])
        self.steps += [self.trade, self.level, self.back]

    def step(self):
        now = self.steps.pop(0)
        now(self.payload)

    def swap(self, value, bit):
        return swap(self.sizes, value, bit)

    def core(self, sent):
        here, come = self.keep, self.swap(sent[0], CORE)
        if self.mode == N.direct:
            self.keep, *self.payload = [add(here[k], come[k]) for k in range(4)]
            return
        if self.mode == N.x:
            here, come = [a.reshape((2, 2) + a.shape[1:]) for a in (here, come)]
            pairs = [(here[:, i], come[:, i]) for i in range(2)]
        else:
            pairs = [(here[i : i + 2], come[i : i + 2]) for i in (0, 2)]
        self.keep, self.payload = add(*pairs[0]), [add(*pairs[1])]

    def direct(self, sent):
        come = [self.swap(value, bit) for value, bit in zip(sent, (XBIT, YBIT, XBIT | YBIT))]
        self.level_in(add(self.keep, *come))

    def near(self, sent):
        come = self.swap(sent[0], XBIT if self.mode == N.x else YBIT)
        self.keep, self.payload = add(self.keep[0], come[0]), [add(self.keep[1], come[1])]

    def far(self, sent):
        self.level_in(add(self.keep, self.swap(sent[0], YBIT if self.mode == N.x else XBIT)))

    def level_in(self, total):
        self.plane_total = total
        if self.odd is None:
            self.payload = [total]
            return
        rows = total.shape[0] // 2
        low, high = total[:rows], total[rows:]
        self.keep, self.payload = jnp.where(self.odd, high, low), [jnp.where(self.odd, low, high)]

    def trade(self, sent):
        self.payload = [add(self.keep, along(sent[0], [(0, 1), (1, 0), (2, 3), (3, 2)]))]

    def level(self, sent):
        self.payload = [add(sent[0], along(sent[0], [(0, 2), (2, 0), (1, 3), (3, 1)]))]

    def back(self, sent):
        come = along(sent[0], [(0, 1), (1, 0), (2, 3), (3, 2)])
        self.halves = (jnp.where(self.odd, come, sent[0]), jnp.where(self.odd, sent[0], come))
        self.payload = list(self.halves)


def make_shards(mesh):
    n, planes = mesh.shape["own"], mesh.shape["dp"]
    fast = n == 8 and planes == 4

    def shards(
        tokens,
        cotangent,
        lengths,
        row_packed_slot,
        shared_attention_matrix,
        shared_output_matrix,
        shared_gate_up_matrix,
        shared_down_matrix,
        norm_gain_table,
        query_key_gains,
        adapter_attention_first,
        adapter_query_second,
        adapter_key_value_second,
        adapter_output_first,
        adapter_output_second,
        adapter_gate_first,
        adapter_gate_second,
        adapter_down_first,
        adapter_down_second,
    ):
        s = Sizes()
        s.n, s.slots = n, (8 if fast else 1)
        s.T, s.D = tokens.shape
        s.HD = adapter_key_value_second.shape[3]
        s.H = adapter_query_second.shape[2] // s.HD
        s.R = adapter_query_second.shape[1] * n
        s.F = shared_down_matrix.shape[0] * n
        s.DB, s.RB, s.HB = s.D // LANES, s.R // LANES, s.HD // LANES
        s.IB = max(16, 256 // n)
        s.QB = s.T // 4
        s.kv_pieces = 8 if fast else 1
        QW, k = s.H * s.HD, s.slots
        s.shard = {
            N.qkv: (s.D // k, (QW + 2 * s.HD) // LANES),
            N.aqkv: (s.D // k, 3 * s.RB),
            N.gug: (s.D // k, s.F // LANES),
            N.guu: (s.D // k, s.F // LANES),
            N.qkvq: (s.D // k, QW // LANES),
            N.qkvkv: (s.D // k, 2 * s.HB),
            N.aqkvq: (s.D // k, s.RB),
            N.aqkvkv: (s.D // k, 2 * s.RB),
            N.bq: (s.R // k, QW // LANES),
            N.bk: (s.R // k, s.HB),
            N.bv: (s.R // k, s.HB),
            N.outw: (QW // k, s.DB),
            N.outa: (QW // k, s.RB),
            N.outb: (s.R // k, s.DB),
            N.gu: (s.D // k, 2 * s.F // LANES),
            N.agu: (s.D // k, 2 * s.RB),
            N.bg: (s.R // k, s.F // LANES),
            N.bu: (s.R // k, s.F // LANES),
            N.dnw: (s.F // k, s.DB),
            N.dna: (s.F // k, s.RB),
            N.dnb: (s.R // k, s.DB),
        }
        own, plane = lax.axis_index("own"), lax.axis_index("dp")

        plain_ids = jnp.stack([own ^ m for m in PIECES]).astype(jnp.int32) if fast else jnp.zeros((1,), jnp.int32)
        slots = row_packed_slot[0]
        seq = lengths[0]
        my_slots = lax.dynamic_slice_in_dim(slots, own * s.T, s.T)
        rank = (my_slots // n).reshape(1, s.T)
        rest = slots.reshape(n, s.T)[:, 0] % n
        my_rest = my_slots[0] % n
        counts = jnp.arange(seq.shape[0])
        ends = jnp.sum(jnp.where(counts[None, :] <= counts[:, None], seq[None, :], 0), axis=1)
        sorted_slots = n * jnp.arange(s.T, dtype=jnp.int32) + my_rest
        past = sorted_slots[:, None] >= ends[None, :]
        starts = jnp.sum(jnp.where(past, seq[None, :], 0), axis=1)
        position = sorted_slots - starts
        inverse = THETA ** (-jnp.arange(s.HD // 2, dtype=F32) * 2.0 / s.HD)
        angles = position.astype(F32)[:, None] * inverse[None, :]
        block_slots = s.IB * n
        first_block = starts.reshape(4, s.QB)[:, 0] // block_slots
        key_rest = rest
        if fast:
            key_rest = jnp.sum(
                jnp.where(plain_ids[:, None] == jnp.arange(n)[None, :], rest[None, :], 0), axis=1
            )
        along_rows = jnp.arange(s.T, dtype=jnp.int32).reshape(s.T // s.IB, 1, 1, s.IB) * n
        kslot = (along_rows + key_rest.reshape(1, 1, n, 1)).reshape(s.T // s.IB, 1, n * s.IB).astype(jnp.int32)
        stream0, cot = sort_rows(s, rank, tokens, cotangent)

        v = {
            N.cos: jnp.cos(angles),
            N.sin: jnp.sin(angles),
            N.qslot: sorted_slots.reshape(s.T, 1),
            N.qstart: starts.reshape(s.T, 1).astype(jnp.int32),
            N.kslot: kslot,
            N.stream0: stream0,
            N.cot: cot,
        }
        def full(array, axis):
            return array if fast else lax.all_gather(array, "own", axis=axis, tiled=True)

        w_att, w_out = full(shared_attention_matrix, 0), full(shared_output_matrix, 0)
        w_gu, w_dn = full(shared_gate_up_matrix, 0), full(shared_down_matrix, 0)
        a_att, b_q = full(adapter_attention_first, 1), full(adapter_query_second, 1)
        b_kv, a_out = full(adapter_key_value_second, 2), full(adapter_output_first, 1)
        b_out, a_gu = full(adapter_output_second, 1), full(adapter_gate_first, 1)
        b_gu, a_dn = full(adapter_gate_second, 2), full(adapter_down_first, 1)
        b_dn = full(adapter_down_second, 1)

        def arrays_of(l):
            return {
                N.qkv: (w_att, ()),
                N.aqkv: (a_att, (l,)),
                N.bq: (b_q, (l,)),
                N.bk: (b_kv, (l, 0)),
                N.bv: (b_kv, (l, 1)),
                N.outw: (w_out, ()),
                N.outa: (a_out, (l,)),
                N.outb: (b_out, (l,)),
                N.gu: (w_gu, ()),
                N.agu: (a_gu, (l,)),
                N.bg: (b_gu, (l, 0)),
                N.bu: (b_gu, (l, 1)),
                N.dnw: (w_dn, ()),
                N.dna: (a_dn, (l,)),
                N.dnb: (b_dn, (l,)),
            }

        q_names, o_names = (N.qkv, N.aqkv, N.bq, N.bk, N.bv), (N.outw, N.outa, N.outb)
        g_names, d_names = (N.gu, N.agu, N.bg, N.bu), (N.dnw, N.dna, N.dnb)
        lq_names, lr_names = (N.aqkv, N.bq, N.bk, N.bv), (N.outa, N.outb, N.agu, N.bg, N.bu, N.dna, N.dnb)
        odd = (plane & 1) == 1
        inner = (plane == 1) | (plane == 2)
        paired_ids = plain_ids
        if fast:
            over_y = jnp.where(odd, XBIT | YBIT, YBIT)
            over_z = jnp.where(odd, YBIT, XBIT | YBIT)
            order = [0, XBIT, over_y, over_z]
            paired_ids = jnp.stack([own ^ m for m in order] + [own ^ m ^ CORE for m in order]).astype(jnp.int32)
        gain_block = None
        if fast:
            gain_block = jnp.concatenate(
                [
                    jnp.pad(norm_gain_table, ((0, 0), (0, LANES - norm_gain_table.shape[1]))),
                    jnp.pad(query_key_gains, ((0, 0), (0, LANES - query_key_gains.shape[1]))),
                    jnp.zeros((10, LANES), BF),
                ],
                axis=0,
            )

        def packed(names, l, gains=False, of=()):
            layout = Layout(s, names, gains)
            arrays = {m: arrays_of(k)[m] for m, k in of} if of else arrays_of(l)
            return layout, pack(s, layout, arrays, gain_block)

        def fetch(made, scheme, start=None, turn=()):
            layout, mine = made
            if not fast:
                return Chunk(layout, [mine], plain_ids)
            if scheme == N.y:
                over = [after(mine, start.pieces[1]), after(mine, start.pieces[3])]
                px, py = swap(s, over[0], XBIT), swap(s, over[1], YBIT)
                here = [mine, px, py, swap(s, py, XBIT)]
                chunk = Chunk(layout, here + [swap(s, piece, CORE) for piece in here], plain_ids)
                chunk.gates = over
                return chunk
            if start is not None:
                mine = after(mine, *start)
            if scheme == N.whole:
                whole = Chunk(layout, [lax.all_gather(mine, "own", axis=0, tiled=True)], jnp.arange(n, dtype=jnp.int32))
                whole.mine = mine
                return whole
            if scheme == N.direct:
                return Chunk(layout, gather_direct(s, mine), plain_ids)
            if scheme == N.paired:
                return Chunk(layout, gather_paired(s, mine, odd, turn), paired_ids)
            return Chunk(layout, gather_plain(s, mine, scheme == N.x, turn), plain_ids)

        pack_g, pack_q = packed(g_names + d_names, 0), packed(q_names, 0, gains=fast)
        pack_lr = packed(lr_names, 1)
        first = [(m, 0) for m in o_names] + [(m, 1) for m in lq_names]
        pack_o = packed(o_names + lq_names, None, of=first)
        chunk_g = fetch(pack_g, N.whole)
        chunk_q = fetch(pack_q, N.x, None, (stream0, v[N.cos], pack_g[1], pack_o[1], pack_lr[1]))
        chunk_o = fetch(pack_o, N.y, chunk_q)
        chunk_lq = chunk_o
        if fast:
            v[N.stream0] = after(v[N.stream0], *chunk_o.gates)
        loop0 = {**{m: chunk_q for m in q_names}, **{m: chunk_o for m in o_names}}
        loop0 |= {m: chunk_g for m in g_names + d_names}
        of_loop = [loop0]

        def wts(names, l):
            return [(m, of_loop[l][m]) for m in names]

        T, D, HD, H, R, F = s.T, s.D, s.HD, s.H, s.R, s.F
        blocks = F // 256
        half = n // 2 if fast else n
        shapes = {
            N.norm: ((16, D), F32),
            N.qkg: ((16, HD), F32),
            N.stream1: ((T, D), F32),
            N.stream2: ((T, D), F32),
            N.o_acc: ((H * s.QB, HD), F32),
            N.l_acc: ((H * s.QB, LANES), F32),
            N.dkv_acc: ((T // s.IB, n * s.IB, 2 * HD), F32),
            N.sgrad1: ((T, D), F32),
            N.sgrad0: ((T, D), F32),
            N.gain_norm: ((16, D), F32),
            N.gain_heads: ((16, HD), F32),
        }
        for l in (0, 1):
            shapes |= {
                N.attn_in(l): ((T, D), BF),
                N.mid(l): ((3, T, R), BF),
                N.raw(l): ((H + 1, T, HD), F32),
                N.q(l): ((H, T, HD), BF),
                N.kv(l): ((T, 2 * HD), BF),
                N.att(l): ((H, T, HD), F32),
                N.lse(l): ((H, T, LANES), F32),
                N.ho(l): ((H, T, HD), BF),
                N.omid(l): ((T, R), BF),
                N.branch(l): ((T, D), F32),
                N.middle(l): ((T, D), F32),
                N.ffn_in(l): ((T, D), BF),
                N.gmid(l): ((2, T, R), BF),
                N.gu(l): ((blocks, T, 512), F32),
                N.hidden(l): ((blocks, T, 256), BF),
                N.dmid(l): ((T, R), BF),
                N.ffn_out(l): ((T, D), F32),
                N.ffn_low(l): ((T, D), BF),
                N.dmg(l): ((T, R), BF),
                N.gug(l): ((2 * blocks, T, 256), BF),
                N.gmg(l): ((2, T, R), BF),
                N.mgrad(l): ((T, D), F32),
                N.blow(l): ((T, D), BF),
                N.omg(l): ((T, R), BF),
                N.hgrad(l): ((H, T, HD), BF),
                N.dq(l): ((H, T, HD), F32),
                N.dkvkeep(l): ((half, T, 2 * HD), BF),
                N.dkvsend(l): ((half, T, 2 * HD), BF),
                N.rawq_low(l): ((H, T, HD), BF),
                N.rawkv_low(l): ((2, T, HD), BF),
                N.midgq(l): ((T, R), BF),
                N.midgkv(l): ((2, T, R), BF),
                N.agrad(l): ((T, D), F32),
                N.dqg(l): ((1, HD), F32),
                N.dkg(l): ((1, HD), F32),
            }
            for i in range(4):
                shapes[N.dnorm(l, i)] = ((1, D), F32)

        def call(name, stages, ins, outs, scratch=(), weights=(), smem=(), micros=0):
            made = run_kernel(
                s,
                name,
                stages,
                {m: v[m] for m in ins},
                {m: shapes[m] for m in outs},
                {m: shapes[m] for m in scratch},
                weights,
                {m: v[m] for m in smem},
                micros,
            )
            v.update(made)

        v[N.first_block] = first_block.astype(jnp.int32)
        v[N.place] = jnp.stack([own & 1, own >> 1]).astype(jnp.int32)

        def share_kv(l):
            if fast:
                pieces = gather_direct(s, v[N.kv(l)])
            else:
                gathered = lax.all_gather(v[N.kv(l)], "own", axis=0, tiled=False)
                pieces = [gathered]
            for i, piece in enumerate(pieces):
                v[N.kvp(l, i)] = piece

        def kv_names(l):
            return [N.kvp(l, i) for i in range(s.kv_pieces)]

        qkv_outs = [N.attn_in, N.mid, N.raw, N.q, N.kv]

        def fill(names, l):
            return [m(l) for m in names]

        if fast:
            call(
                N.qkv0,
                [stage_gains(s, chunk_q), stage_qkv(s, 0, N.stream0)],
                [N.stream0, N.cos, N.sin],
                [N.norm, N.qkg] + fill(qkv_outs, 0),
                weights=[(N.gains, chunk_q)] + wts(q_names, 0),
                micros=6.5,
            )
        else:
            norm = lax.all_gather(norm_gain_table, "own", axis=1, tiled=True).astype(F32)
            heads = lax.all_gather(query_key_gains, "own", axis=1, tiled=True).astype(F32)
            v[N.norm] = jnp.pad(norm, ((0, 12), (0, 0)))
            v[N.qkg] = jnp.pad(heads, ((4, 10), (0, 0)))
            call(
                N.qkv0,
                [stage_qkv(s, 0, N.stream0)],
                [N.stream0, N.cos, N.sin, N.norm, N.qkg],
                fill(qkv_outs, 0),
                weights=wts(q_names, 0),
                micros=6.5,
            )
        share_kv(0)
        if fast:
            mine = after(pack_lr[1], v[N.kvp(0, 3)])
            here = [mine] + [swap(s, mine, bit) for bit in (XBIT, YBIT, XBIT | YBIT)]
        of_loop.append({**loop0, **{m: chunk_lq for m in lq_names}})
        att_ins = [N.qslot, N.qstart, N.kslot]
        out_outs = [N.att, N.lse, N.ho, N.omid, N.branch, N.middle, N.ffn_in]
        ffn_outs = [N.gmid, N.gu, N.hidden, N.dmid, N.ffn_out]
        call(
            N.attend0,
            [stage_attend(s, 0), stage_out(s, 0, N.stream0)],
            [N.stream0, N.q0, N.norm] + att_ins + kv_names(0),
            fill(out_outs, 0),
            scratch=[N.o_acc, N.l_acc],
            weights=wts(o_names, 0),
            smem=[N.first_block],
            micros=11,
        )
        call(
            N.ffn0,
            [stage_ffn(s, 0), stage_qkv(s, 1, N.stream1)],
            [N.ffn_in0, N.middle0, N.norm, N.qkg, N.cos, N.sin],
            fill(ffn_outs, 0) + [N.stream1] + fill(qkv_outs, 1),
            weights=wts(g_names + d_names, 0) + wts(q_names, 1),
            micros=16,
        )
        chunk_lr = Chunk(*pack_lr[:1], [pack_lr[1]], plain_ids)
        if fast:
            *here, v[N.kv1] = after_all(here + [v[N.kv1]], [])
            chunk_lr.pieces = here + [swap(s, piece, CORE) for piece in here]
        of_loop[1] |= {m: chunk_lr for m in lr_names}
        share_kv(1)
        loop1 = [
            stage_attend(s, 1),
            stage_out(s, 1, N.stream1),
            stage_ffn(s, 1),
            stage_ffn_back(s, 1, N.cot),
            stage_out_back(s, 1),
        ]
        loop1_outs = (
            [N.stream2, N.mgrad1]
            + fill([N.ho, N.omid, N.ffn_in, N.gmid, N.hidden, N.dmid], 1)
            + fill([N.ffn_low, N.dmg, N.gug, N.gmg, N.blow, N.omg], 1)
            + [N.dnorm(1, 1), N.dnorm(1, 2), N.dnorm(1, 3)]
        )
        loop1_scratch = [N.o_acc, N.l_acc, N.branch1, N.middle1, N.gu1, N.ffn_out1]
        back_outs = [N.dq, N.dkvkeep] + ([N.dkvsend] if fast else [])
        kept = [N.att1, N.lse1, N.hgrad1]
        call(
            N.loop1,
            loop1 + ([stage_attend_back(s, 1)] if fast else []),
            [N.stream1, N.q1, N.norm, N.cot] + att_ins + kv_names(1),
            loop1_outs + (fill(back_outs, 1) if fast else kept),
            scratch=loop1_scratch + ([N.dkv_acc] + kept if fast else []),
            weights=wts(o_names + g_names + d_names, 1),
            smem=[N.first_block],
            micros=35,
        )
        if not fast:
            call(
                N.attend_back1,
                [stage_attend_back(s, 1)],
                [N.q1] + kept + att_ins + kv_names(1),
                fill(back_outs, 1),
                scratch=[N.o_acc, N.dkv_acc],
                smem=[N.first_block],
                micros=10,
            )

        plans = {
            N.la: [((N.bg, N.bu, N.agu, N.dna, N.dnb, N.outa, N.outb), 1)],
            N.g1: [((N.gug,), 0), ((N.aqkv,), 1)],
            N.g2: [((N.guu,), 0), ((N.bq, N.bk, N.bv), 1)],
            N.g3: [((N.dnw, N.agu), 0)],
            N.g4: [((N.bg, N.bu, N.dna, N.dnb), 0)],
            N.rb: [((N.outw, N.outa, N.outb, N.bq, N.qkvq, N.aqkvq), 0)],
            N.ra: [((N.qkvkv, N.aqkvkv, N.bk, N.bv), 0)],
        }
        modes = {N.la: N.direct, N.g1: N.x, N.g2: N.y, N.g3: N.x, N.g4: N.y, N.rb: N.direct, N.ra: N.direct}
        layouts = {}
        where = {}
        for m, parts in plans.items():
            layouts[m] = Layout(s, [name for names, _ in parts for name in names], gains=(m == N.ra and fast))
            shapes[N.keep(m)] = ((half if fast else 1, layouts[m].total, LANES), BF)
            shapes[N.send(m)] = shapes[N.keep(m)]
            where |= {(name, l): m for names, l in parts for name in names}

        def grads(names, ins, micros, extra=(), extra_outs=()):
            parts = []
            for m in names:
                parts += [(m, layouts[m], group, [0, 1], l) for group, l in plans[m]]
            outs = [end(m) for m in names for end in ((N.keep, N.send) if fast else (N.keep,))]
            call(
                N.grads(names[0]),
                [stage_grads(s, parts)] + list(extra),
                ins,
                outs + list(extra_outs),
                smem=[N.place] if fast else [],
                micros=micros,
            )

        sums = {}

        def open_sum(*names):
            for m in names:
                if fast:
                    sums[m] = Sum(s, v[N.keep(m)], v[N.send(m)], modes[m], odd)

        def open_kv(l):
            if fast:
                sums[N.dkv(l)] = Sum(s, v[N.dkvkeep(l)], v[N.dkvsend(l)], N.direct)
            else:
                keep = v[N.dkvkeep(l)].reshape(n * T, 2 * HD)
                v[N.dkv] = lax.psum_scatter(keep, "own", scatter_dimension=0, tiled=True)

        def close_kv(l):
            if fast:
                v[N.dkv] = sums[N.dkv(l)].payload[0]

        def phase(starts, inputs=(), need=()):
            if not fast:
                return
            starts, inputs = [sums[m] for m in starts], list(inputs)
            others = []
            for m in need:
                others += sums[m].payload if m in sums else [v[m]]
            values = after_all([p for r in starts for p in r.payload] + [v[m] for m in inputs], others)
            for r in starts:
                count = len(r.payload)
                r.payload, values = values[:count], values[count:]
            for m, value in zip(inputs, values):
                v[m] = value
            for r in starts:
                r.step()

        gain_ins = [N.dnorm(l, i) for l in (0, 1) for i in range(4)] + [N.dqg0, N.dqg1, N.dkg0, N.dkg1]
        qkv_l = [N.attn_in, N.mid, N.rawq_low, N.rawkv_low, N.midgq, N.midgkv]

        open_kv(1)
        phase([N.dkv1], [N.dq1])
        call(
            N.q_back1,
            [stage_q_back(s, 1)],
            [N.cos, N.sin, N.qkg, N.dq1, N.raw1],
            [N.rawq_low1, N.midgq1, N.agrad1, N.dqg1],
            weights=wts((N.qkv, N.bq, N.aqkv), 1),
            micros=5.8,
        )
        phase([N.dkv1], [N.gmg1], [N.agrad1])
        grads(
            [N.la],
            [N.ffn_in1, N.gmid1, N.gug1, N.gmg1, N.hidden1, N.dmid1, N.ffn_low1, N.dmg1, N.ho1, N.omid1, N.blow1, N.omg1],
            8.6,
        )
        open_sum(N.la)
        phase([N.la], [N.agrad1], [N.dkv1])
        close_kv(1)
        call(
            N.kv_back1,
            [stage_kv_back(s, 1, N.stream1, N.sgrad1)],
            [N.cos, N.sin, N.qkg, N.norm, N.dkv, N.raw1, N.agrad1, N.stream1, N.mgrad1],
            [N.dkg1, N.rawkv_low1, N.midgkv1, N.dnorm(1, 0), N.sgrad1],
            weights=wts((N.qkv, N.aqkv, N.bk, N.bv), 1),
            micros=6.2,
        )
        phase([N.la], [N.sgrad1])
        call(
            N.ffn_back0,
            [stage_ffn_back(s, 0, N.sgrad1)],
            [N.norm, N.sgrad1, N.ffn_out0, N.gu0, N.middle0],
            [N.dnorm(0, 3), N.dnorm(0, 2)] + fill([N.ffn_low, N.dmg, N.gug, N.gmg, N.mgrad], 0),
            weights=wts(d_names + (N.bg, N.bu, N.gu, N.agu), 0),
            micros=14,
        )
        grads([N.g1, N.g2], fill([N.ffn_in, N.gug], 0) + [N.ffn_in1, N.gug1] + fill(qkv_l, 1), 9.7)
        open_sum(N.g1, N.g2)
        phase([N.g1, N.g2, N.la], [N.dmg0, N.mgrad0])
        grads(
            [N.g3, N.g4],
            fill([N.ffn_in, N.gmid, N.gug, N.gmg, N.hidden, N.dmid, N.ffn_low, N.dmg], 0) + [N.hidden1, N.ffn_low1],
            8.5,
        )
        call(
            N.out_back0,
            [stage_out_back(s, 0)],
            [N.branch0, N.norm, N.mgrad0],
            [N.dnorm(0, 1), N.blow0, N.omg0, N.hgrad0],
            weights=wts(o_names, 0),
            micros=4.5,
        )
        open_sum(N.g3, N.g4)
        phase([N.g1, N.g2, N.g3, N.g4, N.la], [N.hgrad0])
        call(
            N.attend_back0,
            [stage_attend_back(s, 0)],
            [N.hgrad0, N.q0, N.att0, N.lse0] + att_ins + kv_names(0),
            fill(back_outs, 0),
            scratch=[N.o_acc, N.dkv_acc],
            smem=[N.first_block],
            micros=13,
        )
        open_kv(0)
        phase([N.dkv0, N.g1, N.g2, N.la], [N.dq0])
        call(
            N.q_back0,
            [stage_q_back(s, 0)],
            [N.cos, N.sin, N.qkg, N.dq0, N.raw0],
            [N.rawq_low0, N.midgq0, N.agrad0, N.dqg0],
            weights=wts((N.qkv, N.bq, N.aqkv), 0),
            micros=5.8,
        )
        phase([N.dkv0, N.g1, N.g2], [N.rawq_low0])
        grads(
            [N.rb],
            fill([N.ho, N.omid, N.blow, N.omg, N.mid, N.rawq_low, N.attn_in, N.midgq], 0)
            + [N.ho1, N.blow1, N.attn_in1, N.rawq_low1],
            7,
        )
        open_sum(N.rb)
        phase([N.rb, N.g3, N.g4, N.g1, N.g2], [N.agrad0], [N.dkv0])
        close_kv(0)
        call(
            N.kv_back0,
            [stage_kv_back(s, 0, N.stream0, N.sgrad0)],
            [N.cos, N.sin, N.qkg, N.norm, N.dkv, N.raw0, N.agrad0, N.stream0, N.mgrad0],
            [N.dkg0, N.rawkv_low0, N.midgkv0, N.dnorm(0, 0), N.sgrad0],
            weights=wts((N.qkv, N.aqkv, N.bk, N.bv), 0),
            micros=6.2,
        )
        grads(
            [N.ra],
            fill([N.attn_in, N.mid, N.rawkv_low, N.midgkv], 0) + [N.attn_in1, N.rawkv_low1] + gain_ins,
            3,
            [stage_gain_grads(s, N.ra, layouts[N.ra])],
            [] if fast else [N.gain_norm, N.gain_heads],
        )
        open_sum(N.ra)
        phase([N.g3, N.g4, N.rb], [N.stream2, N.sgrad0], [N.g1, N.g2])
        mixed = unsort_rows(s, rank, v[N.stream2])
        tokens_grad = unsort_rows(s, rank, v[N.sgrad0])
        v[N.mixed], v[N.tokens_grad] = mixed, tokens_grad
        phase([N.ra, N.g3, N.g4, N.rb, N.g1], [], [N.mixed, N.tokens_grad])
        phase([N.ra, N.g3, N.g4])
        phase([N.ra, N.rb, N.g3, N.g4, N.g2])
        phase([N.ra, N.rb])
        phase([N.ra])
        for m in sums:
            assert m in (N.dkv0, N.dkv1) or not sums[m].steps
        finished = {m: sums[m].payload for m in plans if fast}

        HB, RB = s.HB, s.RB
        two = (0, 1)
        targets = [
            (shared_attention_matrix.shape, [((), N.qkvq, 0, 0), ((), N.qkvkv, 0, H * HB)]),
            (shared_output_matrix.shape, [((), N.outw, 0, 0)]),
            (shared_gate_up_matrix.shape, [((), N.gug, 0, 0), ((), N.guu, 0, F // LANES)]),
            (shared_down_matrix.shape, [((), N.dnw, 0, 0)]),
            (
                adapter_attention_first.shape,
                [((0,), N.aqkvq, 0, 0), ((0,), N.aqkvkv, 0, RB), ((1,), N.aqkv, 1, 0)],
            ),
            (adapter_query_second.shape, [((l,), N.bq, l, 0) for l in two]),
            (
                adapter_key_value_second.shape,
                [((l, j), m, l, 0) for l in two for j, m in enumerate((N.bk, N.bv))],
            ),
            (adapter_output_first.shape, [((l,), N.outa, l, 0) for l in two]),
            (adapter_output_second.shape, [((l,), N.outb, l, 0) for l in two]),
            (adapter_gate_first.shape, [((l,), N.agu, l, 0) for l in two]),
            (adapter_gate_second.shape, [((l, j), m, l, 0) for l in two for j, m in enumerate((N.bg, N.bu))]),
            (adapter_down_first.shape, [((l,), N.dna, l, 0) for l in two]),
            (adapter_down_second.shape, [((l,), N.dnb, l, 0) for l in two]),
        ]
        if fast:
            plan = [(shape, [(lead, where[m, l], m, col) for lead, m, l, col in parts]) for shape, parts in targets]
            made = [None] * len(plan)
            early = [i for i, (_, parts) in enumerate(plan) if all(part[1][0] in N.lg for part in parts)]
            late = [i for i in range(len(plan)) if i not in early]
            for which, ends in ((early, []), (late, [((16, LANES), [((), N.ra, N.norm, 0)])])):
                chosen = [plan[i] for i in which] + ends
                used = sorted({part[1] for _, parts in chosen for part in parts})
                results = unpack(s, chosen, {m: (*finished[m], layouts[m]) for m in used})
                for i, value in zip(which, results):
                    made[i] = value
            grads, gains = made, results[-1]
            norm_grad = gains[:4, : norm_gain_table.shape[1]]
            heads_grad = gains[4:6, : query_key_gains.shape[1]]
        else:

            def natural(name, l):
                layout = layouts[where[name, l]]
                first, rows, count = layout.at[name]
                block = v[N.keep(where[name, l])][0, first : first + rows * count]
                return block.reshape(count, rows, LANES).transpose(1, 0, 2).reshape(rows, count * LANES)

            def reduced(value, axis):
                part = lax.psum_scatter(value.astype(BF), "own", scatter_dimension=axis, tiled=True)
                return lax.psum(part, "dp").astype(F32)

            grads = []
            for shape, parts in targets:
                of_lead = {}
                for lead, m, l, _ in parts:
                    of_lead.setdefault(lead, []).append(natural(m, l))
                value = jnp.stack([side_by_side(columns_of) for columns_of in of_lead.values()])
                value = value.reshape(shape[:-2] + value.shape[1:])
                grads.append(reduced(value, len(shape) - 2))
            norm_grad = reduced(v[N.gain_norm][:4], 1)
            heads_grad = reduced(v[N.gain_heads][4:6], 1)
        return (mixed, tokens_grad) + tuple(grads[:4]) + (norm_grad, heads_grad) + tuple(grads[4:])

    return shards


def solution(mesh):
    both, rows = P(("dp", "own"), None), P("own", None)
    second, third = P(None, "own", None), P(None, None, "own", None)
    wide_gain = P(None, "own")
    in_specs = (
        (both, both, P("dp", None), P("dp", None), rows, rows, rows, rows, wide_gain, wide_gain)
        + (second, second, third, second, second, second, third, second, second)
    )
    out_specs = (
        (both, both, rows, rows, rows, rows, wide_gain, wide_gain)
        + (second, second, third, second, second, second, third, second, second)
    )
    return jax.shard_map(make_shards(mesh), mesh=mesh, in_specs=in_specs, out_specs=out_specs, check_vma=False)
```

```python
import math

import jax
import jax.numpy as jnp
from jax import lax
from jax.experimental import pallas as pl
from jax.experimental.pallas import tpu as pltpu
from jax.sharding import PartitionSpec as P

BF = jnp.bfloat16
F32 = jnp.float32
EPS = 1e-06
THETA = 1000000.0
LANES = 128
LOG2E = 1.4426950408889634
VMEM_LIMIT = 60 * 2**20
PEAK = 1e6
CORE, XBIT, YBIT = 1, 2, 4


def dot(a, b):
    return jnp.dot(a, b, preferred_element_type=F32)


def dot_nt(a, b):
    return lax.dot_general(a, b, (((1,), (1,)), ((), ())), preferred_element_type=F32)


def dot_tn(a, b):
    return lax.dot_general(a, b, (((0,), (0,)), ((), ())), preferred_element_type=F32)


def side_by_side(parts):
    return parts[0] if len(parts) == 1 else jnp.concatenate(parts, axis=1)


def stacked(parts):
    return parts[0] if len(parts) == 1 else jnp.concatenate(parts, axis=0)


class Name(str):
    def __call__(self, *more):
        return Name(self + str().join(str(m) for m in more))


class Names:
    def __getattr__(self, name):
        return Name(name)


N = Names()


class Sizes:
    pass


class Layout:
    def __init__(self, sizes, names, gains=False):
        self.at = {}
        total = 0
        for name in names:
            rows, blocks = sizes.shard[name]
            self.at[name] = (total, rows, blocks)
            total += rows * blocks
        self.gains = None
        if gains:
            self.gains = total
            total += 16
        self.total = total


class Chunk:
    def __init__(self, layout, pieces, ids):
        self.layout, self.pieces, self.ids, self.mine = layout, pieces, ids, pieces[0]


class Env:
    def __init__(self):
        self.refs = {}
        self.pending = {}
        self.later = []

    def __getitem__(self, name):
        return self.refs[name]

    def w(self, name):
        if name in self.pending:
            sem = self.pending.pop(name)
            ref = self.refs[N.w(name)]
            pltpu.make_async_copy(ref, ref, sem).wait()
            if name == self.hold:
                for copy in self.later:
                    copy.start()
                self.later = []
        return self.refs[N.w(name)]


def run_kernel(sizes, name, stages, ins, outs, scratch=(), weights=(), smem=(), micros=0, hold=None):
    chunks = []
    for _, chunk in weights:
        if chunk not in chunks:
            chunks.append(chunk)
    smem = dict(smem)
    for number, chunk in enumerate(chunks):
        smem[N.ids(number)] = chunk.ids
    scratch = dict(scratch)
    names_in = list(ins)
    names_smem = list(smem)
    pieces = [piece for chunk in chunks for piece in chunk.pieces]
    names_out = list(outs)
    names_scratch = list(scratch)
    shapes = []
    for wname, chunk in weights:
        if wname == N.gains:
            shapes.append(((sizes.slots, 16, LANES), BF))
        else:
            _, rows, blocks = chunk.layout.at[wname]
            shapes.append(((blocks, rows * sizes.slots, LANES), BF))

    def kernel(*refs):
        env = Env()
        env.hold, held = hold, False
        position = 0
        for key in names_smem + names_in:
            env.refs[key] = refs[position]
            position += 1
        piece_refs = refs[position : position + len(pieces)]
        position += len(pieces)
        for key in names_out + names_scratch:
            env.refs[key] = refs[position]
            position += 1
        of_chunk = {}
        start = 0
        for number, chunk in enumerate(chunks):
            of_chunk[number] = piece_refs[start : start + len(chunk.pieces)]
            start += len(chunk.pieces)
        for number, (wname, chunk) in enumerate(weights):
            buffer = refs[position]
            position += 1
            env.refs[N.w(wname)] = buffer
        for number, (wname, chunk) in enumerate(weights):
            sem = refs[position]
            position += 1
            buffer = env.refs[N.w(wname)]
            which = chunks.index(chunk)
            for slot in range(sizes.slots):
                piece = of_chunk[which][0 if len(chunk.pieces) == 1 else slot]
                offset = slot * chunk.layout.total if len(chunk.pieces) == 1 else 0
                if wname == N.gains:
                    source = piece.at[pl.ds(offset + chunk.layout.gains, 16), :]
                    target = buffer.at[slot]
                else:
                    first, rows, blocks = chunk.layout.at[wname]
                    first = offset + first
                    source = piece.at[pl.ds(first, blocks * rows), :].reshape(blocks, rows, LANES)
                    if sizes.slots == 1:
                        target = buffer
                    else:
                        row = pl.multiple_of(env[N.ids(which)][slot] * rows, 16)
                        target = buffer.at[:, pl.ds(row, rows), :]
                copy = pltpu.make_async_copy(source, target, sem)
                if held:
                    env.later.append(copy)
                else:
                    copy.start()
            env.pending[wname] = sem
            held = held or wname == hold
        env.ids = lambda chunk: env[N.ids(chunks.index(chunk))]
        for stage in stages:
            stage(env)
        for wname, _ in weights:
            env.w(wname)

    any_space = pl.BlockSpec(memory_space=pl.ANY)
    vmem = pl.BlockSpec(memory_space=pltpu.VMEM)
    nbytes = sum(math.prod(a.shape) * a.dtype.itemsize for a in list(ins.values()) + pieces)
    nbytes += sum(math.prod(s) * jnp.dtype(d).itemsize for s, d in outs.values())
    results = pl.pallas_call(
        kernel,
        name=name,
        out_shape=[jax.ShapeDtypeStruct(*outs[key]) for key in names_out],
        in_specs=[pl.BlockSpec(memory_space=pltpu.SMEM)] * len(names_smem)
        + [vmem] * len(names_in)
        + [any_space] * len(pieces),
        out_specs=[vmem] * len(names_out),
        scratch_shapes=[pltpu.VMEM(*scratch[key]) for key in names_scratch]
        + [pltpu.VMEM(*shape) for shape in shapes]
        + [pltpu.SemaphoreType.DMA] * len(weights),
        compiler_params=pltpu.CompilerParams(vmem_limit_bytes=VMEM_LIMIT),
        cost_estimate=pl.CostEstimate(flops=int(micros * PEAK), bytes_accessed=0, transcendentals=0),
    )(*smem.values(), *ins.values(), *pieces)
    return dict(zip(names_out, results))


def columns(weight, first, count, rows=None):
    if rows is None:
        return side_by_side([weight[first + i] for i in range(count)])
    return side_by_side([weight[first + i, rows] for i in range(count)])


def root(values):
    return lax.rsqrt(jnp.mean(values * values, axis=-1, keepdims=True) + EPS)


def rms_back(values, gain, grad):
    r = root(values)
    scaled = grad * gain
    back = r * scaled - values * (r * r * r * jnp.mean(values * scaled, axis=-1, keepdims=True))
    return back, jnp.sum(values * r * grad, axis=0, keepdims=True)


def rotate(values, cos, sin):
    half = values.shape[-1] // 2
    p, q = values[:, :half], values[:, half:]
    return jnp.concatenate([p * cos - q * sin, q * cos + p * sin], axis=1)


def rotate_back(grad, cos, sin):
    half = grad.shape[-1] // 2
    a, b = grad[:, :half], grad[:, half:]
    return jnp.concatenate([a * cos + b * sin, b * cos - a * sin], axis=1)


GELU_A = math.sqrt(2.0 / math.pi)
GELU_B = 0.044715


def gelu_parts(v):
    t = jnp.tanh(GELU_A * (v + GELU_B * v * v * v))
    return 0.5 * v * (1.0 + t), t


def gelu_slope(v, t):
    return 0.5 * (1.0 + t) + 0.5 * v * (1.0 - t * t) * (GELU_A * (1.0 + 3.0 * GELU_B * v * v))


def stage_gains(sizes, chunk):
    def stage(env):
        blocks = env.w(N.gains)
        ids = env.ids(chunk)
        norm = jnp.zeros((16, sizes.D), F32)
        heads = jnp.zeros((16, sizes.HD), F32)
        width, head_width = sizes.D // sizes.slots, sizes.HD // sizes.slots

        def pick(total, each, index):
            a = lax.broadcasted_iota(jnp.int32, (LANES, total), 0)
            b = lax.broadcasted_iota(jnp.int32, (LANES, total), 1)
            return jnp.where((b == a + index * each) & (a < each), 1.0, 0.0).astype(BF)

        for m in range(sizes.slots):
            norm = norm + dot(blocks[m], pick(sizes.D, width, ids[m]))
            heads = heads + dot(blocks[m], pick(sizes.HD, head_width, ids[m]))
        env[N.norm][...] = norm
        env[N.qkg][...] = heads

    return stage


def stage_qkv(sizes, l, stream):
    def stage(env):
        x = env[stream][...]
        attn_in = (x * root(x) * env[N.norm][0:1, :]).astype(BF)
        env[N.attn_in(l)][...] = attn_in
        first = env.w(N.aqkv)
        mids = []
        for j in range(3):
            mid = dot(attn_in, columns(first, sizes.RB * j, sizes.RB)).astype(BF)
            env[N.mid(l)][j] = mid
            mids.append(mid)
        qkv, hb = env.w(N.qkv), sizes.HB
        cos, sin = env[N.cos][...], env[N.sin][...]
        gq, gk = env[N.qkg][4:5, :], env[N.qkg][5:6, :]
        bk, bv, bq = env.w(N.bk), env.w(N.bv), env.w(N.bq)
        raw = dot(attn_in, columns(qkv, hb * sizes.H, hb)) + dot(mids[1], columns(bk, 0, hb))
        env[N.raw(l)][sizes.H] = raw
        env[N.kv(l)][:, : sizes.HD] = rotate(raw * root(raw) * gk, cos, sin).astype(BF)
        raw = dot(attn_in, columns(qkv, hb * (sizes.H + 1), hb)) + dot(mids[2], columns(bv, 0, hb))
        env[N.kv(l)][:, sizes.HD :] = raw.astype(BF)
        for h in range(sizes.H):
            raw = dot(attn_in, columns(qkv, hb * h, hb)) + dot(mids[0], columns(bq, hb * h, hb))
            env[N.raw(l)][h] = raw
            env[N.q(l)][h] = rotate(raw * root(raw) * gq, cos, sin).astype(BF)

    return stage


def key_block(sizes, pieces, b, value):
    lanes = slice(sizes.HD, 2 * sizes.HD) if value else slice(0, sizes.HD)
    rows = pl.ds(pl.multiple_of(b * sizes.IB, 16), sizes.IB)
    parts = []
    for piece in pieces:
        if len(piece.shape) == 3:
            parts += [piece[g, rows, lanes] for g in range(piece.shape[0])]
        else:
            parts.append(piece[rows, lanes])
    return stacked(parts)


def query_limits(sizes, env, qb):
    rows = slice(qb * sizes.QB, (qb + 1) * sizes.QB)
    slot = jnp.concatenate([env[N.qslot][rows, :]] * sizes.H, axis=0)
    low = jnp.concatenate([env[N.qstart][rows, :]] * sizes.H, axis=0)
    last = -(-(qb + 1) * sizes.QB // sizes.IB)
    return rows, slot, low, last


def stage_attend(sizes, l):
    scale = sizes.HD ** (-0.5) * LOG2E
    M = sizes.H * sizes.QB

    def stage(env):
        pieces = [env[N.kvp(l, i)] for i in range(sizes.kv_pieces)]
        for qb in range(sizes.T // sizes.QB):
            rows, slot, low, last = query_limits(sizes, env, qb)
            query = env[N.q(l)][:, rows, :].reshape(M, sizes.HD)
            env[N.o_acc][...] = jnp.zeros((M, sizes.HD), F32)
            env[N.l_acc][...] = jnp.zeros((M, LANES), F32)

            def body(b, carry):
                keys = env[N.kslot][b]
                scores = dot_nt(query, key_block(sizes, pieces, b, False))
                allowed = (keys <= slot) & (keys >= low)
                probs = jnp.where(allowed, jnp.exp2(scores * scale), 0.0)
                part = probs[:, :LANES]
                for i in range(1, probs.shape[1] // LANES):
                    part = part + probs[:, i * LANES : (i + 1) * LANES]
                env[N.l_acc][...] += part
                env[N.o_acc][...] += dot(probs.astype(BF), key_block(sizes, pieces, b, True))
                return carry

            lax.fori_loop(env[N.first_block][qb], last, body, 0)
            total = jnp.sum(env[N.l_acc][...], axis=1, keepdims=True)
            env[N.att(l)][:, rows, :] = (env[N.o_acc][...] / total).reshape(sizes.H, sizes.QB, sizes.HD)
            env[N.lse(l)][:, rows, :] = jnp.broadcast_to(jnp.log2(total), (M, LANES)).reshape(
                sizes.H, sizes.QB, LANES
            )

    return stage


def stage_out(sizes, l, stream):
    def stage(env):
        outa, outw, outb = env.w(N.outa), env.w(N.outw), env.w(N.outb)
        mid = jnp.zeros((sizes.T, sizes.R), F32)
        branch = jnp.zeros((sizes.T, sizes.D), F32)
        for h in range(sizes.H):
            heads = env[N.att(l)][h].astype(BF)
            env[N.ho(l)][h] = heads
            rows = slice(h * sizes.HD, (h + 1) * sizes.HD)
            mid = mid + dot(heads, columns(outa, 0, sizes.RB, rows))
            branch = branch + dot(heads, columns(outw, 0, sizes.DB, rows))
        mid = mid.astype(BF)
        env[N.omid(l)][...] = mid
        branch = branch + dot(mid, columns(outb, 0, sizes.DB))
        env[N.branch(l)][...] = branch
        middle = env[stream][...] + branch * root(branch) * env[N.norm][1:2, :]
        env[N.middle(l)][...] = middle
        env[N.ffn_in(l)][...] = (middle * root(middle) * env[N.norm][2:3, :]).astype(BF)

    return stage


def stage_ffn(sizes, l):
    def stage(env):
        x = env[N.ffn_in(l)][...]
        agu = env.w(N.agu)
        mids = []
        for j in range(2):
            mid = dot(x, columns(agu, sizes.RB * j, sizes.RB)).astype(BF)
            env[N.gmid(l)][j] = mid
            mids.append(mid)
        bg, bu, gu = env.w(N.bg), env.w(N.bu), env.w(N.gu)
        blocks = sizes.F // 256
        out = jnp.zeros((sizes.T, sizes.D), F32)
        down = jnp.zeros((sizes.T, sizes.R), F32)
        for b in range(blocks):
            gate = dot(x, columns(gu, 2 * b, 2)) + dot(mids[0], columns(bg, 2 * b, 2))
            up = dot(x, columns(gu, 2 * (blocks + b), 2)) + dot(mids[1], columns(bu, 2 * b, 2))
            env[N.gu(l)][b, :, :256] = gate.astype(env[N.gu(l)].dtype)
            env[N.gu(l)][b, :, 256:] = up.astype(env[N.gu(l)].dtype)
            hidden = (gelu_parts(gate)[0] * up).astype(BF)
            env[N.hidden(l)][b] = hidden
            rows = slice(b * 256, (b + 1) * 256)
            dnw, dna = env.w(N.dnw), env.w(N.dna)
            out = out + dot(hidden, columns(dnw, 0, sizes.DB, rows))
            down = down + dot(hidden, columns(dna, 0, sizes.RB, rows))
        down = down.astype(BF)
        env[N.dmid(l)][...] = down
        out = out + dot(down, columns(env.w(N.dnb), 0, sizes.DB))
        env[N.ffn_out(l)][...] = out
        env[N.stream(l + 1)][...] = env[N.middle(l)][...] + out * root(out) * env[N.norm][3:4, :]

    return stage


def stage_ffn_back(sizes, l, grad):
    def stage(env):
        out_grad = env[grad][...]
        back, gain = rms_back(env[N.ffn_out(l)][...], env[N.norm][3:4, :], out_grad)
        env[N.dnorm(l, 3)][...] = gain
        low = back.astype(BF)
        env[N.ffn_low(l)][...] = low
        dmg = dot_nt(low, columns(env.w(N.dnb), 0, sizes.DB)).astype(BF)
        env[N.dmg(l)][...] = dmg
        dnw, dna = env.w(N.dnw), env.w(N.dna)
        blocks = sizes.F // 256
        gate_mid = jnp.zeros((sizes.T, sizes.R), F32)
        up_mid = jnp.zeros((sizes.T, sizes.R), F32)
        total = jnp.zeros((sizes.T, sizes.D), F32)
        for b in range(blocks):
            rows = slice(b * 256, (b + 1) * 256)
            hidden_grad = dot_nt(low, columns(dnw, 0, sizes.DB, rows)) + dot_nt(
                dmg, columns(dna, 0, sizes.RB, rows)
            )
            gate, up = env[N.gu(l)][b, :, :256].astype(F32), env[N.gu(l)][b, :, 256:].astype(F32)
            value, t = gelu_parts(gate)
            gate_grad = (hidden_grad * up * gelu_slope(gate, t)).astype(BF)
            up_grad = (hidden_grad * value).astype(BF)
            env[N.gug(l)][b] = gate_grad
            env[N.gug(l)][blocks + b] = up_grad
            bg, bu, gu = env.w(N.bg), env.w(N.bu), env.w(N.gu)
            gate_mid = gate_mid + dot_nt(gate_grad, columns(bg, 2 * b, 2))
            up_mid = up_mid + dot_nt(up_grad, columns(bu, 2 * b, 2))
            total = total + dot_nt(gate_grad, columns(gu, 2 * b, 2))
            total = total + dot_nt(up_grad, columns(gu, 2 * (blocks + b), 2))
        agu = env.w(N.agu)
        for j, mid in enumerate((gate_mid, up_mid)):
            mid = mid.astype(BF)
            env[N.gmg(l)][j] = mid
            total = total + dot_nt(mid, columns(agu, sizes.RB * j, sizes.RB))
        back, gain = rms_back(env[N.middle(l)][...], env[N.norm][2:3, :], total)
        env[N.dnorm(l, 2)][...] = gain
        env[N.mgrad(l)][...] = out_grad + back

    return stage


def stage_out_back(sizes, l):
    def stage(env):
        back, gain = rms_back(env[N.branch(l)][...], env[N.norm][1:2, :], env[N.mgrad(l)][...])
        env[N.dnorm(l, 1)][...] = gain
        low = back.astype(BF)
        env[N.blow(l)][...] = low
        omg = dot_nt(low, columns(env.w(N.outb), 0, sizes.DB)).astype(BF)
        env[N.omg(l)][...] = omg
        outw, outa = env.w(N.outw), env.w(N.outa)
        for h in range(sizes.H):
            rows = slice(h * sizes.HD, (h + 1) * sizes.HD)
            grad = dot_nt(low, columns(outw, 0, sizes.DB, rows)) + dot_nt(omg, columns(outa, 0, sizes.RB, rows))
            env[N.hgrad(l)][h] = grad.astype(BF)

    return stage


def stage_attend_back(sizes, l):
    factor = sizes.HD ** (-0.5)
    scale = factor * LOG2E
    M = sizes.H * sizes.QB
    HD = sizes.HD

    def stage(env):
        pieces = [env[N.kvp(l, i)] for i in range(sizes.kv_pieces)]
        total_blocks = sizes.T // sizes.IB
        for b in range(total_blocks):
            env[N.dkv_acc][b] = jnp.zeros((sizes.n * sizes.IB, 2 * HD), F32)
        for qb in range(sizes.T // sizes.QB):
            rows, slot, low, last = query_limits(sizes, env, qb)
            query = env[N.q(l)][:, rows, :].reshape(M, HD)
            grad = env[N.hgrad(l)][:, rows, :].reshape(M, HD)
            attended = env[N.att(l)][:, rows, :].reshape(M, HD)
            row_dot = jnp.sum(grad.astype(F32) * attended, axis=1, keepdims=True)
            lse = env[N.lse(l)][:, rows, :].reshape(M, LANES)[:, 0:1]
            env[N.o_acc][...] = jnp.zeros((M, HD), F32)

            def body(b, carry):
                keys = env[N.kslot][b]
                k = key_block(sizes, pieces, b, False)
                v = key_block(sizes, pieces, b, True)
                allowed = (keys <= slot) & (keys >= low)
                probs = jnp.where(allowed, jnp.exp2(dot_nt(query, k) * scale - lse), 0.0)
                scores_grad = (probs * (dot_nt(grad, v) - row_dot)).astype(BF)
                env[N.o_acc][...] += dot(scores_grad, k)
                env[N.dkv_acc][b, :, :HD] += dot_tn(scores_grad, query)
                env[N.dkv_acc][b, :, HD:] += dot_tn(probs.astype(BF), grad)
                return carry

            lax.fori_loop(env[N.first_block][qb], last, body, 0)
            env[N.dq(l)][:, rows, :] = (env[N.o_acc][...] * factor).reshape(sizes.H, sizes.QB, HD)
        IB = sizes.IB
        for m in range(sizes.n):
            if sizes.slots > 1:
                where = (N.dkvkeep if m < sizes.n // 2 else N.dkvsend, m % (sizes.n // 2))
            else:
                where = (N.dkvkeep, m)
            for b in range(total_blocks):
                for j, by in enumerate((factor, 1.0)):
                    lanes = slice(j * HD, (j + 1) * HD)
                    part = env[N.dkv_acc][b, m * IB : (m + 1) * IB, lanes]
                    env[where[0](l)][where[1], b * IB : (b + 1) * IB, lanes] = (part * by).astype(BF)

    return stage


def stage_q_back(sizes, l):
    def stage(env):
        cos, sin = env[N.cos][...], env[N.sin][...]
        gq = env[N.qkg][4:5, :]
        hb = sizes.HB
        qkv, bq, aqkv = env.w(N.qkv), env.w(N.bq), env.w(N.aqkv)
        gains = jnp.zeros((1, sizes.HD), F32)
        mid = jnp.zeros((sizes.T, sizes.R), F32)
        total = jnp.zeros((sizes.T, sizes.D), F32)
        for h in range(sizes.H):
            turned = rotate_back(env[N.dq(l)][h], cos, sin)
            back, gain = rms_back(env[N.raw(l)][h], gq, turned)
            gains = gains + gain
            low = back.astype(BF)
            env[N.rawq_low(l)][h] = low
            mid = mid + dot_nt(low, columns(bq, hb * h, hb))
            total = total + dot_nt(low, columns(qkv, hb * h, hb))
        mid = mid.astype(BF)
        env[N.midgq(l)][...] = mid
        total = total + dot_nt(mid, columns(aqkv, 0, sizes.RB))
        env[N.agrad(l)][...] = total
        env[N.dqg(l)][...] = gains

    return stage


def stage_kv_back(sizes, l, stream, result):
    def stage(env):
        cos, sin = env[N.cos][...], env[N.sin][...]
        hb = sizes.HB
        qkv, aqkv = env.w(N.qkv), env.w(N.aqkv)
        turned = rotate_back(env[N.dkv][:, : sizes.HD].astype(F32), cos, sin)
        back, gain = rms_back(env[N.raw(l)][sizes.H], env[N.qkg][5:6, :], turned)
        env[N.dkg(l)][...] = gain
        total = env[N.agrad(l)][...]
        for j, (low, second) in enumerate(((back.astype(BF), N.bk), (env[N.dkv][:, sizes.HD :], N.bv))):
            env[N.rawkv_low(l)][j] = low
            mid = dot_nt(low, columns(env.w(second), 0, hb)).astype(BF)
            env[N.midgkv(l)][j] = mid
            total = total + dot_nt(low, columns(qkv, hb * (sizes.H + j), hb))
            total = total + dot_nt(mid, columns(aqkv, sizes.RB * (j + 1), sizes.RB))
        back, gain = rms_back(env[stream][...], env[N.norm][0:1, :], total)
        env[N.dnorm(l, 0)][...] = gain
        env[result][...] = env[N.mgrad(l)][...] + back

    return stage


def put(sizes, env, layout, prefix, name, block, value, first_row=0):
    first, rows, _ = layout.at[name]
    count = value.shape[1] // LANES
    keep = env[N.keep(prefix)]
    if sizes.slots == 1:
        value = value.astype(BF)
        for i in range(count):
            at = first + (block + i) * rows + first_row
            keep[0, at : at + value.shape[0], :] = value[:, i * LANES : (i + 1) * LANES]
        return
    send = env[N.send(prefix)]
    core, chip = env[N.place][0], env[N.place][1]
    even_stays = core == 0
    for pair in range(value.shape[0] // (2 * rows)):
        a = value[2 * pair * rows : (2 * pair + 1) * rows]
        b = value[(2 * pair + 1) * rows : (2 * pair + 2) * rows]
        stays = jnp.where(even_stays, a, b).astype(BF)
        goes = jnp.where(even_stays, b, a).astype(BF)
        slot = jnp.bitwise_xor(first_row // (2 * rows) + pair, chip)
        for i in range(count):
            at = first + (block + i) * rows
            keep[slot, at : at + rows, :] = stays[:, i * LANES : (i + 1) * LANES]
            send[slot, at : at + rows, :] = goes[:, i * LANES : (i + 1) * LANES]


def grad_product(sizes, env, layout, prefix, name, lefts, rights, first_block=0, first_row=0):
    left = stacked([a.T if len(lefts) == 1 else a.T for a in lefts]) if len(lefts) == 1 else side_by_side(
        [a.T for a in lefts]
    )
    for block, right in rights:
        value = dot(left, stacked(right))
        put(sizes, env, layout, prefix, name, first_block + block, value, first_row)


def wide(ref, width, step=256):
    out = []
    at = 0
    while at < width:
        size = min(step, width - at)
        out.append((at // LANES, slice(at, at + size)))
        at += size
    return out


def grads_ffn_wide(sizes, env, layout, prefix, names, loops, pl_l):
    blocks = sizes.F // 256
    for j, name in enumerate((N.gug, N.guu)):
        if name in names:
            left = [env[N.ffn_in(l)][...] for l in loops]
            rights = [(2 * b, [env[N.gug(l)][j * blocks + b] for l in loops]) for b in range(blocks)]
            grad_product(sizes, env, layout, prefix, name, left, rights)
    if N.agu in names:
        rights = [(sizes.RB * j, [env[N.gmg(pl_l)][j]]) for j in range(2)]
        grad_product(sizes, env, layout, prefix, N.agu, [env[N.ffn_in(pl_l)][...]], rights)
    for j, name in enumerate((N.bg, N.bu)):
        if name in names:
            rights = [(2 * b, [env[N.gug(pl_l)][j * blocks + b]]) for b in range(blocks)]
            grad_product(sizes, env, layout, prefix, name, [env[N.gmid(pl_l)][j]], rights)


def grads_ffn_down(sizes, env, layout, prefix, names, loops, pl_l):
    blocks = sizes.F // 256
    step = 512
    for b in range(0, blocks, 2):
        row = b * 256
        if N.dnw in names:
            left = [side_by_side([env[N.hidden(l)][b], env[N.hidden(l)][b + 1]]) for l in loops]
            rights = [(i, [env[N.ffn_low(l)][:, s] for l in loops]) for i, s in wide(None, sizes.D, 640)]
            grad_product(sizes, env, layout, prefix, N.dnw, left, rights, 0, row)
        if N.dna in names:
            left = [side_by_side([env[N.hidden(pl_l)][b], env[N.hidden(pl_l)][b + 1]])]
            grad_product(sizes, env, layout, prefix, N.dna, left, [(0, [env[N.dmg(pl_l)][...]])], 0, row)
    if N.dnb in names:
        grad_product(
            sizes, env, layout, prefix, N.dnb, [env[N.dmid(pl_l)][...]], [(0, [env[N.ffn_low(pl_l)][...]])]
        )


def grads_out(sizes, env, layout, prefix, names, loops, pl_l):
    for h in range(0, sizes.H, 2):
        row = h * sizes.HD
        if N.outw in names:
            left = [side_by_side([env[N.ho(l)][h], env[N.ho(l)][h + 1]]) for l in loops]
            grad_product(
                sizes, env, layout, prefix, N.outw, left, [(0, [env[N.blow(l)][...] for l in loops])], 0, row
            )
        if N.outa in names:
            left = [side_by_side([env[N.ho(pl_l)][h], env[N.ho(pl_l)][h + 1]])]
            grad_product(sizes, env, layout, prefix, N.outa, left, [(0, [env[N.omg(pl_l)][...]])], 0, row)
    if N.outb in names:
        grad_product(
            sizes, env, layout, prefix, N.outb, [env[N.omid(pl_l)][...]], [(0, [env[N.blow(pl_l)][...]])]
        )


def grads_qkv(sizes, env, layout, prefix, names, loops, pl_l):
    hb = sizes.HB
    left = [env[N.attn_in(l)][...] for l in loops] if {N.qkvq, N.qkvkv} & set(names) else None
    if N.qkvq in names:
        rights = [(hb * h, [env[N.rawq_low(l)][h] for l in loops]) for h in range(sizes.H)]
        grad_product(sizes, env, layout, prefix, N.qkvq, left, rights)
    if N.qkvkv in names:
        rights = [(hb * j, [env[N.rawkv_low(l)][j] for l in loops]) for j in range(2)]
        grad_product(sizes, env, layout, prefix, N.qkvkv, left, rights)
    first = ([(0, N.midgq(pl_l), None)] if {N.aqkv, N.aqkvq} & set(names) else []) + (
        [(sizes.RB * j, N.midgkv(pl_l), j) for j in range(2)] if {N.aqkv, N.aqkvkv} & set(names) else []
    )
    for name in (N.aqkv, N.aqkvq, N.aqkvkv):
        if name in names:
            rights = [
                (at + (sizes.RB if name == N.aqkv and j is not None else 0), [env[ref][...] if j is None else env[ref][j]])
                for at, ref, j in first
            ]
            grad_product(sizes, env, layout, prefix, name, [env[N.attn_in(pl_l)][...]], rights)
    if N.bq in names:
        rights = [(hb * h, [env[N.rawq_low(pl_l)][h]]) for h in range(sizes.H)]
        grad_product(sizes, env, layout, prefix, N.bq, [env[N.mid(pl_l)][0]], rights)
    for j, name in enumerate((N.bk, N.bv)):
        if name in names:
            grad_product(
                sizes, env, layout, prefix, name, [env[N.mid(pl_l)][j + 1]], [(0, [env[N.rawkv_low(pl_l)][j]])]
            )


def stage_grads(sizes, parts):
    def stage(env):
        for prefix, layout, names, loops, pl_l in parts:
            for build in (grads_ffn_wide, grads_ffn_down, grads_out, grads_qkv):
                build(sizes, env, layout, prefix, names, loops, pl_l)

    return stage


def stage_gain_grads(sizes, prefix, layout):
    def stage(env):
        norm = stacked(
            [env[N.dnorm(0, i)][...] + env[N.dnorm(1, i)][...] for i in range(4)] + [jnp.zeros((12, sizes.D), F32)]
        )
        heads = stacked(
            [jnp.zeros((4, sizes.HD), F32)]
            + [env[kind(0)][...] + env[kind(1)][...] for kind in (N.dqg, N.dkg)]
            + [jnp.zeros((10, sizes.HD), F32)]
        )
        if sizes.slots == 1:
            env[N.gain_norm][...] = norm
            env[N.gain_heads][...] = heads
            return
        norm, heads = norm.astype(BF), heads.astype(BF)
        width, head_width = sizes.D // sizes.slots, sizes.HD // sizes.slots

        def pick(total, each, index):
            a = lax.broadcasted_iota(jnp.int32, (total, LANES), 0)
            b = lax.broadcasted_iota(jnp.int32, (total, LANES), 1)
            return jnp.where((a == b + index * each) & (b < each), 1.0, 0.0).astype(BF)

        at = layout.gains
        chip, core = env[N.place][1], env[N.place][0]
        for k in range(sizes.slots // 2):
            for name, flip in ((N.keep, core), (N.send, 1 - core)):
                index = 2 * jnp.bitwise_xor(k, chip) + flip
                block = dot(norm, pick(sizes.D, width, index)) + dot(heads, pick(sizes.HD, head_width, index))
                env[name(prefix)][k, at : at + 16, :] = block.astype(BF)

    return stage


def pack(sizes, layout, arrays, gains=None):
    names = list(layout.at)
    unique = []
    for name in names:
        if not any(arrays[name][0] is u for u in unique):
            unique.append(arrays[name][0])
    extra = [] if layout.gains is None else [gains]

    def kernel(*refs):
        out = refs[-1]
        for name in names:
            array, lead = arrays[name]
            source = refs[[array is u for u in unique].index(True)]
            first, rows, blocks = layout.at[name]
            for b in range(blocks):
                out[first + b * rows : first + (b + 1) * rows, :] = source[
                    lead + (slice(None), slice(b * LANES, (b + 1) * LANES))
                ]
        if layout.gains is not None:
            out[layout.gains : layout.gains + 16, :] = refs[len(unique)][...]

    return pl.pallas_call(
        kernel,
        name=N.pack,
        out_shape=jax.ShapeDtypeStruct((layout.total, LANES), BF),
        compiler_params=pltpu.CompilerParams(vmem_limit_bytes=VMEM_LIMIT),
        cost_estimate=pl.CostEstimate(flops=0, bytes_accessed=4 * layout.total * LANES, transcendentals=0),
    )(*unique, *extra)


def sort_rows(sizes, rank, *arrays):
    def kernel(rank_ref, *refs):
        count = len(refs) // 2
        place = lax.broadcasted_iota(jnp.int32, (sizes.T, sizes.T), 0)
        matrix = jnp.where(place == rank_ref[...], 1.0, 0.0).astype(BF)
        for source, target in zip(refs[:count], refs[count:]):
            target[...] = dot(matrix, source[...])

    return pl.pallas_call(
        kernel,
        name=N.sort_rows,
        out_shape=[jax.ShapeDtypeStruct(a.shape, F32) for a in arrays],
        compiler_params=pltpu.CompilerParams(vmem_limit_bytes=VMEM_LIMIT),
        cost_estimate=pl.CostEstimate(flops=0, bytes_accessed=2**21, transcendentals=0),
    )(rank, *arrays)


def unsort_rows(sizes, rank, value):
    def kernel(rank_ref, source, target):
        place = lax.broadcasted_iota(jnp.int32, (sizes.T, sizes.T), 0)
        matrix = jnp.where(place == rank_ref[...], 1.0, 0.0).astype(BF)
        target[...] = dot_tn(matrix, source[...].astype(BF)).astype(BF)

    return pl.pallas_call(
        kernel,
        name=N.unsort_rows,
        out_shape=jax.ShapeDtypeStruct(value.shape, BF),
        compiler_params=pltpu.CompilerParams(vmem_limit_bytes=VMEM_LIMIT),
        cost_estimate=pl.CostEstimate(flops=0, bytes_accessed=2**20, transcendentals=0),
    )(rank, value)


def unpack(sizes, targets, sources):
    names = list(sources)
    shapes = [jax.ShapeDtypeStruct(shape, F32) for shape, _ in targets]

    def kernel(*refs):
        ins = {name: refs[2 * i : 2 * i + 2] for i, name in enumerate(names)}
        outs = refs[2 * len(names) :]

        def rows_of(prefix, first, count):
            low, high = ins[prefix]
            half = low.shape[0]
            if first + count <= half:
                return low[first : first + count, :].astype(F32)
            if first >= half:
                return high[first - half : first + count - half, :].astype(F32)
            return jnp.concatenate(
                [low[first:half, :].astype(F32), high[: first + count - half, :].astype(F32)], axis=0
            )

        for out, (_, parts) in zip(outs, targets):
            for lead, prefix, name, column in parts:
                layout = sources[prefix][2]
                if name == N.norm:
                    first, count = lead
                    out[...] = rows_of(prefix, layout.gains, 16)[first : first + count, : out.shape[1]]
                    continue
                first, rows, blocks = layout.at[name]
                for b in range(blocks):
                    out[lead + (slice(None), slice((column + b) * LANES, (column + b + 1) * LANES))] = rows_of(
                        prefix, first + b * rows, rows
                    )

    return pl.pallas_call(
        kernel,
        name=N.unpack,
        out_shape=shapes,
        compiler_params=pltpu.CompilerParams(vmem_limit_bytes=VMEM_LIMIT),
        cost_estimate=pl.CostEstimate(flops=0, bytes_accessed=2**22, transcendentals=0),
    )(*[half for name in names for half in sources[name][:2]])


def swap(sizes, value, bit):
    return lax.ppermute(value, "own", [(i, i ^ bit) for i in range(sizes.n)])


def along(value, pairs):
    return lax.ppermute(value, "dp", pairs)


def after_all(values, others):
    others = [o for o in others if not any(o is value for value in values)]
    count = len(values)

    def kernel(*refs):
        pass

    space = pl.BlockSpec(memory_space=pl.ANY)
    return pl.pallas_call(
        kernel,
        name=N.after,
        out_shape=[jax.ShapeDtypeStruct(value.shape, value.dtype) for value in values],
        in_specs=[space] * (count + len(others)),
        out_specs=[space] * count,
        input_output_aliases={i: i for i in range(count)},
        cost_estimate=pl.CostEstimate(flops=0, bytes_accessed=0, transcendentals=0),
    )(*values, *others)


def after(value, *others):
    return after_all([value], others)[0]


def gather_plain(sizes, mine, x_first, others=()):
    px, py = swap(sizes, mine, XBIT), swap(sizes, mine, YBIT)
    px = after(px, *others) if others else px
    pd = swap(sizes, px, YBIT) if x_first else swap(sizes, py, XBIT)
    here = [mine, px, py, pd]
    return here + [swap(sizes, piece, CORE) for piece in here]


def gather_direct(sizes, mine):
    here = [mine] + [swap(sizes, mine, bit) for bit in (XBIT, YBIT, XBIT | YBIT)]
    return here + [swap(sizes, piece, CORE) for piece in here]


PIECES = (0, XBIT, YBIT, XBIT | YBIT, CORE, CORE | XBIT, CORE | YBIT, CORE | XBIT | YBIT)


def gather_paired(sizes, mine, odd, others=()):
    px = swap(sizes, mine, XBIT)
    chosen = jnp.where(odd, px, mine)
    py = swap(sizes, after(chosen, *others) if others else chosen, YBIT)
    pz = along(py, [(0, 1), (1, 0), (2, 3), (3, 2)])
    here = [mine, px, py, pz]
    return here + [swap(sizes, piece, CORE) for piece in here]


def add(first, *others):
    total = first.astype(F32)
    for other in others:
        total = total + other.astype(F32)
    return total.astype(BF)


class Sum:
    def __init__(self, sizes, keep, send, mode, odd=None):
        self.sizes, self.keep, self.mode, self.odd = sizes, keep, mode, odd
        self.payload, self.done = [send], []
        self.steps = [self.core] + ([self.direct] if mode == N.direct else [self.near, self.far])
        self.steps += [self.trade, self.level, self.back]

    def step(self):
        now = self.steps.pop(0)
        now(self.payload)

    def swap(self, value, bit):
        return swap(self.sizes, value, bit)

    def core(self, sent):
        here, come = self.keep, self.swap(sent[0], CORE)
        if self.mode == N.direct:
            self.keep, *self.payload = [add(here[k], come[k]) for k in range(4)]
            return
        if self.mode == N.x:
            here, come = [a.reshape((2, 2) + a.shape[1:]) for a in (here, come)]
            pairs = [(here[:, i], come[:, i]) for i in range(2)]
        else:
            pairs = [(here[i : i + 2], come[i : i + 2]) for i in (0, 2)]
        self.keep, self.payload = add(*pairs[0]), [add(*pairs[1])]

    def direct(self, sent):
        come = [self.swap(value, bit) for value, bit in zip(sent, (XBIT, YBIT, XBIT | YBIT))]
        self.level_in(add(self.keep, *come))

    def near(self, sent):
        come = self.swap(sent[0], XBIT if self.mode == N.x else YBIT)
        self.keep, self.payload = add(self.keep[0], come[0]), [add(self.keep[1], come[1])]

    def far(self, sent):
        self.level_in(add(self.keep, self.swap(sent[0], YBIT if self.mode == N.x else XBIT)))

    def level_in(self, total):
        self.plane_total = total
        if self.odd is None:
            self.payload = [total]
            return
        rows = total.shape[0] // 2
        low, high = total[:rows], total[rows:]
        self.keep, self.payload = jnp.where(self.odd, high, low), [jnp.where(self.odd, low, high)]

    def trade(self, sent):
        self.payload = [add(self.keep, along(sent[0], [(0, 1), (1, 0), (2, 3), (3, 2)]))]

    def level(self, sent):
        self.payload = [add(sent[0], along(sent[0], [(0, 2), (2, 0), (1, 3), (3, 1)]))]

    def back(self, sent):
        come = along(sent[0], [(0, 1), (1, 0), (2, 3), (3, 2)])
        self.halves = (jnp.where(self.odd, come, sent[0]), jnp.where(self.odd, sent[0], come))
        self.payload = list(self.halves)


def make_shards(mesh):
    n, planes = mesh.shape["own"], mesh.shape["dp"]
    fast = n == 8 and planes == 4

    def shards(
        tokens,
        cotangent,
        lengths,
        row_packed_slot,
        shared_attention_matrix,
        shared_output_matrix,
        shared_gate_up_matrix,
        shared_down_matrix,
        norm_gain_table,
        query_key_gains,
        adapter_attention_first,
        adapter_query_second,
        adapter_key_value_second,
        adapter_output_first,
        adapter_output_second,
        adapter_gate_first,
        adapter_gate_second,
        adapter_down_first,
        adapter_down_second,
    ):
        s = Sizes()
        s.n, s.slots = n, (8 if fast else 1)
        s.T, s.D = tokens.shape
        s.HD = adapter_key_value_second.shape[3]
        s.H = adapter_query_second.shape[2] // s.HD
        s.R = adapter_query_second.shape[1] * n
        s.F = shared_down_matrix.shape[0] * n
        s.DB, s.RB, s.HB = s.D // LANES, s.R // LANES, s.HD // LANES
        s.IB = max(16, 1024 // n)
        s.QB = s.T // 4
        s.kv_pieces = 8 if fast else 1
        QW, k = s.H * s.HD, s.slots
        s.shard = {
            N.qkv: (s.D // k, (QW + 2 * s.HD) // LANES),
            N.aqkv: (s.D // k, 3 * s.RB),
            N.gug: (s.D // k, s.F // LANES),
            N.guu: (s.D // k, s.F // LANES),
            N.qkvq: (s.D // k, QW // LANES),
            N.qkvkv: (s.D // k, 2 * s.HB),
            N.aqkvq: (s.D // k, s.RB),
            N.aqkvkv: (s.D // k, 2 * s.RB),
            N.bq: (s.R // k, QW // LANES),
            N.bk: (s.R // k, s.HB),
            N.bv: (s.R // k, s.HB),
            N.outw: (QW // k, s.DB),
            N.outa: (QW // k, s.RB),
            N.outb: (s.R // k, s.DB),
            N.gu: (s.D // k, 2 * s.F // LANES),
            N.agu: (s.D // k, 2 * s.RB),
            N.bg: (s.R // k, s.F // LANES),
            N.bu: (s.R // k, s.F // LANES),
            N.dnw: (s.F // k, s.DB),
            N.dna: (s.F // k, s.RB),
            N.dnb: (s.R // k, s.DB),
        }
        own, plane = lax.axis_index("own"), lax.axis_index("dp")

        plain_ids = jnp.stack([own ^ m for m in PIECES]).astype(jnp.int32) if fast else jnp.zeros((1,), jnp.int32)
        slots = row_packed_slot[0]
        seq = lengths[0]
        my_slots = lax.dynamic_slice_in_dim(slots, own * s.T, s.T)
        rank = (my_slots // n).reshape(1, s.T)
        rest = slots.reshape(n, s.T)[:, 0] % n
        my_rest = my_slots[0] % n
        counts = jnp.arange(seq.shape[0])
        ends = jnp.sum(jnp.where(counts[None, :] <= counts[:, None], seq[None, :], 0), axis=1)
        sorted_slots = n * jnp.arange(s.T, dtype=jnp.int32) + my_rest
        past = sorted_slots[:, None] >= ends[None, :]
        starts = jnp.sum(jnp.where(past, seq[None, :], 0), axis=1)
        position = sorted_slots - starts
        inverse = THETA ** (-jnp.arange(s.HD // 2, dtype=F32) * 2.0 / s.HD)
        angles = position.astype(F32)[:, None] * inverse[None, :]
        block_slots = s.IB * n
        first_block = starts.reshape(4, s.QB)[:, 0] // block_slots
        key_rest = rest
        if fast:
            key_rest = jnp.sum(
                jnp.where(plain_ids[:, None] == jnp.arange(n)[None, :], rest[None, :], 0), axis=1
            )
        along_rows = jnp.arange(s.T, dtype=jnp.int32).reshape(s.T // s.IB, 1, 1, s.IB) * n
        kslot = (along_rows + key_rest.reshape(1, 1, n, 1)).reshape(s.T // s.IB, 1, n * s.IB).astype(jnp.int32)
        stream0, cot = sort_rows(s, rank, tokens, cotangent)

        v = {
            N.cos: jnp.cos(angles),
            N.sin: jnp.sin(angles),
            N.qslot: sorted_slots.reshape(s.T, 1),
            N.qstart: starts.reshape(s.T, 1).astype(jnp.int32),
            N.kslot: kslot,
            N.stream0: stream0,
            N.cot: cot,
        }
        def full(array, axis):
            return array if fast else lax.all_gather(array, "own", axis=axis, tiled=True)

        w_att, w_out = full(shared_attention_matrix, 0), full(shared_output_matrix, 0)
        w_gu, w_dn = full(shared_gate_up_matrix, 0), full(shared_down_matrix, 0)
        a_att, b_q = full(adapter_attention_first, 1), full(adapter_query_second, 1)
        b_kv, a_out = full(adapter_key_value_second, 2), full(adapter_output_first, 1)
        b_out, a_gu = full(adapter_output_second, 1), full(adapter_gate_first, 1)
        b_gu, a_dn = full(adapter_gate_second, 2), full(adapter_down_first, 1)
        b_dn = full(adapter_down_second, 1)

        def arrays_of(l):
            return {
                N.qkv: (w_att, ()),
                N.aqkv: (a_att, (l,)),
                N.bq: (b_q, (l,)),
                N.bk: (b_kv, (l, 0)),
                N.bv: (b_kv, (l, 1)),
                N.outw: (w_out, ()),
                N.outa: (a_out, (l,)),
                N.outb: (b_out, (l,)),
                N.gu: (w_gu, ()),
                N.agu: (a_gu, (l,)),
                N.bg: (b_gu, (l, 0)),
                N.bu: (b_gu, (l, 1)),
                N.dnw: (w_dn, ()),
                N.dna: (a_dn, (l,)),
                N.dnb: (b_dn, (l,)),
            }

        q_names, o_names = (N.qkv, N.aqkv, N.bq, N.bk, N.bv), (N.outw, N.outa, N.outb)
        g_names, d_names = (N.gu, N.agu, N.bg, N.bu), (N.dnw, N.dna, N.dnb)
        lq_names, lr_names = (N.aqkv, N.bq, N.bk, N.bv), (N.outa, N.outb, N.agu, N.bg, N.bu, N.dna, N.dnb)
        odd = (plane & 1) == 1
        inner = (plane == 1) | (plane == 2)
        paired_ids = plain_ids
        if fast:
            over_y = jnp.where(odd, XBIT | YBIT, YBIT)
            over_z = jnp.where(odd, YBIT, XBIT | YBIT)
            order = [0, XBIT, over_y, over_z]
            paired_ids = jnp.stack([own ^ m for m in order] + [own ^ m ^ CORE for m in order]).astype(jnp.int32)
        gain_block = None
        if fast:
            gain_block = jnp.concatenate(
                [
                    jnp.pad(norm_gain_table, ((0, 0), (0, LANES - norm_gain_table.shape[1]))),
                    jnp.pad(query_key_gains, ((0, 0), (0, LANES - query_key_gains.shape[1]))),
                    jnp.zeros((10, LANES), BF),
                ],
                axis=0,
            )

        def packed(names, l, gains=False, of=()):
            layout = Layout(s, names, gains)
            arrays = {m: arrays_of(k)[m] for m, k in of} if of else arrays_of(l)
            return layout, pack(s, layout, arrays, gain_block)

        def fetch(made, scheme, start=None, turn=()):
            layout, mine = made
            if not fast:
                return Chunk(layout, [mine], plain_ids)
            if scheme == N.y:
                over = [after(mine, start.pieces[1]), after(mine, start.pieces[3])]
                px, py = swap(s, over[0], XBIT), swap(s, over[1], YBIT)
                here = [mine, px, py, swap(s, py, XBIT)]
                chunk = Chunk(layout, here + [swap(s, piece, CORE) for piece in here], plain_ids)
                chunk.gates = over
                return chunk
            if start is not None:
                mine = after(mine, *start)
            if scheme == N.whole:
                whole = Chunk(layout, [lax.all_gather(mine, "own", axis=0, tiled=True)], jnp.arange(n, dtype=jnp.int32))
                whole.mine = mine
                return whole
            if scheme == N.direct:
                return Chunk(layout, gather_direct(s, mine), plain_ids)
            if scheme == N.paired:
                return Chunk(layout, gather_paired(s, mine, odd, turn), paired_ids)
            return Chunk(layout, gather_plain(s, mine, scheme == N.x, turn), plain_ids)

        pack_g, pack_q = packed(g_names + d_names, 0), packed(q_names, 0, gains=fast)
        pack_lr = packed(lr_names, 1)
        first = [(m, 0) for m in o_names] + [(m, 1) for m in lq_names]
        pack_o = packed(o_names + lq_names, None, of=first)
        chunk_g = fetch(pack_g, N.whole)
        chunk_q = fetch(pack_q, N.x, None, (stream0, v[N.cos], pack_g[1], pack_o[1], pack_lr[1]))
        chunk_o = fetch(pack_o, N.y, chunk_q)
        chunk_lq = chunk_o
        if fast:
            v[N.stream0] = after(v[N.stream0], *chunk_o.gates)
        loop0 = {**{m: chunk_q for m in q_names}, **{m: chunk_o for m in o_names}}
        loop0 |= {m: chunk_g for m in g_names + d_names}
        of_loop = [loop0]

        def wts(names, l):
            return [(m, of_loop[l][m]) for m in names]

        T, D, HD, H, R, F = s.T, s.D, s.HD, s.H, s.R, s.F
        blocks = F // 256
        half = n // 2 if fast else n
        shapes = {
            N.norm: ((16, D), F32),
            N.qkg: ((16, HD), F32),
            N.stream1: ((T, D), F32),
            N.stream2: ((T, D), F32),
            N.o_acc: ((H * s.QB, HD), F32),
            N.l_acc: ((H * s.QB, LANES), F32),
            N.dkv_acc: ((T // s.IB, n * s.IB, 2 * HD), F32),
            N.sgrad1: ((T, D), F32),
            N.sgrad0: ((T, D), F32),
            N.gain_norm: ((16, D), F32),
            N.gain_heads: ((16, HD), F32),
        }
        for l in (0, 1):
            shapes |= {
                N.attn_in(l): ((T, D), BF),
                N.mid(l): ((3, T, R), BF),
                N.raw(l): ((H + 1, T, HD), F32),
                N.q(l): ((H, T, HD), BF),
                N.kv(l): ((T, 2 * HD), BF),
                N.att(l): ((H, T, HD), F32),
                N.lse(l): ((H, T, LANES), F32),
                N.ho(l): ((H, T, HD), BF),
                N.omid(l): ((T, R), BF),
                N.branch(l): ((T, D), F32),
                N.middle(l): ((T, D), F32),
                N.ffn_in(l): ((T, D), BF),
                N.gmid(l): ((2, T, R), BF),
                N.gu(l): ((blocks, T, 512), BF if l == 0 else F32),
                N.hidden(l): ((blocks, T, 256), BF),
                N.dmid(l): ((T, R), BF),
                N.ffn_out(l): ((T, D), F32),
                N.ffn_low(l): ((T, D), BF),
                N.dmg(l): ((T, R), BF),
                N.gug(l): ((2 * blocks, T, 256), BF),
                N.gmg(l): ((2, T, R), BF),
                N.mgrad(l): ((T, D), F32),
                N.blow(l): ((T, D), BF),
                N.omg(l): ((T, R), BF),
                N.hgrad(l): ((H, T, HD), BF),
                N.dq(l): ((H, T, HD), F32),
                N.dkvkeep(l): ((half, T, 2 * HD), BF),
                N.dkvsend(l): ((half, T, 2 * HD), BF),
                N.rawq_low(l): ((H, T, HD), BF),
                N.rawkv_low(l): ((2, T, HD), BF),
                N.midgq(l): ((T, R), BF),
                N.midgkv(l): ((2, T, R), BF),
                N.agrad(l): ((T, D), F32),
                N.dqg(l): ((1, HD), F32),
                N.dkg(l): ((1, HD), F32),
            }
            for i in range(4):
                shapes[N.dnorm(l, i)] = ((1, D), F32)

        def call(name, stages, ins, outs, scratch=(), weights=(), smem=(), micros=0, hold=None):
            made = run_kernel(
                s,
                name,
                stages,
                {m: v[m] for m in ins},
                {m: shapes[m] for m in outs},
                {m: shapes[m] for m in scratch},
                weights,
                {m: v[m] for m in smem},
                micros,
                hold,
            )
            v.update(made)

        v[N.first_block] = first_block.astype(jnp.int32)
        v[N.place] = jnp.stack([own & 1, own >> 1]).astype(jnp.int32)

        def share_kv(l):
            if fast:
                pieces = gather_direct(s, v[N.kv(l)])
            else:
                gathered = lax.all_gather(v[N.kv(l)], "own", axis=0, tiled=False)
                pieces = [gathered]
            for i, piece in enumerate(pieces):
                v[N.kvp(l, i)] = piece

        def kv_names(l):
            return [N.kvp(l, i) for i in range(s.kv_pieces)]

        qkv_outs = [N.attn_in, N.mid, N.raw, N.q, N.kv]

        def fill(names, l):
            return [m(l) for m in names]

        if fast:
            call(
                N.qkv0,
                [stage_gains(s, chunk_q), stage_qkv(s, 0, N.stream0)],
                [N.stream0, N.cos, N.sin],
                [N.norm, N.qkg] + fill(qkv_outs, 0),
                weights=[(N.gains, chunk_q)] + wts(q_names, 0),
                micros=6.5,
            )
        else:
            norm = lax.all_gather(norm_gain_table, "own", axis=1, tiled=True).astype(F32)
            heads = lax.all_gather(query_key_gains, "own", axis=1, tiled=True).astype(F32)
            v[N.norm] = jnp.pad(norm, ((0, 12), (0, 0)))
            v[N.qkg] = jnp.pad(heads, ((4, 10), (0, 0)))
            call(
                N.qkv0,
                [stage_qkv(s, 0, N.stream0)],
                [N.stream0, N.cos, N.sin, N.norm, N.qkg],
                fill(qkv_outs, 0),
                weights=wts(q_names, 0),
                micros=6.5,
            )
        share_kv(0)
        if fast:
            mine = after(pack_lr[1], v[N.kvp(0, 3)])
            here = [mine] + [swap(s, mine, bit) for bit in (XBIT, YBIT, XBIT | YBIT)]
        of_loop.append({**loop0, **{m: chunk_lq for m in lq_names}})
        att_ins = [N.qslot, N.qstart, N.kslot]
        out_outs = [N.att, N.lse, N.ho, N.omid, N.branch, N.middle, N.ffn_in]
        ffn_outs = [N.gmid, N.gu, N.hidden, N.dmid, N.ffn_out]
        call(
            N.attend0,
            [stage_attend(s, 0), stage_out(s, 0, N.stream0)],
            [N.stream0, N.q0, N.norm] + att_ins + kv_names(0),
            fill(out_outs, 0),
            scratch=[N.o_acc, N.l_acc],
            weights=wts(o_names, 0),
            smem=[N.first_block],
            micros=11,
        )
        call(
            N.ffn0,
            [stage_ffn(s, 0), stage_qkv(s, 1, N.stream1)],
            [N.ffn_in0, N.middle0, N.norm, N.qkg, N.cos, N.sin],
            fill(ffn_outs, 0) + [N.stream1] + fill(qkv_outs, 1),
            weights=wts((N.agu, N.gu, N.bg, N.bu) + d_names, 0) + wts((N.aqkv, N.qkv, N.bk, N.bv, N.bq), 1),
            hold=N.bu,
            micros=16,
        )
        chunk_lr = Chunk(*pack_lr[:1], [pack_lr[1]], plain_ids)
        if fast:
            *here, v[N.kv1] = after_all(here + [v[N.kv1]], [])
            chunk_lr.pieces = here + [swap(s, piece, CORE) for piece in here]
        of_loop[1] |= {m: chunk_lr for m in lr_names}
        share_kv(1)
        loop1 = [
            stage_attend(s, 1),
            stage_out(s, 1, N.stream1),
            stage_ffn(s, 1),
            stage_ffn_back(s, 1, N.cot),
            stage_out_back(s, 1),
        ]
        loop1_outs = (
            [N.stream2, N.mgrad1]
            + fill([N.ho, N.omid, N.ffn_in, N.gmid, N.hidden, N.dmid], 1)
            + fill([N.ffn_low, N.dmg, N.gug, N.gmg, N.blow, N.omg], 1)
            + [N.dnorm(1, 1), N.dnorm(1, 2), N.dnorm(1, 3)]
        )
        loop1_scratch = [N.o_acc, N.l_acc, N.branch1, N.middle1, N.gu1, N.ffn_out1]
        back_outs = [N.dq, N.dkvkeep] + ([N.dkvsend] if fast else [])
        kept = [N.att1, N.lse1, N.hgrad1]
        call(
            N.loop1,
            loop1 + ([stage_attend_back(s, 1)] if fast else []),
            [N.stream1, N.q1, N.norm, N.cot] + att_ins + kv_names(1),
            loop1_outs + (fill(back_outs, 1) if fast else kept),
            scratch=loop1_scratch + ([N.dkv_acc] + kept if fast else []),
            weights=wts(o_names + g_names + d_names, 1),
            smem=[N.first_block],
            micros=35,
        )
        if not fast:
            call(
                N.attend_back1,
                [stage_attend_back(s, 1)],
                [N.q1] + kept + att_ins + kv_names(1),
                fill(back_outs, 1),
                scratch=[N.o_acc, N.dkv_acc],
                smem=[N.first_block],
                micros=10,
            )

        plans = {
            N.la: [((N.bg, N.bu, N.agu, N.dna, N.dnb, N.outa, N.outb), 1)],
            N.g1: [((N.gug,), 0), ((N.aqkv,), 1)],
            N.g2: [((N.guu,), 0), ((N.bq, N.bk, N.bv), 1)],
            N.g3: [((N.dnw, N.agu), 0)],
            N.g4: [((N.bg, N.bu, N.dna, N.dnb), 0)],
            N.rb: [((N.outw, N.outa, N.outb, N.bq, N.qkvq, N.aqkvq), 0)],
            N.ra: [((N.qkvkv, N.aqkvkv, N.bk, N.bv), 0)],
        }
        modes = {N.la: N.direct, N.g1: N.x, N.g2: N.y, N.g3: N.x, N.g4: N.y, N.rb: N.direct, N.ra: N.direct}
        layouts = {}
        where = {}
        for m, parts in plans.items():
            layouts[m] = Layout(s, [name for names, _ in parts for name in names], gains=(m == N.ra and fast))
            shapes[N.keep(m)] = ((half if fast else 1, layouts[m].total, LANES), BF)
            shapes[N.send(m)] = shapes[N.keep(m)]
            where |= {(name, l): m for names, l in parts for name in names}

        def grads(names, ins, micros, extra=(), extra_outs=()):
            parts = []
            for m in names:
                parts += [(m, layouts[m], group, [0, 1], l) for group, l in plans[m]]
            outs = [end(m) for m in names for end in ((N.keep, N.send) if fast else (N.keep,))]
            call(
                N.grads(names[0]),
                [stage_grads(s, parts)] + list(extra),
                ins,
                outs + list(extra_outs),
                smem=[N.place] if fast else [],
                micros=micros,
            )

        sums = {}

        def open_sum(*names):
            for m in names:
                if fast:
                    sums[m] = Sum(s, v[N.keep(m)], v[N.send(m)], modes[m], odd)

        def open_kv(l):
            if fast:
                sums[N.dkv(l)] = Sum(s, v[N.dkvkeep(l)], v[N.dkvsend(l)], N.direct)
            else:
                keep = v[N.dkvkeep(l)].reshape(n * T, 2 * HD)
                v[N.dkv] = lax.psum_scatter(keep, "own", scatter_dimension=0, tiled=True)

        def close_kv(l):
            if fast:
                v[N.dkv] = sums[N.dkv(l)].payload[0]

        def phase(starts, inputs=(), need=()):
            if not fast:
                return
            starts, inputs = [sums[m] for m in starts], list(inputs)
            others = []
            for m in need:
                others += sums[m].payload if m in sums else [v[m]]
            values = after_all([p for r in starts for p in r.payload] + [v[m] for m in inputs], others)
            for r in starts:
                count = len(r.payload)
                r.payload, values = values[:count], values[count:]
            for m, value in zip(inputs, values):
                v[m] = value
            for r in starts:
                r.step()

        gain_ins = [N.dnorm(l, i) for l in (0, 1) for i in range(4)] + [N.dqg0, N.dqg1, N.dkg0, N.dkg1]
        qkv_l = [N.attn_in, N.mid, N.rawq_low, N.rawkv_low, N.midgq, N.midgkv]

        open_kv(1)
        phase([N.dkv1], [N.gmg1])
        grads(
            [N.la],
            [N.ffn_in1, N.gmid1, N.gug1, N.gmg1, N.hidden1, N.dmid1, N.ffn_low1, N.dmg1, N.ho1, N.omid1, N.blow1, N.omg1],
            8.6,
        )
        open_sum(N.la)
        phase([N.dkv1, N.la], [N.dq1])
        call(
            N.q_back1,
            [stage_q_back(s, 1)],
            [N.cos, N.sin, N.qkg, N.dq1, N.raw1],
            [N.rawq_low1, N.midgq1, N.agrad1, N.dqg1],
            weights=wts((N.qkv, N.bq, N.aqkv), 1),
            micros=5.8,
        )
        phase([N.la], [N.agrad1], [N.dkv1])
        close_kv(1)
        call(
            N.kv_back1,
            [stage_kv_back(s, 1, N.stream1, N.sgrad1)],
            [N.cos, N.sin, N.qkg, N.norm, N.dkv, N.raw1, N.agrad1, N.stream1, N.mgrad1],
            [N.dkg1, N.rawkv_low1, N.midgkv1, N.dnorm(1, 0), N.sgrad1],
            weights=wts((N.qkv, N.aqkv, N.bk, N.bv), 1),
            micros=6.2,
        )
        call(
            N.ffn_back0,
            [stage_ffn_back(s, 0, N.sgrad1)],
            [N.norm, N.sgrad1, N.ffn_out0, N.gu0, N.middle0],
            [N.dnorm(0, 3), N.dnorm(0, 2)] + fill([N.ffn_low, N.dmg, N.gug, N.gmg, N.mgrad], 0),
            weights=wts((N.dnb, N.dnw, N.dna, N.bg, N.bu, N.gu, N.agu), 0),
            hold=N.dnw,
            micros=14,
        )
        grads([N.g1, N.g2], fill([N.ffn_in, N.gug], 0) + [N.ffn_in1, N.gug1] + fill(qkv_l, 1), 9.7)
        open_sum(N.g1, N.g2)
        phase([N.g1, N.g2], [N.mgrad0], [N.la])
        call(
            N.out_back0,
            [stage_out_back(s, 0)],
            [N.branch0, N.norm, N.mgrad0],
            [N.dnorm(0, 1), N.blow0, N.omg0, N.hgrad0],
            weights=wts(o_names, 0),
            micros=4.5,
        )
        phase([N.g1, N.g2, N.la], [N.dmg0, N.hgrad0], [N.blow0])
        grads(
            [N.g3, N.g4],
            fill([N.ffn_in, N.gmid, N.gug, N.gmg, N.hidden, N.dmid, N.ffn_low, N.dmg], 0) + [N.hidden1, N.ffn_low1],
            8.5,
        )
        open_sum(N.g3, N.g4)
        if fast:
            v[N.hgrad0] = after(v[N.hgrad0], v[N.keep(N.g3)])
        call(
            N.attend_back0,
            [stage_attend_back(s, 0)],
            [N.hgrad0, N.q0, N.att0, N.lse0] + att_ins + kv_names(0),
            fill(back_outs, 0),
            scratch=[N.o_acc, N.dkv_acc],
            smem=[N.first_block],
            micros=13,
        )
        open_kv(0)
        phase([N.dkv0, N.g1, N.g2, N.la], [N.dq0])
        call(
            N.q_back0,
            [stage_q_back(s, 0)],
            [N.cos, N.sin, N.qkg, N.dq0, N.raw0],
            [N.rawq_low0, N.midgq0, N.agrad0, N.dqg0],
            weights=wts((N.qkv, N.bq, N.aqkv), 0),
            micros=5.8,
        )
        phase([N.dkv0, N.g3, N.g4], [N.rawq_low0], [N.g1, N.g2])
        grads(
            [N.rb],
            fill([N.ho, N.omid, N.blow, N.omg, N.mid, N.rawq_low, N.attn_in, N.midgq], 0)
            + [N.ho1, N.blow1, N.attn_in1, N.rawq_low1],
            7,
        )
        open_sum(N.rb)
        phase([N.g3, N.g4, N.rb, N.g1, N.g2], [N.agrad0, N.stream2], [N.dkv0])
        close_kv(0)
        mixed = unsort_rows(s, rank, v[N.stream2])
        v[N.mixed] = mixed
        call(
            N.kv_back0,
            [stage_kv_back(s, 0, N.stream0, N.sgrad0)],
            [N.cos, N.sin, N.qkg, N.norm, N.dkv, N.raw0, N.agrad0, N.stream0, N.mgrad0],
            [N.dkg0, N.rawkv_low0, N.midgkv0, N.dnorm(0, 0), N.sgrad0],
            weights=wts((N.qkv, N.aqkv, N.bk, N.bv), 0),
            micros=6.2,
        )
        grads(
            [N.ra],
            fill([N.attn_in, N.mid, N.rawkv_low, N.midgkv], 0) + [N.attn_in1, N.rawkv_low1] + gain_ins,
            3,
            [stage_gain_grads(s, N.ra, layouts[N.ra])],
            [] if fast else [N.gain_norm, N.gain_heads],
        )
        open_sum(N.ra)
        tokens_grad = unsort_rows(s, rank, v[N.sgrad0])
        v[N.tokens_grad] = tokens_grad
        phase([N.g3, N.g4, N.ra, N.la], [], [N.mixed, N.tokens_grad, N.g1, N.g2])
        phase([N.rb, N.g1, N.g2], [], [N.g3, N.g4, N.ra])
        phase([N.ra, N.g3, N.g4], [], [N.rb, N.g1, N.g2])
        phase([N.ra, N.rb, N.g3, N.g4, N.g1])
        phase([N.ra, N.rb, N.g3, N.g4, N.g2])
        phase([N.ra, N.rb])
        for m in sums:
            assert m in (N.dkv0, N.dkv1) or not sums[m].steps
        finished = {m: sums[m].payload for m in plans if fast}

        HB, RB = s.HB, s.RB
        two = (0, 1)
        targets = [
            (shared_attention_matrix.shape, [((), N.qkvq, 0, 0), ((), N.qkvkv, 0, H * HB)]),
            (shared_output_matrix.shape, [((), N.outw, 0, 0)]),
            (shared_gate_up_matrix.shape, [((), N.gug, 0, 0), ((), N.guu, 0, F // LANES)]),
            (shared_down_matrix.shape, [((), N.dnw, 0, 0)]),
            (
                adapter_attention_first.shape,
                [((0,), N.aqkvq, 0, 0), ((0,), N.aqkvkv, 0, RB), ((1,), N.aqkv, 1, 0)],
            ),
            (adapter_query_second.shape, [((l,), N.bq, l, 0) for l in two]),
            (
                adapter_key_value_second.shape,
                [((l, j), m, l, 0) for l in two for j, m in enumerate((N.bk, N.bv))],
            ),
            (adapter_output_first.shape, [((l,), N.outa, l, 0) for l in two]),
            (adapter_output_second.shape, [((l,), N.outb, l, 0) for l in two]),
            (adapter_gate_first.shape, [((l,), N.agu, l, 0) for l in two]),
            (adapter_gate_second.shape, [((l, j), m, l, 0) for l in two for j, m in enumerate((N.bg, N.bu))]),
            (adapter_down_first.shape, [((l,), N.dna, l, 0) for l in two]),
            (adapter_down_second.shape, [((l,), N.dnb, l, 0) for l in two]),
        ]
        if fast:
            plan = [(shape, [(lead, where[m, l], m, col) for lead, m, l, col in parts]) for shape, parts in targets]
            made = [None] * len(plan)
            early = [i for i, (_, parts) in enumerate(plan) if all(part[1][0] in N.lg for part in parts)]
            late = [i for i in range(len(plan)) if i not in early]
            ends = [
                (norm_gain_table.shape, [((0, 4), N.ra, N.norm, 0)]),
                (query_key_gains.shape, [((4, 2), N.ra, N.norm, 0)]),
            ]
            for which, last in ((early, []), (late, ends)):
                chosen = [plan[i] for i in which] + last
                used = sorted({part[1] for _, parts in chosen for part in parts})
                results = unpack(s, chosen, {m: (*finished[m], layouts[m]) for m in used})
                for i, value in zip(which, results):
                    made[i] = value
            grads, (norm_grad, heads_grad) = made, results[-2:]
        else:

            def natural(name, l):
                layout = layouts[where[name, l]]
                first, rows, count = layout.at[name]
                block = v[N.keep(where[name, l])][0, first : first + rows * count]
                return block.reshape(count, rows, LANES).transpose(1, 0, 2).reshape(rows, count * LANES)

            def reduced(value, axis):
                part = lax.psum_scatter(value.astype(BF), "own", scatter_dimension=axis, tiled=True)
                return lax.psum(part, "dp").astype(F32)

            grads = []
            for shape, parts in targets:
                of_lead = {}
                for lead, m, l, _ in parts:
                    of_lead.setdefault(lead, []).append(natural(m, l))
                value = jnp.stack([side_by_side(columns_of) for columns_of in of_lead.values()])
                value = value.reshape(shape[:-2] + value.shape[1:])
                grads.append(reduced(value, len(shape) - 2))
            norm_grad = reduced(v[N.gain_norm][:4], 1)
            heads_grad = reduced(v[N.gain_heads][4:6], 1)
        return (mixed, tokens_grad) + tuple(grads[:4]) + (norm_grad, heads_grad) + tuple(grads[4:])

    return shards


def solution(mesh):
    both, rows = P(("dp", "own"), None), P("own", None)
    second, third = P(None, "own", None), P(None, None, "own", None)
    wide_gain = P(None, "own")
    in_specs = (
        (both, both, P("dp", None), P("dp", None), rows, rows, rows, rows, wide_gain, wide_gain)
        + (second, second, third, second, second, second, third, second, second)
    )
    out_specs = (
        (both, both, rows, rows, rows, rows, wide_gain, wide_gain)
        + (second, second, third, second, second, second, third, second, second)
    )
    return jax.shard_map(make_shards(mesh), mesh=mesh, in_specs=in_specs, out_specs=out_specs, check_vma=False)
```

```python
import math

import jax
import jax.numpy as jnp
from jax import lax
from jax.experimental import pallas as pl
from jax.experimental.pallas import tpu as pltpu
from jax.sharding import PartitionSpec as P

BF = jnp.bfloat16
F32 = jnp.float32
EPS = 1e-06
THETA = 1000000.0
LANES = 128
LOG2E = 1.4426950408889634
VMEM_LIMIT = 60 * 2**20
PEAK = 1e6
CORE, XBIT, YBIT = 1, 2, 4


def dot(a, b):
    return jnp.dot(a, b, preferred_element_type=F32)


def dot_nt(a, b):
    return lax.dot_general(a, b, (((1,), (1,)), ((), ())), preferred_element_type=F32)


def dot_tn(a, b):
    return lax.dot_general(a, b, (((0,), (0,)), ((), ())), preferred_element_type=F32)


def side_by_side(parts):
    return parts[0] if len(parts) == 1 else jnp.concatenate(parts, axis=1)


def stacked(parts):
    return parts[0] if len(parts) == 1 else jnp.concatenate(parts, axis=0)


class Name(str):
    def __call__(self, *more):
        return Name(self + str().join(str(m) for m in more))


class Names:
    def __getattr__(self, name):
        return Name(name)


N = Names()


class Sizes:
    pass


class Layout:
    def __init__(self, sizes, names, gains=False):
        self.at = {}
        total = 0
        for name in names:
            rows, blocks = sizes.shard[name]
            self.at[name] = (total, rows, blocks)
            total += rows * blocks
        self.gains = None
        if gains:
            self.gains = total
            total += 16
        self.total = total


class Chunk:
    def __init__(self, layout, pieces, ids):
        self.layout, self.pieces, self.ids, self.mine = layout, pieces, ids, pieces[0]


class Env:
    def __init__(self):
        self.refs = {}
        self.pending = {}
        self.later = []

    def __getitem__(self, name):
        return self.refs[name]

    def w(self, name):
        if name in self.pending:
            sem = self.pending.pop(name)
            ref = self.refs[N.w(name)]
            pltpu.make_async_copy(ref, ref, sem).wait()
            if name == self.hold:
                for copy in self.later:
                    copy.start()
                self.later = []
        return self.refs[N.w(name)]


def run_kernel(sizes, name, stages, ins, outs, scratch=(), weights=(), smem=(), micros=0, hold=None, early=()):
    early = dict(early)
    chunks = []
    for _, chunk in weights:
        if chunk not in chunks:
            chunks.append(chunk)
    smem = dict(smem)
    for number, chunk in enumerate(chunks):
        smem[N.ids(number)] = chunk.ids
    scratch = dict(scratch)
    names_in = list(ins)
    names_smem = list(smem)
    pieces = [piece for chunk in chunks for piece in chunk.pieces]
    names_out = list(outs)
    names_scratch = list(scratch)
    shapes = []
    for wname, chunk in weights:
        if wname == N.gains:
            shapes.append(((sizes.slots, 16, LANES), BF))
        else:
            _, rows, blocks = chunk.layout.at[wname]
            shapes.append(((blocks, rows * sizes.slots, LANES), BF))

    def kernel(*refs):
        env = Env()
        env.hold, held = hold, False
        position = 0
        for key in names_smem + names_in:
            env.refs[key] = refs[position]
            position += 1
        piece_refs = refs[position : position + len(pieces)]
        position += len(pieces)
        for key in names_out + names_scratch:
            env.refs[key] = refs[position]
            position += 1
        whole = {}
        for key in early:
            whole[key] = env.refs[key]
            env.refs[key] = refs[len(refs) - 2 * len(early) + list(early).index(key)]
        of_chunk = {}
        start = 0
        for number, chunk in enumerate(chunks):
            of_chunk[number] = piece_refs[start : start + len(chunk.pieces)]
            start += len(chunk.pieces)
        for number, (wname, chunk) in enumerate(weights):
            buffer = refs[position]
            position += 1
            env.refs[N.w(wname)] = buffer
        for number, (wname, chunk) in enumerate(weights):
            sem = refs[position]
            position += 1
            buffer = env.refs[N.w(wname)]
            which = chunks.index(chunk)
            for slot in range(sizes.slots):
                piece = of_chunk[which][0 if len(chunk.pieces) == 1 else slot]
                offset = slot * chunk.layout.total if len(chunk.pieces) == 1 else 0
                if wname == N.gains:
                    source = piece.at[pl.ds(offset + chunk.layout.gains, 16), :]
                    target = buffer.at[slot]
                else:
                    first, rows, blocks = chunk.layout.at[wname]
                    first = offset + first
                    source = piece.at[pl.ds(first, blocks * rows), :].reshape(blocks, rows, LANES)
                    if sizes.slots == 1:
                        target = buffer
                    else:
                        row = pl.multiple_of(env[N.ids(which)][slot] * rows, 16)
                        target = buffer.at[:, pl.ds(row, rows), :]
                copy = pltpu.make_async_copy(source, target, sem)
                if held:
                    env.later.append(copy)
                else:
                    copy.start()
            env.pending[wname] = sem
            held = held or wname == hold
        env.ids = lambda chunk: env[N.ids(chunks.index(chunk))]
        going = []
        early_sems = dict(zip(early, refs[len(refs) - len(early) :]))
        for number, stage in enumerate(stages):
            stage(env)
            for key, last in early.items():
                if last == number:
                    going.append(pltpu.make_async_copy(env[key], whole[key], early_sems[key]))
                    going[-1].start()
        for wname, _ in weights:
            env.w(wname)
        for copy in going:
            copy.wait()

    any_space = pl.BlockSpec(memory_space=pl.ANY)
    vmem = pl.BlockSpec(memory_space=pltpu.VMEM)
    nbytes = sum(math.prod(a.shape) * a.dtype.itemsize for a in list(ins.values()) + pieces)
    nbytes += sum(math.prod(s) * jnp.dtype(d).itemsize for s, d in outs.values())
    results = pl.pallas_call(
        kernel,
        name=name,
        out_shape=[jax.ShapeDtypeStruct(*outs[key]) for key in names_out],
        in_specs=[pl.BlockSpec(memory_space=pltpu.SMEM)] * len(names_smem)
        + [vmem] * len(names_in)
        + [any_space] * len(pieces),
        out_specs=[any_space if key in early else vmem for key in names_out],
        scratch_shapes=[pltpu.VMEM(*scratch[key]) for key in names_scratch]
        + [pltpu.VMEM(*shape) for shape in shapes]
        + [pltpu.SemaphoreType.DMA] * len(weights)
        + [pltpu.VMEM(*outs[key]) for key in early]
        + [pltpu.SemaphoreType.DMA] * len(early),
        compiler_params=pltpu.CompilerParams(vmem_limit_bytes=VMEM_LIMIT),
        cost_estimate=pl.CostEstimate(flops=int(micros * PEAK), bytes_accessed=0, transcendentals=0),
    )(*smem.values(), *ins.values(), *pieces)
    return dict(zip(names_out, results))


def columns(weight, first, count, rows=None):
    if rows is None:
        return side_by_side([weight[first + i] for i in range(count)])
    return side_by_side([weight[first + i, rows] for i in range(count)])


def root(values):
    return lax.rsqrt(jnp.mean(values * values, axis=-1, keepdims=True) + EPS)


def rms_back(values, gain, grad):
    r = root(values)
    scaled = grad * gain
    back = r * scaled - values * (r * r * r * jnp.mean(values * scaled, axis=-1, keepdims=True))
    return back, jnp.sum(values * r * grad, axis=0, keepdims=True)


def rotate(values, cos, sin):
    half = values.shape[-1] // 2
    p, q = values[:, :half], values[:, half:]
    return jnp.concatenate([p * cos - q * sin, q * cos + p * sin], axis=1)


def rotate_back(grad, cos, sin):
    half = grad.shape[-1] // 2
    a, b = grad[:, :half], grad[:, half:]
    return jnp.concatenate([a * cos + b * sin, b * cos - a * sin], axis=1)


GELU_A = math.sqrt(2.0 / math.pi)
GELU_B = 0.044715


def gelu_parts(v):
    t = jnp.tanh(GELU_A * (v + GELU_B * v * v * v))
    return 0.5 * v * (1.0 + t), t


def gelu_slope(v, t):
    return 0.5 * (1.0 + t) + 0.5 * v * (1.0 - t * t) * (GELU_A * (1.0 + 3.0 * GELU_B * v * v))


def stage_gains(sizes, chunk):
    def stage(env):
        blocks = env.w(N.gains)
        ids = env.ids(chunk)
        norm = jnp.zeros((16, sizes.D), F32)
        heads = jnp.zeros((16, sizes.HD), F32)
        width, head_width = sizes.D // sizes.slots, sizes.HD // sizes.slots

        def pick(total, each, index):
            a = lax.broadcasted_iota(jnp.int32, (LANES, total), 0)
            b = lax.broadcasted_iota(jnp.int32, (LANES, total), 1)
            return jnp.where((b == a + index * each) & (a < each), 1.0, 0.0).astype(BF)

        for m in range(sizes.slots):
            norm = norm + dot(blocks[m], pick(sizes.D, width, ids[m]))
            heads = heads + dot(blocks[m], pick(sizes.HD, head_width, ids[m]))
        env[N.norm][...] = norm
        env[N.qkg][...] = heads

    return stage


def stage_qkv(sizes, l, stream):
    def stage(env):
        x = env[stream][...]
        attn_in = (x * root(x) * env[N.norm][0:1, :]).astype(BF)
        env[N.attn_in(l)][...] = attn_in
        first = env.w(N.aqkv)
        mids = []
        for j in range(3):
            mid = dot(attn_in, columns(first, sizes.RB * j, sizes.RB)).astype(BF)
            env[N.mid(l)][j] = mid
            mids.append(mid)
        qkv, hb = env.w(N.qkv), sizes.HB
        cos, sin = env[N.cos][...], env[N.sin][...]
        gq, gk = env[N.qkg][4:5, :], env[N.qkg][5:6, :]
        bk, bv, bq = env.w(N.bk), env.w(N.bv), env.w(N.bq)
        raw = dot(attn_in, columns(qkv, hb * sizes.H, hb)) + dot(mids[1], columns(bk, 0, hb))
        env[N.raw(l)][sizes.H] = raw
        env[N.kv(l)][:, : sizes.HD] = rotate(raw * root(raw) * gk, cos, sin).astype(BF)
        raw = dot(attn_in, columns(qkv, hb * (sizes.H + 1), hb)) + dot(mids[2], columns(bv, 0, hb))
        env[N.kv(l)][:, sizes.HD :] = raw.astype(BF)
        for h in range(sizes.H):
            raw = dot(attn_in, columns(qkv, hb * h, hb)) + dot(mids[0], columns(bq, hb * h, hb))
            env[N.raw(l)][h] = raw
            env[N.q(l)][h] = rotate(raw * root(raw) * gq, cos, sin).astype(BF)

    return stage


def key_block(sizes, pieces, b, value):
    lanes = slice(sizes.HD, 2 * sizes.HD) if value else slice(0, sizes.HD)
    rows = pl.ds(pl.multiple_of(b * sizes.IB, 16), sizes.IB)
    parts = []
    for piece in pieces:
        if len(piece.shape) == 3:
            parts += [piece[g, rows, lanes] for g in range(piece.shape[0])]
        else:
            parts.append(piece[rows, lanes])
    return stacked(parts)


def query_limits(sizes, env, qb):
    rows = slice(qb * sizes.QB, (qb + 1) * sizes.QB)
    slot = jnp.concatenate([env[N.qslot][rows, :]] * sizes.H, axis=0)
    low = jnp.concatenate([env[N.qstart][rows, :]] * sizes.H, axis=0)
    last = -(-(qb + 1) * sizes.QB // sizes.IB)
    return rows, slot, low, last


def stage_attend(sizes, l):
    scale = sizes.HD ** (-0.5) * LOG2E
    M = sizes.H * sizes.QB

    def stage(env):
        pieces = [env[N.kvp(l, i)] for i in range(sizes.kv_pieces)]
        for qb in range(sizes.T // sizes.QB):
            rows, slot, low, last = query_limits(sizes, env, qb)
            query = env[N.q(l)][:, rows, :].reshape(M, sizes.HD)
            env[N.o_acc][...] = jnp.zeros((M, sizes.HD), F32)
            env[N.l_acc][...] = jnp.zeros((M, LANES), F32)

            def body(b, carry):
                keys = env[N.kslot][b]
                scores = dot_nt(query, key_block(sizes, pieces, b, False))
                allowed = (keys <= slot) & (keys >= low)
                probs = jnp.where(allowed, jnp.exp2(scores * scale), 0.0)
                part = probs[:, :LANES]
                for i in range(1, probs.shape[1] // LANES):
                    part = part + probs[:, i * LANES : (i + 1) * LANES]
                env[N.l_acc][...] += part
                env[N.o_acc][...] += dot(probs.astype(BF), key_block(sizes, pieces, b, True))
                return carry

            lax.fori_loop(env[N.first_block][qb], last, body, 0)
            total = jnp.sum(env[N.l_acc][...], axis=1, keepdims=True)
            env[N.att(l)][:, rows, :] = (env[N.o_acc][...] / total).reshape(sizes.H, sizes.QB, sizes.HD)
            env[N.lse(l)][:, rows, :] = jnp.broadcast_to(jnp.log2(total), (M, LANES)).reshape(
                sizes.H, sizes.QB, LANES
            )

    return stage


def stage_out(sizes, l, stream):
    def stage(env):
        outa, outw, outb = env.w(N.outa), env.w(N.outw), env.w(N.outb)
        mid = jnp.zeros((sizes.T, sizes.R), F32)
        branch = jnp.zeros((sizes.T, sizes.D), F32)
        for h in range(sizes.H):
            heads = env[N.att(l)][h].astype(BF)
            env[N.ho(l)][h] = heads
            rows = slice(h * sizes.HD, (h + 1) * sizes.HD)
            mid = mid + dot(heads, columns(outa, 0, sizes.RB, rows))
            branch = branch + dot(heads, columns(outw, 0, sizes.DB, rows))
        mid = mid.astype(BF)
        env[N.omid(l)][...] = mid
        branch = branch + dot(mid, columns(outb, 0, sizes.DB))
        env[N.branch(l)][...] = branch
        middle = env[stream][...] + branch * root(branch) * env[N.norm][1:2, :]
        env[N.middle(l)][...] = middle
        env[N.ffn_in(l)][...] = (middle * root(middle) * env[N.norm][2:3, :]).astype(BF)

    return stage


def stage_ffn(sizes, l):
    def stage(env):
        x = env[N.ffn_in(l)][...]
        agu = env.w(N.agu)
        mids = []
        for j in range(2):
            mid = dot(x, columns(agu, sizes.RB * j, sizes.RB)).astype(BF)
            env[N.gmid(l)][j] = mid
            mids.append(mid)
        bg, bu, gu = env.w(N.bg), env.w(N.bu), env.w(N.gu)
        blocks = sizes.F // 256
        out = jnp.zeros((sizes.T, sizes.D), F32)
        down = jnp.zeros((sizes.T, sizes.R), F32)
        for b in range(blocks):
            gate = dot(x, columns(gu, 2 * b, 2)) + dot(mids[0], columns(bg, 2 * b, 2))
            up = dot(x, columns(gu, 2 * (blocks + b), 2)) + dot(mids[1], columns(bu, 2 * b, 2))
            env[N.gu(l)][b, :, :256] = gate.astype(env[N.gu(l)].dtype)
            env[N.gu(l)][b, :, 256:] = up.astype(env[N.gu(l)].dtype)
            hidden = (gelu_parts(gate)[0] * up).astype(BF)
            env[N.hidden(l)][b] = hidden
            rows = slice(b * 256, (b + 1) * 256)
            dnw, dna = env.w(N.dnw), env.w(N.dna)
            out = out + dot(hidden, columns(dnw, 0, sizes.DB, rows))
            down = down + dot(hidden, columns(dna, 0, sizes.RB, rows))
        down = down.astype(BF)
        env[N.dmid(l)][...] = down
        out = out + dot(down, columns(env.w(N.dnb), 0, sizes.DB))
        env[N.ffn_out(l)][...] = out
        env[N.stream(l + 1)][...] = env[N.middle(l)][...] + out * root(out) * env[N.norm][3:4, :]

    return stage


def stage_ffn_back(sizes, l, grad):
    def stage(env):
        out_grad = env[grad][...]
        back, gain = rms_back(env[N.ffn_out(l)][...], env[N.norm][3:4, :], out_grad)
        env[N.dnorm(l, 3)][...] = gain
        low = back.astype(BF)
        env[N.ffn_low(l)][...] = low
        dmg = dot_nt(low, columns(env.w(N.dnb), 0, sizes.DB)).astype(BF)
        env[N.dmg(l)][...] = dmg
        dnw, dna = env.w(N.dnw), env.w(N.dna)
        blocks = sizes.F // 256
        gate_mid = jnp.zeros((sizes.T, sizes.R), F32)
        up_mid = jnp.zeros((sizes.T, sizes.R), F32)
        total = jnp.zeros((sizes.T, sizes.D), F32)
        for b in range(blocks):
            rows = slice(b * 256, (b + 1) * 256)
            hidden_grad = dot_nt(low, columns(dnw, 0, sizes.DB, rows)) + dot_nt(
                dmg, columns(dna, 0, sizes.RB, rows)
            )
            gate, up = env[N.gu(l)][b, :, :256].astype(F32), env[N.gu(l)][b, :, 256:].astype(F32)
            value, t = gelu_parts(gate)
            gate_grad = (hidden_grad * up * gelu_slope(gate, t)).astype(BF)
            up_grad = (hidden_grad * value).astype(BF)
            env[N.gug(l)][b] = gate_grad
            env[N.gug(l)][blocks + b] = up_grad
            bg, bu, gu = env.w(N.bg), env.w(N.bu), env.w(N.gu)
            gate_mid = gate_mid + dot_nt(gate_grad, columns(bg, 2 * b, 2))
            up_mid = up_mid + dot_nt(up_grad, columns(bu, 2 * b, 2))
            total = total + dot_nt(gate_grad, columns(gu, 2 * b, 2))
            total = total + dot_nt(up_grad, columns(gu, 2 * (blocks + b), 2))
        agu = env.w(N.agu)
        for j, mid in enumerate((gate_mid, up_mid)):
            mid = mid.astype(BF)
            env[N.gmg(l)][j] = mid
            total = total + dot_nt(mid, columns(agu, sizes.RB * j, sizes.RB))
        back, gain = rms_back(env[N.middle(l)][...], env[N.norm][2:3, :], total)
        env[N.dnorm(l, 2)][...] = gain
        env[N.mgrad(l)][...] = out_grad + back

    return stage


def stage_out_back(sizes, l):
    def stage(env):
        back, gain = rms_back(env[N.branch(l)][...], env[N.norm][1:2, :], env[N.mgrad(l)][...])
        env[N.dnorm(l, 1)][...] = gain
        low = back.astype(BF)
        env[N.blow(l)][...] = low
        omg = dot_nt(low, columns(env.w(N.outb), 0, sizes.DB)).astype(BF)
        env[N.omg(l)][...] = omg
        outw, outa = env.w(N.outw), env.w(N.outa)
        for h in range(sizes.H):
            rows = slice(h * sizes.HD, (h + 1) * sizes.HD)
            grad = dot_nt(low, columns(outw, 0, sizes.DB, rows)) + dot_nt(omg, columns(outa, 0, sizes.RB, rows))
            env[N.hgrad(l)][h] = grad.astype(BF)

    return stage


def stage_attend_back(sizes, l):
    factor = sizes.HD ** (-0.5)
    scale = factor * LOG2E
    M = sizes.H * sizes.QB
    HD = sizes.HD

    def stage(env):
        pieces = [env[N.kvp(l, i)] for i in range(sizes.kv_pieces)]
        total_blocks = sizes.T // sizes.IB
        for b in range(total_blocks):
            env[N.dkv_acc][b] = jnp.zeros((sizes.n * sizes.IB, 2 * HD), F32)
        for qb in range(sizes.T // sizes.QB):
            rows, slot, low, last = query_limits(sizes, env, qb)
            query = env[N.q(l)][:, rows, :].reshape(M, HD)
            grad = env[N.hgrad(l)][:, rows, :].reshape(M, HD)
            attended = env[N.att(l)][:, rows, :].reshape(M, HD)
            row_dot = jnp.sum(grad.astype(F32) * attended, axis=1, keepdims=True)
            lse = env[N.lse(l)][:, rows, :].reshape(M, LANES)[:, 0:1]
            env[N.o_acc][...] = jnp.zeros((M, HD), F32)

            def body(b, carry):
                keys = env[N.kslot][b]
                k = key_block(sizes, pieces, b, False)
                v = key_block(sizes, pieces, b, True)
                allowed = (keys <= slot) & (keys >= low)
                probs = jnp.where(allowed, jnp.exp2(dot_nt(query, k) * scale - lse), 0.0)
                scores_grad = (probs * (dot_nt(grad, v) - row_dot)).astype(BF)
                env[N.o_acc][...] += dot(scores_grad, k)
                env[N.dkv_acc][b, :, :HD] += dot_tn(scores_grad, query)
                env[N.dkv_acc][b, :, HD:] += dot_tn(probs.astype(BF), grad)
                return carry

            lax.fori_loop(env[N.first_block][qb], last, body, 0)
            env[N.dq(l)][:, rows, :] = (env[N.o_acc][...] * factor).reshape(sizes.H, sizes.QB, HD)
        IB = sizes.IB
        for m in range(sizes.n):
            if sizes.slots > 1:
                where = (N.dkvkeep if m < sizes.n // 2 else N.dkvsend, m % (sizes.n // 2))
            else:
                where = (N.dkvkeep, m)
            for b in range(total_blocks):
                for j, by in enumerate((factor, 1.0)):
                    lanes = slice(j * HD, (j + 1) * HD)
                    part = env[N.dkv_acc][b, m * IB : (m + 1) * IB, lanes]
                    env[where[0](l)][where[1], b * IB : (b + 1) * IB, lanes] = (part * by).astype(BF)

    return stage


def stage_q_back(sizes, l):
    def stage(env):
        cos, sin = env[N.cos][...], env[N.sin][...]
        gq = env[N.qkg][4:5, :]
        hb = sizes.HB
        qkv, bq, aqkv = env.w(N.qkv), env.w(N.bq), env.w(N.aqkv)
        gains = jnp.zeros((1, sizes.HD), F32)
        mid = jnp.zeros((sizes.T, sizes.R), F32)
        total = jnp.zeros((sizes.T, sizes.D), F32)
        for h in range(sizes.H):
            turned = rotate_back(env[N.dq(l)][h], cos, sin)
            back, gain = rms_back(env[N.raw(l)][h], gq, turned)
            gains = gains + gain
            low = back.astype(BF)
            env[N.rawq_low(l)][h] = low
            mid = mid + dot_nt(low, columns(bq, hb * h, hb))
            total = total + dot_nt(low, columns(qkv, hb * h, hb))
        mid = mid.astype(BF)
        env[N.midgq(l)][...] = mid
        total = total + dot_nt(mid, columns(aqkv, 0, sizes.RB))
        env[N.agrad(l)][...] = total
        env[N.dqg(l)][...] = gains

    return stage


def stage_kv_back(sizes, l, stream, result):
    def stage(env):
        cos, sin = env[N.cos][...], env[N.sin][...]
        hb = sizes.HB
        qkv, aqkv = env.w(N.qkv), env.w(N.aqkv)
        turned = rotate_back(env[N.dkv][:, : sizes.HD].astype(F32), cos, sin)
        back, gain = rms_back(env[N.raw(l)][sizes.H], env[N.qkg][5:6, :], turned)
        env[N.dkg(l)][...] = gain
        total = env[N.agrad(l)][...]
        for j, (low, second) in enumerate(((back.astype(BF), N.bk), (env[N.dkv][:, sizes.HD :], N.bv))):
            env[N.rawkv_low(l)][j] = low
            mid = dot_nt(low, columns(env.w(second), 0, hb)).astype(BF)
            env[N.midgkv(l)][j] = mid
            total = total + dot_nt(low, columns(qkv, hb * (sizes.H + j), hb))
            total = total + dot_nt(mid, columns(aqkv, sizes.RB * (j + 1), sizes.RB))
        back, gain = rms_back(env[stream][...], env[N.norm][0:1, :], total)
        env[N.dnorm(l, 0)][...] = gain
        env[result][...] = env[N.mgrad(l)][...] + back

    return stage


def put(sizes, env, layout, prefix, name, block, value, first_row=0):
    first, rows, _ = layout.at[name]
    count = value.shape[1] // LANES
    keep = env[N.keep(prefix)]
    if sizes.slots == 1:
        value = value.astype(BF)
        for i in range(count):
            at = first + (block + i) * rows + first_row
            keep[0, at : at + value.shape[0], :] = value[:, i * LANES : (i + 1) * LANES]
        return
    send = env[N.send(prefix)]
    core, chip = env[N.place][0], env[N.place][1]
    even_stays = core == 0
    for pair in range(value.shape[0] // (2 * rows)):
        a = value[2 * pair * rows : (2 * pair + 1) * rows]
        b = value[(2 * pair + 1) * rows : (2 * pair + 2) * rows]
        stays = jnp.where(even_stays, a, b).astype(BF)
        goes = jnp.where(even_stays, b, a).astype(BF)
        slot = jnp.bitwise_xor(first_row // (2 * rows) + pair, chip)
        for i in range(count):
            at = first + (block + i) * rows
            keep[slot, at : at + rows, :] = stays[:, i * LANES : (i + 1) * LANES]
            send[slot, at : at + rows, :] = goes[:, i * LANES : (i + 1) * LANES]


def grad_product(sizes, env, layout, prefix, name, lefts, rights, first_block=0, first_row=0):
    left = stacked([a.T if len(lefts) == 1 else a.T for a in lefts]) if len(lefts) == 1 else side_by_side(
        [a.T for a in lefts]
    )
    for block, right in rights:
        value = dot(left, stacked(right))
        put(sizes, env, layout, prefix, name, first_block + block, value, first_row)


def wide(ref, width, step=256):
    out = []
    at = 0
    while at < width:
        size = min(step, width - at)
        out.append((at // LANES, slice(at, at + size)))
        at += size
    return out


def grads_ffn_wide(sizes, env, layout, prefix, names, loops, pl_l):
    blocks = sizes.F // 256
    for j, name in enumerate((N.gug, N.guu)):
        if name in names:
            left = [env[N.ffn_in(l)][...] for l in loops]
            rights = [(2 * b, [env[N.gug(l)][j * blocks + b] for l in loops]) for b in range(blocks)]
            grad_product(sizes, env, layout, prefix, name, left, rights)
    if N.agu in names:
        rights = [(sizes.RB * j, [env[N.gmg(pl_l)][j]]) for j in range(2)]
        grad_product(sizes, env, layout, prefix, N.agu, [env[N.ffn_in(pl_l)][...]], rights)
    for j, name in enumerate((N.bg, N.bu)):
        if name in names:
            rights = [(2 * b, [env[N.gug(pl_l)][j * blocks + b]]) for b in range(blocks)]
            grad_product(sizes, env, layout, prefix, name, [env[N.gmid(pl_l)][j]], rights)


def grads_ffn_down(sizes, env, layout, prefix, names, loops, pl_l):
    blocks = sizes.F // 256
    step = 512
    for b in range(0, blocks, 2):
        row = b * 256
        if N.dnw in names:
            left = [side_by_side([env[N.hidden(l)][b], env[N.hidden(l)][b + 1]]) for l in loops]
            rights = [(i, [env[N.ffn_low(l)][:, s] for l in loops]) for i, s in wide(None, sizes.D, 640)]
            grad_product(sizes, env, layout, prefix, N.dnw, left, rights, 0, row)
        if N.dna in names:
            left = [side_by_side([env[N.hidden(pl_l)][b], env[N.hidden(pl_l)][b + 1]])]
            grad_product(sizes, env, layout, prefix, N.dna, left, [(0, [env[N.dmg(pl_l)][...]])], 0, row)
    if N.dnb in names:
        grad_product(
            sizes, env, layout, prefix, N.dnb, [env[N.dmid(pl_l)][...]], [(0, [env[N.ffn_low(pl_l)][...]])]
        )


def grads_out(sizes, env, layout, prefix, names, loops, pl_l):
    for h in range(0, sizes.H, 2):
        row = h * sizes.HD
        if N.outw in names:
            left = [side_by_side([env[N.ho(l)][h], env[N.ho(l)][h + 1]]) for l in loops]
            grad_product(
                sizes, env, layout, prefix, N.outw, left, [(0, [env[N.blow(l)][...] for l in loops])], 0, row
            )
        if N.outa in names:
            left = [side_by_side([env[N.ho(pl_l)][h], env[N.ho(pl_l)][h + 1]])]
            grad_product(sizes, env, layout, prefix, N.outa, left, [(0, [env[N.omg(pl_l)][...]])], 0, row)
    if N.outb in names:
        grad_product(
            sizes, env, layout, prefix, N.outb, [env[N.omid(pl_l)][...]], [(0, [env[N.blow(pl_l)][...]])]
        )


def grads_qkv(sizes, env, layout, prefix, names, loops, pl_l):
    hb = sizes.HB
    left = [env[N.attn_in(l)][...] for l in loops] if {N.qkvq, N.qkvkv} & set(names) else None
    if N.qkvq in names:
        rights = [(hb * h, [env[N.rawq_low(l)][h] for l in loops]) for h in range(sizes.H)]
        grad_product(sizes, env, layout, prefix, N.qkvq, left, rights)
    if N.qkvkv in names:
        rights = [(hb * j, [env[N.rawkv_low(l)][j] for l in loops]) for j in range(2)]
        grad_product(sizes, env, layout, prefix, N.qkvkv, left, rights)
    first = ([(0, N.midgq(pl_l), None)] if {N.aqkv, N.aqkvq} & set(names) else []) + (
        [(sizes.RB * j, N.midgkv(pl_l), j) for j in range(2)] if {N.aqkv, N.aqkvkv} & set(names) else []
    )
    for name in (N.aqkv, N.aqkvq, N.aqkvkv):
        if name in names:
            rights = [
                (at + (sizes.RB if name == N.aqkv and j is not None else 0), [env[ref][...] if j is None else env[ref][j]])
                for at, ref, j in first
            ]
            grad_product(sizes, env, layout, prefix, name, [env[N.attn_in(pl_l)][...]], rights)
    if N.bq in names:
        rights = [(hb * h, [env[N.rawq_low(pl_l)][h]]) for h in range(sizes.H)]
        grad_product(sizes, env, layout, prefix, N.bq, [env[N.mid(pl_l)][0]], rights)
    for j, name in enumerate((N.bk, N.bv)):
        if name in names:
            grad_product(
                sizes, env, layout, prefix, name, [env[N.mid(pl_l)][j + 1]], [(0, [env[N.rawkv_low(pl_l)][j]])]
            )


def stage_grads(sizes, parts):
    def stage(env):
        for prefix, layout, names, loops, pl_l in parts:
            for build in (grads_ffn_wide, grads_ffn_down, grads_out, grads_qkv):
                build(sizes, env, layout, prefix, names, loops, pl_l)

    return stage


def stage_gain_grads(sizes, prefix, layout):
    def stage(env):
        norm = stacked(
            [env[N.dnorm(0, i)][...] + env[N.dnorm(1, i)][...] for i in range(4)] + [jnp.zeros((12, sizes.D), F32)]
        )
        heads = stacked(
            [jnp.zeros((4, sizes.HD), F32)]
            + [env[kind(0)][...] + env[kind(1)][...] for kind in (N.dqg, N.dkg)]
            + [jnp.zeros((10, sizes.HD), F32)]
        )
        if sizes.slots == 1:
            env[N.gain_norm][...] = norm
            env[N.gain_heads][...] = heads
            return
        norm, heads = norm.astype(BF), heads.astype(BF)
        width, head_width = sizes.D // sizes.slots, sizes.HD // sizes.slots

        def pick(total, each, index):
            a = lax.broadcasted_iota(jnp.int32, (total, LANES), 0)
            b = lax.broadcasted_iota(jnp.int32, (total, LANES), 1)
            return jnp.where((a == b + index * each) & (b < each), 1.0, 0.0).astype(BF)

        at = layout.gains
        chip, core = env[N.place][1], env[N.place][0]
        for k in range(sizes.slots // 2):
            for name, flip in ((N.keep, core), (N.send, 1 - core)):
                index = 2 * jnp.bitwise_xor(k, chip) + flip
                block = dot(norm, pick(sizes.D, width, index)) + dot(heads, pick(sizes.HD, head_width, index))
                env[name(prefix)][k, at : at + 16, :] = block.astype(BF)

    return stage


def pack(sizes, layout, arrays, gains=None):
    names = list(layout.at)
    unique = []
    for name in names:
        if not any(arrays[name][0] is u for u in unique):
            unique.append(arrays[name][0])
    extra = [] if layout.gains is None else [gains]

    def kernel(*refs):
        out = refs[-1]
        for name in names:
            array, lead = arrays[name]
            source = refs[[array is u for u in unique].index(True)]
            first, rows, blocks = layout.at[name]
            for b in range(blocks):
                out[first + b * rows : first + (b + 1) * rows, :] = source[
                    lead + (slice(None), slice(b * LANES, (b + 1) * LANES))
                ]
        if layout.gains is not None:
            out[layout.gains : layout.gains + 16, :] = refs[len(unique)][...]

    return pl.pallas_call(
        kernel,
        name=N.pack,
        out_shape=jax.ShapeDtypeStruct((layout.total, LANES), BF),
        compiler_params=pltpu.CompilerParams(vmem_limit_bytes=VMEM_LIMIT),
        cost_estimate=pl.CostEstimate(flops=0, bytes_accessed=4 * layout.total * LANES, transcendentals=0),
    )(*unique, *extra)


def sort_rows(sizes, rank, *arrays):
    def kernel(rank_ref, *refs):
        count = len(refs) // 2
        place = lax.broadcasted_iota(jnp.int32, (sizes.T, sizes.T), 0)
        matrix = jnp.where(place == rank_ref[...], 1.0, 0.0).astype(BF)
        for source, target in zip(refs[:count], refs[count:]):
            target[...] = dot(matrix, source[...])

    return pl.pallas_call(
        kernel,
        name=N.sort_rows,
        out_shape=[jax.ShapeDtypeStruct(a.shape, F32) for a in arrays],
        compiler_params=pltpu.CompilerParams(vmem_limit_bytes=VMEM_LIMIT),
        cost_estimate=pl.CostEstimate(flops=0, bytes_accessed=2**21, transcendentals=0),
    )(rank, *arrays)


def unsort_rows(sizes, rank, value):
    def kernel(rank_ref, source, target):
        place = lax.broadcasted_iota(jnp.int32, (sizes.T, sizes.T), 0)
        matrix = jnp.where(place == rank_ref[...], 1.0, 0.0).astype(BF)
        target[...] = dot_tn(matrix, source[...].astype(BF)).astype(BF)

    return pl.pallas_call(
        kernel,
        name=N.unsort_rows,
        out_shape=jax.ShapeDtypeStruct(value.shape, BF),
        compiler_params=pltpu.CompilerParams(vmem_limit_bytes=VMEM_LIMIT),
        cost_estimate=pl.CostEstimate(flops=0, bytes_accessed=2**20, transcendentals=0),
    )(rank, value)


def unpack(sizes, targets, sources):
    names = list(sources)
    shapes = [jax.ShapeDtypeStruct(shape, F32) for shape, _ in targets]

    def kernel(*refs):
        ins = {name: refs[2 * i : 2 * i + 2] for i, name in enumerate(names)}
        outs = refs[2 * len(names) :]

        def rows_of(prefix, first, count):
            low, high = ins[prefix]
            half = low.shape[0]
            if first + count <= half:
                return low[first : first + count, :].astype(F32)
            if first >= half:
                return high[first - half : first + count - half, :].astype(F32)
            return jnp.concatenate(
                [low[first:half, :].astype(F32), high[: first + count - half, :].astype(F32)], axis=0
            )

        for out, (_, parts) in zip(outs, targets):
            for lead, prefix, name, column in parts:
                layout = sources[prefix][2]
                if name == N.norm:
                    first, count = lead
                    out[...] = rows_of(prefix, layout.gains, 16)[first : first + count, : out.shape[1]]
                    continue
                first, rows, blocks = layout.at[name]
                for b in range(blocks):
                    out[lead + (slice(None), slice((column + b) * LANES, (column + b + 1) * LANES))] = rows_of(
                        prefix, first + b * rows, rows
                    )

    return pl.pallas_call(
        kernel,
        name=N.unpack,
        out_shape=shapes,
        compiler_params=pltpu.CompilerParams(vmem_limit_bytes=VMEM_LIMIT),
        cost_estimate=pl.CostEstimate(flops=0, bytes_accessed=2**22, transcendentals=0),
    )(*[half for name in names for half in sources[name][:2]])


def swap(sizes, value, bit):
    return lax.ppermute(value, "own", [(i, i ^ bit) for i in range(sizes.n)])


def along(value, pairs):
    return lax.ppermute(value, "dp", pairs)


def after_all(values, others):
    others = [o for o in others if not any(o is value for value in values)]
    count = len(values)

    def kernel(*refs):
        pass

    space = pl.BlockSpec(memory_space=pl.ANY)
    return pl.pallas_call(
        kernel,
        name=N.after,
        out_shape=[jax.ShapeDtypeStruct(value.shape, value.dtype) for value in values],
        in_specs=[space] * (count + len(others)),
        out_specs=[space] * count,
        input_output_aliases={i: i for i in range(count)},
        cost_estimate=pl.CostEstimate(flops=0, bytes_accessed=0, transcendentals=0),
    )(*values, *others)


def after(value, *others):
    return after_all([value], others)[0]


def gather_plain(sizes, mine, x_first, others=()):
    px, py = swap(sizes, mine, XBIT), swap(sizes, mine, YBIT)
    px = after(px, *others) if others else px
    pd = swap(sizes, px, YBIT) if x_first else swap(sizes, py, XBIT)
    here = [mine, px, py, pd]
    return here + [swap(sizes, piece, CORE) for piece in here]


def gather_direct(sizes, mine):
    here = [mine] + [swap(sizes, mine, bit) for bit in (XBIT, YBIT, XBIT | YBIT)]
    return here + [swap(sizes, piece, CORE) for piece in here]


PIECES = (0, XBIT, YBIT, XBIT | YBIT, CORE, CORE | XBIT, CORE | YBIT, CORE | XBIT | YBIT)


def gather_paired(sizes, mine, odd, others=()):
    px = swap(sizes, mine, XBIT)
    chosen = jnp.where(odd, px, mine)
    py = swap(sizes, after(chosen, *others) if others else chosen, YBIT)
    pz = along(py, [(0, 1), (1, 0), (2, 3), (3, 2)])
    here = [mine, px, py, pz]
    return here + [swap(sizes, piece, CORE) for piece in here]


def add(first, *others):
    total = first.astype(F32)
    for other in others:
        total = total + other.astype(F32)
    return total.astype(BF)


class Sum:
    def __init__(self, sizes, keep, send, mode, odd=None):
        self.sizes, self.keep, self.mode, self.odd = sizes, keep, mode, odd
        self.payload, self.done = [send], []
        self.steps = [self.core] + ([self.direct] if mode == N.direct else [self.near, self.far])
        self.steps += [self.trade, self.level, self.back]

    def step(self):
        now = self.steps.pop(0)
        now(self.payload)

    def swap(self, value, bit):
        return swap(self.sizes, value, bit)

    def core(self, sent):
        here, come = self.keep, self.swap(sent[0], CORE)
        if self.mode == N.direct:
            self.keep, *self.payload = [add(here[k], come[k]) for k in range(4)]
            return
        if self.mode == N.x:
            here, come = [a.reshape((2, 2) + a.shape[1:]) for a in (here, come)]
            pairs = [(here[:, i], come[:, i]) for i in range(2)]
        else:
            pairs = [(here[i : i + 2], come[i : i + 2]) for i in (0, 2)]
        self.keep, self.payload = add(*pairs[0]), [add(*pairs[1])]

    def direct(self, sent):
        come = [self.swap(value, bit) for value, bit in zip(sent, (XBIT, YBIT, XBIT | YBIT))]
        self.level_in(add(self.keep, *come))

    def near(self, sent):
        come = self.swap(sent[0], XBIT if self.mode == N.x else YBIT)
        self.keep, self.payload = add(self.keep[0], come[0]), [add(self.keep[1], come[1])]

    def far(self, sent):
        self.level_in(add(self.keep, self.swap(sent[0], YBIT if self.mode == N.x else XBIT)))

    def level_in(self, total):
        self.plane_total = total
        if self.odd is None:
            self.payload = [total]
            return
        rows = total.shape[0] // 2
        low, high = total[:rows], total[rows:]
        self.keep, self.payload = jnp.where(self.odd, high, low), [jnp.where(self.odd, low, high)]

    def trade(self, sent):
        self.payload = [add(self.keep, along(sent[0], [(0, 1), (1, 0), (2, 3), (3, 2)]))]

    def level(self, sent):
        self.payload = [add(sent[0], along(sent[0], [(0, 2), (2, 0), (1, 3), (3, 1)]))]

    def back(self, sent):
        come = along(sent[0], [(0, 1), (1, 0), (2, 3), (3, 2)])
        self.halves = (jnp.where(self.odd, come, sent[0]), jnp.where(self.odd, sent[0], come))
        self.payload = list(self.halves)


def make_shards(mesh):
    n, planes = mesh.shape["own"], mesh.shape["dp"]
    fast = n == 8 and planes == 4

    def shards(
        tokens,
        cotangent,
        lengths,
        row_packed_slot,
        shared_attention_matrix,
        shared_output_matrix,
        shared_gate_up_matrix,
        shared_down_matrix,
        norm_gain_table,
        query_key_gains,
        adapter_attention_first,
        adapter_query_second,
        adapter_key_value_second,
        adapter_output_first,
        adapter_output_second,
        adapter_gate_first,
        adapter_gate_second,
        adapter_down_first,
        adapter_down_second,
    ):
        s = Sizes()
        s.n, s.slots = n, (8 if fast else 1)
        s.T, s.D = tokens.shape
        s.HD = adapter_key_value_second.shape[3]
        s.H = adapter_query_second.shape[2] // s.HD
        s.R = adapter_query_second.shape[1] * n
        s.F = shared_down_matrix.shape[0] * n
        s.DB, s.RB, s.HB = s.D // LANES, s.R // LANES, s.HD // LANES
        s.IB = max(16, 1024 // n)
        s.QB = s.T // 4
        s.kv_pieces = 8 if fast else 1
        QW, k = s.H * s.HD, s.slots
        s.shard = {
            N.qkv: (s.D // k, (QW + 2 * s.HD) // LANES),
            N.aqkv: (s.D // k, 3 * s.RB),
            N.gug: (s.D // k, s.F // LANES),
            N.guu: (s.D // k, s.F // LANES),
            N.qkvq: (s.D // k, QW // LANES),
            N.qkvkv: (s.D // k, 2 * s.HB),
            N.aqkvq: (s.D // k, s.RB),
            N.aqkvkv: (s.D // k, 2 * s.RB),
            N.bq: (s.R // k, QW // LANES),
            N.bk: (s.R // k, s.HB),
            N.bv: (s.R // k, s.HB),
            N.outw: (QW // k, s.DB),
            N.outa: (QW // k, s.RB),
            N.outb: (s.R // k, s.DB),
            N.gu: (s.D // k, 2 * s.F // LANES),
            N.agu: (s.D // k, 2 * s.RB),
            N.bg: (s.R // k, s.F // LANES),
            N.bu: (s.R // k, s.F // LANES),
            N.dnw: (s.F // k, s.DB),
            N.dna: (s.F // k, s.RB),
            N.dnb: (s.R // k, s.DB),
        }
        own, plane = lax.axis_index("own"), lax.axis_index("dp")

        plain_ids = jnp.stack([own ^ m for m in PIECES]).astype(jnp.int32) if fast else jnp.zeros((1,), jnp.int32)
        slots = row_packed_slot[0]
        seq = lengths[0]
        my_slots = lax.dynamic_slice_in_dim(slots, own * s.T, s.T)
        rank = (my_slots // n).reshape(1, s.T)
        rest = slots.reshape(n, s.T)[:, 0] % n
        my_rest = my_slots[0] % n
        counts = jnp.arange(seq.shape[0])
        ends = jnp.sum(jnp.where(counts[None, :] <= counts[:, None], seq[None, :], 0), axis=1)
        sorted_slots = n * jnp.arange(s.T, dtype=jnp.int32) + my_rest
        past = sorted_slots[:, None] >= ends[None, :]
        starts = jnp.sum(jnp.where(past, seq[None, :], 0), axis=1)
        position = sorted_slots - starts
        inverse = THETA ** (-jnp.arange(s.HD // 2, dtype=F32) * 2.0 / s.HD)
        angles = position.astype(F32)[:, None] * inverse[None, :]
        block_slots = s.IB * n
        first_block = starts.reshape(4, s.QB)[:, 0] // block_slots
        key_rest = rest
        if fast:
            key_rest = jnp.sum(
                jnp.where(plain_ids[:, None] == jnp.arange(n)[None, :], rest[None, :], 0), axis=1
            )
        along_rows = jnp.arange(s.T, dtype=jnp.int32).reshape(s.T // s.IB, 1, 1, s.IB) * n
        kslot = (along_rows + key_rest.reshape(1, 1, n, 1)).reshape(s.T // s.IB, 1, n * s.IB).astype(jnp.int32)
        stream0, cot = sort_rows(s, rank, tokens, cotangent)

        v = {
            N.cos: jnp.cos(angles),
            N.sin: jnp.sin(angles),
            N.qslot: sorted_slots.reshape(s.T, 1),
            N.qstart: starts.reshape(s.T, 1).astype(jnp.int32),
            N.kslot: kslot,
            N.stream0: stream0,
            N.cot: cot,
        }
        def full(array, axis):
            return array if fast else lax.all_gather(array, "own", axis=axis, tiled=True)

        w_att, w_out = full(shared_attention_matrix, 0), full(shared_output_matrix, 0)
        w_gu, w_dn = full(shared_gate_up_matrix, 0), full(shared_down_matrix, 0)
        a_att, b_q = full(adapter_attention_first, 1), full(adapter_query_second, 1)
        b_kv, a_out = full(adapter_key_value_second, 2), full(adapter_output_first, 1)
        b_out, a_gu = full(adapter_output_second, 1), full(adapter_gate_first, 1)
        b_gu, a_dn = full(adapter_gate_second, 2), full(adapter_down_first, 1)
        b_dn = full(adapter_down_second, 1)

        def arrays_of(l):
            return {
                N.qkv: (w_att, ()),
                N.aqkv: (a_att, (l,)),
                N.bq: (b_q, (l,)),
                N.bk: (b_kv, (l, 0)),
                N.bv: (b_kv, (l, 1)),
                N.outw: (w_out, ()),
                N.outa: (a_out, (l,)),
                N.outb: (b_out, (l,)),
                N.gu: (w_gu, ()),
                N.agu: (a_gu, (l,)),
                N.bg: (b_gu, (l, 0)),
                N.bu: (b_gu, (l, 1)),
                N.dnw: (w_dn, ()),
                N.dna: (a_dn, (l,)),
                N.dnb: (b_dn, (l,)),
            }

        q_names, o_names = (N.qkv, N.aqkv, N.bq, N.bk, N.bv), (N.outw, N.outa, N.outb)
        g_names, d_names = (N.gu, N.agu, N.bg, N.bu), (N.dnw, N.dna, N.dnb)
        lq_names, lr_names = (N.aqkv, N.bq, N.bk, N.bv), (N.outa, N.outb, N.agu, N.bg, N.bu, N.dna, N.dnb)
        odd = (plane & 1) == 1
        inner = (plane == 1) | (plane == 2)
        paired_ids = plain_ids
        if fast:
            over_y = jnp.where(odd, XBIT | YBIT, YBIT)
            over_z = jnp.where(odd, YBIT, XBIT | YBIT)
            order = [0, XBIT, over_y, over_z]
            paired_ids = jnp.stack([own ^ m for m in order] + [own ^ m ^ CORE for m in order]).astype(jnp.int32)
        gain_block = None
        if fast:
            gain_block = jnp.concatenate(
                [
                    jnp.pad(norm_gain_table, ((0, 0), (0, LANES - norm_gain_table.shape[1]))),
                    jnp.pad(query_key_gains, ((0, 0), (0, LANES - query_key_gains.shape[1]))),
                    jnp.zeros((10, LANES), BF),
                ],
                axis=0,
            )

        def packed(names, l, gains=False, of=()):
            layout = Layout(s, names, gains)
            arrays = {m: arrays_of(k)[m] for m, k in of} if of else arrays_of(l)
            return layout, pack(s, layout, arrays, gain_block)

        def fetch(made, scheme, start=None, turn=()):
            layout, mine = made
            if not fast:
                return Chunk(layout, [mine], plain_ids)
            if scheme == N.y:
                over = [after(mine, start.pieces[1]), after(mine, start.pieces[3])]
                px, py = swap(s, over[0], XBIT), swap(s, over[1], YBIT)
                here = [mine, px, py, swap(s, py, XBIT)]
                chunk = Chunk(layout, here + [swap(s, piece, CORE) for piece in here], plain_ids)
                chunk.gates = over
                return chunk
            if start is not None:
                mine = after(mine, *start)
            if scheme == N.whole:
                whole = Chunk(layout, [lax.all_gather(mine, "own", axis=0, tiled=True)], jnp.arange(n, dtype=jnp.int32))
                whole.mine = mine
                return whole
            if scheme == N.direct:
                return Chunk(layout, gather_direct(s, mine), plain_ids)
            if scheme == N.paired:
                return Chunk(layout, gather_paired(s, mine, odd, turn), paired_ids)
            return Chunk(layout, gather_plain(s, mine, scheme == N.x, turn), plain_ids)

        pack_g, pack_q = packed(g_names + d_names, 0), packed(q_names, 0, gains=fast)
        pack_lr = packed(lr_names, 1)
        first = [(m, 0) for m in o_names] + [(m, 1) for m in lq_names]
        pack_o = packed(o_names + lq_names, None, of=first)
        chunk_g = fetch(pack_g, N.whole)
        chunk_q = fetch(pack_q, N.x, None, (stream0, v[N.cos], pack_g[1], pack_o[1], pack_lr[1]))
        chunk_o = fetch(pack_o, N.y, chunk_q)
        chunk_lq = chunk_o
        if fast:
            v[N.stream0] = after(v[N.stream0], *chunk_o.gates)
        loop0 = {**{m: chunk_q for m in q_names}, **{m: chunk_o for m in o_names}}
        loop0 |= {m: chunk_g for m in g_names + d_names}
        of_loop = [loop0]

        def wts(names, l):
            return [(m, of_loop[l][m]) for m in names]

        T, D, HD, H, R, F = s.T, s.D, s.HD, s.H, s.R, s.F
        blocks = F // 256
        half = n // 2 if fast else n
        shapes = {
            N.norm: ((16, D), F32),
            N.qkg: ((16, HD), F32),
            N.stream1: ((T, D), F32),
            N.stream2: ((T, D), F32),
            N.o_acc: ((H * s.QB, HD), F32),
            N.l_acc: ((H * s.QB, LANES), F32),
            N.dkv_acc: ((T // s.IB, n * s.IB, 2 * HD), F32),
            N.sgrad1: ((T, D), F32),
            N.sgrad0: ((T, D), F32),
            N.gain_norm: ((16, D), F32),
            N.gain_heads: ((16, HD), F32),
        }
        for l in (0, 1):
            shapes |= {
                N.attn_in(l): ((T, D), BF),
                N.mid(l): ((3, T, R), BF),
                N.raw(l): ((H + 1, T, HD), F32),
                N.q(l): ((H, T, HD), BF),
                N.kv(l): ((T, 2 * HD), BF),
                N.att(l): ((H, T, HD), F32),
                N.lse(l): ((H, T, LANES), F32),
                N.ho(l): ((H, T, HD), BF),
                N.omid(l): ((T, R), BF),
                N.branch(l): ((T, D), F32),
                N.middle(l): ((T, D), F32),
                N.ffn_in(l): ((T, D), BF),
                N.gmid(l): ((2, T, R), BF),
                N.gu(l): ((blocks, T, 512), BF if l == 0 else F32),
                N.hidden(l): ((blocks, T, 256), BF),
                N.dmid(l): ((T, R), BF),
                N.ffn_out(l): ((T, D), F32),
                N.ffn_low(l): ((T, D), BF),
                N.dmg(l): ((T, R), BF),
                N.gug(l): ((2 * blocks, T, 256), BF),
                N.gmg(l): ((2, T, R), BF),
                N.mgrad(l): ((T, D), F32),
                N.blow(l): ((T, D), BF),
                N.omg(l): ((T, R), BF),
                N.hgrad(l): ((H, T, HD), BF),
                N.dq(l): ((H, T, HD), F32),
                N.dkvkeep(l): ((half, T, 2 * HD), BF),
                N.dkvsend(l): ((half, T, 2 * HD), BF),
                N.rawq_low(l): ((H, T, HD), BF),
                N.rawkv_low(l): ((2, T, HD), BF),
                N.midgq(l): ((T, R), BF),
                N.midgkv(l): ((2, T, R), BF),
                N.agrad(l): ((T, D), F32),
                N.dqg(l): ((1, HD), F32),
                N.dkg(l): ((1, HD), F32),
            }
            for i in range(4):
                shapes[N.dnorm(l, i)] = ((1, D), F32)

        def call(name, stages, ins, outs, scratch=(), weights=(), smem=(), micros=0, hold=None, early=()):
            made = run_kernel(
                s,
                name,
                stages,
                {m: v[m] for m in ins},
                {m: shapes[m] for m in outs},
                {m: shapes[m] for m in scratch},
                weights,
                {m: v[m] for m in smem},
                micros,
                hold,
                early,
            )
            v.update(made)

        v[N.first_block] = first_block.astype(jnp.int32)
        v[N.place] = jnp.stack([own & 1, own >> 1]).astype(jnp.int32)

        def share_kv(l):
            if fast:
                pieces = gather_direct(s, v[N.kv(l)])
            else:
                gathered = lax.all_gather(v[N.kv(l)], "own", axis=0, tiled=False)
                pieces = [gathered]
            for i, piece in enumerate(pieces):
                v[N.kvp(l, i)] = piece

        def kv_names(l):
            return [N.kvp(l, i) for i in range(s.kv_pieces)]

        qkv_outs = [N.attn_in, N.mid, N.raw, N.q, N.kv]

        def fill(names, l):
            return [m(l) for m in names]

        if fast:
            call(
                N.qkv0,
                [stage_gains(s, chunk_q), stage_qkv(s, 0, N.stream0)],
                [N.stream0, N.cos, N.sin],
                [N.norm, N.qkg] + fill(qkv_outs, 0),
                weights=[(N.gains, chunk_q)] + wts(q_names, 0),
                micros=6.5,
            )
        else:
            norm = lax.all_gather(norm_gain_table, "own", axis=1, tiled=True).astype(F32)
            heads = lax.all_gather(query_key_gains, "own", axis=1, tiled=True).astype(F32)
            v[N.norm] = jnp.pad(norm, ((0, 12), (0, 0)))
            v[N.qkg] = jnp.pad(heads, ((4, 10), (0, 0)))
            call(
                N.qkv0,
                [stage_qkv(s, 0, N.stream0)],
                [N.stream0, N.cos, N.sin, N.norm, N.qkg],
                fill(qkv_outs, 0),
                weights=wts(q_names, 0),
                micros=6.5,
            )
        share_kv(0)
        if fast:
            mine = after(pack_lr[1], v[N.kvp(0, 3)])
            here = [mine] + [swap(s, mine, bit) for bit in (XBIT, YBIT, XBIT | YBIT)]
        of_loop.append({**loop0, **{m: chunk_lq for m in lq_names}})
        att_ins = [N.qslot, N.qstart, N.kslot]
        out_outs = [N.att, N.lse, N.ho, N.omid, N.branch, N.middle, N.ffn_in]
        ffn_outs = [N.gmid, N.gu, N.hidden, N.dmid, N.ffn_out]
        call(
            N.loop0,
            [stage_attend(s, 0), stage_out(s, 0, N.stream0), stage_ffn(s, 0), stage_qkv(s, 1, N.stream1)],
            [N.stream0, N.q0, N.norm, N.qkg, N.cos, N.sin] + att_ins + kv_names(0),
            fill(out_outs + ffn_outs, 0) + [N.stream1] + fill(qkv_outs, 1),
            scratch=[N.o_acc, N.l_acc],
            weights=wts(o_names + (N.agu, N.gu, N.bg, N.bu) + d_names, 0)
            + wts((N.aqkv, N.qkv, N.bk, N.bv, N.bq), 1),
            smem=[N.first_block],
            micros=20,
            early={N.att0: 0, N.lse0: 0, N.ho0: 1, N.branch0: 1, N.middle0: 1, N.gu0: 2, N.hidden0: 2, N.ffn_out0: 2}
            if fast
            else (),
        )
        chunk_lr = Chunk(*pack_lr[:1], [pack_lr[1]], plain_ids)
        if fast:
            here = list(after_all(here, [v[N.stream1]]))
            chunk_lr.pieces = here + [swap(s, piece, CORE) for piece in here]
        of_loop[1] |= {m: chunk_lr for m in lr_names}
        share_kv(1)
        loop1 = [
            stage_attend(s, 1),
            stage_out(s, 1, N.stream1),
            stage_ffn(s, 1),
            stage_ffn_back(s, 1, N.cot),
            stage_out_back(s, 1),
        ]
        loop1_outs = (
            [N.stream2, N.mgrad1]
            + fill([N.ho, N.omid, N.ffn_in, N.gmid, N.hidden, N.dmid], 1)
            + fill([N.ffn_low, N.dmg, N.gug, N.gmg, N.blow, N.omg], 1)
            + [N.dnorm(1, 1), N.dnorm(1, 2), N.dnorm(1, 3)]
        )
        loop1_scratch = [N.o_acc, N.l_acc, N.branch1, N.middle1, N.gu1, N.ffn_out1]
        back_outs = [N.dq, N.dkvkeep] + ([N.dkvsend] if fast else [])
        kept = [N.att1, N.lse1, N.hgrad1]
        call(
            N.loop1,
            loop1 + ([stage_attend_back(s, 1)] if fast else []),
            [N.stream1, N.q1, N.norm, N.cot] + att_ins + kv_names(1),
            loop1_outs + (fill(back_outs, 1) if fast else kept),
            scratch=loop1_scratch + ([N.dkv_acc] + kept if fast else []),
            weights=wts(o_names + g_names + d_names, 1),
            smem=[N.first_block],
            micros=35,
            early={N.ho1: 1, N.hidden1: 2, N.stream2: 2, N.gug1: 3, N.mgrad1: 3} if fast else (),
        )
        if not fast:
            call(
                N.attend_back1,
                [stage_attend_back(s, 1)],
                [N.q1] + kept + att_ins + kv_names(1),
                fill(back_outs, 1),
                scratch=[N.o_acc, N.dkv_acc],
                smem=[N.first_block],
                micros=10,
            )

        plans = {
            N.la: [((N.bg, N.bu, N.agu, N.dna, N.dnb, N.outa, N.outb), 1)],
            N.g1: [((N.gug,), 0), ((N.aqkv,), 1)],
            N.g2: [((N.guu,), 0), ((N.bq, N.bk, N.bv), 1)],
            N.g3: [((N.dnw, N.agu), 0)],
            N.g4: [((N.bg, N.bu, N.dna, N.dnb), 0)],
            N.rb: [((N.outw, N.outa, N.outb, N.bq, N.qkvq, N.aqkvq), 0)],
            N.ra: [((N.qkvkv, N.aqkvkv, N.bk, N.bv), 0)],
        }
        modes = {N.la: N.direct, N.g1: N.x, N.g2: N.y, N.g3: N.x, N.g4: N.y, N.rb: N.direct, N.ra: N.direct}
        layouts = {}
        where = {}
        for m, parts in plans.items():
            layouts[m] = Layout(s, [name for names, _ in parts for name in names], gains=(m == N.ra and fast))
            shapes[N.keep(m)] = ((half if fast else 1, layouts[m].total, LANES), BF)
            shapes[N.send(m)] = shapes[N.keep(m)]
            where |= {(name, l): m for names, l in parts for name in names}

        def grads(names, ins, micros, extra=(), extra_outs=()):
            parts = []
            for m in names:
                parts += [(m, layouts[m], group, [0, 1], l) for group, l in plans[m]]
            outs = [end(m) for m in names for end in ((N.keep, N.send) if fast else (N.keep,))]
            call(
                N.grads(names[0]),
                [stage_grads(s, parts)] + list(extra),
                ins,
                outs + list(extra_outs),
                smem=[N.place] if fast else [],
                micros=micros,
            )

        sums = {}

        def open_sum(*names):
            for m in names:
                if fast:
                    sums[m] = Sum(s, v[N.keep(m)], v[N.send(m)], modes[m], odd)

        def open_kv(l):
            if fast:
                sums[N.dkv(l)] = Sum(s, v[N.dkvkeep(l)], v[N.dkvsend(l)], N.direct)
            else:
                keep = v[N.dkvkeep(l)].reshape(n * T, 2 * HD)
                v[N.dkv] = lax.psum_scatter(keep, "own", scatter_dimension=0, tiled=True)

        def close_kv(l):
            if fast:
                v[N.dkv] = sums[N.dkv(l)].payload[0]

        def phase(starts, inputs=(), need=()):
            if not fast:
                return
            starts, inputs = [sums[m] for m in starts], list(inputs)
            others = []
            for m in need:
                others += sums[m].payload if m in sums else [v[m]]
            values = after_all([p for r in starts for p in r.payload] + [v[m] for m in inputs], others)
            for r in starts:
                count = len(r.payload)
                r.payload, values = values[:count], values[count:]
            for m, value in zip(inputs, values):
                v[m] = value
            for r in starts:
                r.step()

        gain_ins = [N.dnorm(l, i) for l in (0, 1) for i in range(4)] + [N.dqg0, N.dqg1, N.dkg0, N.dkg1]
        qkv_l = [N.attn_in, N.mid, N.rawq_low, N.rawkv_low, N.midgq, N.midgkv]

        open_kv(1)
        phase([N.dkv1], [N.gmg1])
        grads(
            [N.la],
            [N.ffn_in1, N.gmid1, N.gug1, N.gmg1, N.hidden1, N.dmid1, N.ffn_low1, N.dmg1, N.ho1, N.omid1, N.blow1, N.omg1],
            8.6,
        )
        open_sum(N.la)
        phase([N.dkv1, N.la], [N.dq1])
        call(
            N.q_back1,
            [stage_q_back(s, 1)],
            [N.cos, N.sin, N.qkg, N.dq1, N.raw1],
            [N.rawq_low1, N.midgq1, N.agrad1, N.dqg1],
            weights=wts((N.qkv, N.bq, N.aqkv), 1),
            micros=5.8,
        )
        phase([N.la], [N.agrad1], [N.dkv1])
        close_kv(1)
        call(
            N.kv_back1,
            [stage_kv_back(s, 1, N.stream1, N.sgrad1), stage_ffn_back(s, 0, N.sgrad1)],
            [N.cos, N.sin, N.qkg, N.norm, N.dkv, N.raw1, N.agrad1, N.stream1, N.mgrad1]
            + [N.ffn_out0, N.gu0, N.middle0],
            [N.dkg1, N.rawkv_low1, N.midgkv1, N.dnorm(1, 0), N.dnorm(0, 3), N.dnorm(0, 2)]
            + fill([N.ffn_low, N.dmg, N.gug, N.gmg, N.mgrad], 0),
            scratch=[N.sgrad1],
            weights=wts((N.qkv, N.aqkv, N.bk, N.bv), 1) + wts((N.dnb, N.dnw, N.dna, N.bg, N.bu, N.gu, N.agu), 0),
            micros=17,
        )
        grads([N.g1, N.g2], fill([N.ffn_in, N.gug], 0) + [N.ffn_in1, N.gug1] + fill(qkv_l, 1), 9.7)
        open_sum(N.g1, N.g2)
        phase([N.g1, N.g2], [N.mgrad0], [N.la])
        call(
            N.out_back0,
            [stage_out_back(s, 0)],
            [N.branch0, N.norm, N.mgrad0],
            [N.dnorm(0, 1), N.blow0, N.omg0, N.hgrad0],
            weights=wts(o_names, 0),
            micros=4.5,
        )
        phase([N.g1, N.g2, N.la], [N.dmg0, N.hgrad0], [N.blow0])
        grads(
            [N.g3, N.g4],
            fill([N.ffn_in, N.gmid, N.gug, N.gmg, N.hidden, N.dmid, N.ffn_low, N.dmg], 0) + [N.hidden1, N.ffn_low1],
            8.5,
        )
        open_sum(N.g3, N.g4)
        if fast:
            v[N.hgrad0] = after(v[N.hgrad0], v[N.keep(N.g3)])
        call(
            N.attend_back0,
            [stage_attend_back(s, 0)],
            [N.hgrad0, N.q0, N.att0, N.lse0] + att_ins + kv_names(0),
            fill(back_outs, 0),
            scratch=[N.o_acc, N.dkv_acc],
            smem=[N.first_block],
            micros=13,
        )
        open_kv(0)
        phase([N.dkv0, N.g1, N.g2, N.la], [N.dq0])
        call(
            N.q_back0,
            [stage_q_back(s, 0)],
            [N.cos, N.sin, N.qkg, N.dq0, N.raw0],
            [N.rawq_low0, N.midgq0, N.agrad0, N.dqg0],
            weights=wts((N.qkv, N.bq, N.aqkv), 0),
            micros=5.8,
        )
        phase([N.dkv0, N.g3, N.g4], [N.rawq_low0], [N.g1, N.g2])
        grads(
            [N.rb],
            fill([N.ho, N.omid, N.blow, N.omg, N.mid, N.rawq_low, N.attn_in, N.midgq], 0)
            + [N.ho1, N.blow1, N.attn_in1, N.rawq_low1],
            7,
        )
        open_sum(N.rb)
        phase([N.g3, N.g4, N.rb, N.g1, N.g2], [N.agrad0, N.stream2], [N.dkv0])
        close_kv(0)
        mixed = unsort_rows(s, rank, v[N.stream2])
        v[N.mixed] = mixed
        call(
            N.kv_back0,
            [stage_kv_back(s, 0, N.stream0, N.sgrad0)],
            [N.cos, N.sin, N.qkg, N.norm, N.dkv, N.raw0, N.agrad0, N.stream0, N.mgrad0],
            [N.dkg0, N.rawkv_low0, N.midgkv0, N.dnorm(0, 0), N.sgrad0],
            weights=wts((N.qkv, N.aqkv, N.bk, N.bv), 0),
            micros=6.2,
        )
        grads(
            [N.ra],
            fill([N.attn_in, N.mid, N.rawkv_low, N.midgkv], 0) + [N.attn_in1, N.rawkv_low1] + gain_ins,
            3,
            [stage_gain_grads(s, N.ra, layouts[N.ra])],
            [] if fast else [N.gain_norm, N.gain_heads],
        )
        open_sum(N.ra)
        tokens_grad = unsort_rows(s, rank, v[N.sgrad0])
        v[N.tokens_grad] = tokens_grad
        phase([N.g3, N.g4, N.ra, N.la], [], [N.mixed, N.tokens_grad, N.g1, N.g2])
        phase([N.rb, N.g1, N.g2], [], [N.g3, N.g4, N.ra])
        phase([N.ra, N.g3, N.g4], [], [N.rb, N.g1, N.g2])
        phase([N.ra, N.rb, N.g3, N.g4, N.g1])
        phase([N.ra, N.rb, N.g3, N.g4, N.g2])
        phase([N.ra, N.rb])
        for m in sums:
            assert m in (N.dkv0, N.dkv1) or not sums[m].steps
        finished = {m: sums[m].payload for m in plans if fast}

        HB, RB = s.HB, s.RB
        two = (0, 1)
        targets = [
            (shared_attention_matrix.shape, [((), N.qkvq, 0, 0), ((), N.qkvkv, 0, H * HB)]),
            (shared_output_matrix.shape, [((), N.outw, 0, 0)]),
            (shared_gate_up_matrix.shape, [((), N.gug, 0, 0), ((), N.guu, 0, F // LANES)]),
            (shared_down_matrix.shape, [((), N.dnw, 0, 0)]),
            (
                adapter_attention_first.shape,
                [((0,), N.aqkvq, 0, 0), ((0,), N.aqkvkv, 0, RB), ((1,), N.aqkv, 1, 0)],
            ),
            (adapter_query_second.shape, [((l,), N.bq, l, 0) for l in two]),
            (
                adapter_key_value_second.shape,
                [((l, j), m, l, 0) for l in two for j, m in enumerate((N.bk, N.bv))],
            ),
            (adapter_output_first.shape, [((l,), N.outa, l, 0) for l in two]),
            (adapter_output_second.shape, [((l,), N.outb, l, 0) for l in two]),
            (adapter_gate_first.shape, [((l,), N.agu, l, 0) for l in two]),
            (adapter_gate_second.shape, [((l, j), m, l, 0) for l in two for j, m in enumerate((N.bg, N.bu))]),
            (adapter_down_first.shape, [((l,), N.dna, l, 0) for l in two]),
            (adapter_down_second.shape, [((l,), N.dnb, l, 0) for l in two]),
        ]
        if fast:
            plan = [(shape, [(lead, where[m, l], m, col) for lead, m, l, col in parts]) for shape, parts in targets]
            made = [None] * len(plan)
            early = [i for i, (_, parts) in enumerate(plan) if all(part[1][0] in N.lg for part in parts)]
            late = [i for i in range(len(plan)) if i not in early]
            ends = [
                (norm_gain_table.shape, [((0, 4), N.ra, N.norm, 0)]),
                (query_key_gains.shape, [((4, 2), N.ra, N.norm, 0)]),
            ]
            for which, last in ((early, []), (late, ends)):
                chosen = [plan[i] for i in which] + last
                used = sorted({part[1] for _, parts in chosen for part in parts})
                results = unpack(s, chosen, {m: (*finished[m], layouts[m]) for m in used})
                for i, value in zip(which, results):
                    made[i] = value
            grads, (norm_grad, heads_grad) = made, results[-2:]
        else:

            def natural(name, l):
                layout = layouts[where[name, l]]
                first, rows, count = layout.at[name]
                block = v[N.keep(where[name, l])][0, first : first + rows * count]
                return block.reshape(count, rows, LANES).transpose(1, 0, 2).reshape(rows, count * LANES)

            def reduced(value, axis):
                part = lax.psum_scatter(value.astype(BF), "own", scatter_dimension=axis, tiled=True)
                return lax.psum(part, "dp").astype(F32)

            grads = []
            for shape, parts in targets:
                of_lead = {}
                for lead, m, l, _ in parts:
                    of_lead.setdefault(lead, []).append(natural(m, l))
                value = jnp.stack([side_by_side(columns_of) for columns_of in of_lead.values()])
                value = value.reshape(shape[:-2] + value.shape[1:])
                grads.append(reduced(value, len(shape) - 2))
            norm_grad = reduced(v[N.gain_norm][:4], 1)
            heads_grad = reduced(v[N.gain_heads][4:6], 1)
        return (mixed, tokens_grad) + tuple(grads[:4]) + (norm_grad, heads_grad) + tuple(grads[4:])

    return shards


def solution(mesh):
    both, rows = P(("dp", "own"), None), P("own", None)
    second, third = P(None, "own", None), P(None, None, "own", None)
    wide_gain = P(None, "own")
    in_specs = (
        (both, both, P("dp", None), P("dp", None), rows, rows, rows, rows, wide_gain, wide_gain)
        + (second, second, third, second, second, second, third, second, second)
    )
    out_specs = (
        (both, both, rows, rows, rows, rows, wide_gain, wide_gain)
        + (second, second, third, second, second, second, third, second, second)
    )
    return jax.shard_map(make_shards(mesh), mesh=mesh, in_specs=in_specs, out_specs=out_specs, check_vma=False)
```

```python
import math

import jax
import jax.numpy as jnp
from jax import lax
from jax.experimental import pallas as pl
from jax.experimental.pallas import tpu as pltpu
from jax.sharding import PartitionSpec as P

BF = jnp.bfloat16
F32 = jnp.float32
EPS = 1e-06
THETA = 1000000.0
LANES = 128
LOG2E = 1.4426950408889634
VMEM_LIMIT = 60 * 2**20
PEAK = 1e6
CORE, XBIT, YBIT = 1, 2, 4


def dot(a, b):
    return jnp.dot(a, b, preferred_element_type=F32)


def dot_nt(a, b):
    return lax.dot_general(a, b, (((1,), (1,)), ((), ())), preferred_element_type=F32)


def dot_tn(a, b):
    return lax.dot_general(a, b, (((0,), (0,)), ((), ())), preferred_element_type=F32)


def side_by_side(parts):
    return parts[0] if len(parts) == 1 else jnp.concatenate(parts, axis=1)


def stacked(parts):
    return parts[0] if len(parts) == 1 else jnp.concatenate(parts, axis=0)


class Name(str):
    def __call__(self, *more):
        return Name(self + str().join(str(m) for m in more))


class Names:
    def __getattr__(self, name):
        return Name(name)


N = Names()


class Sizes:
    pass


class Layout:
    def __init__(self, sizes, names, gains=False):
        self.at = {}
        total = 0
        for name in names:
            rows, blocks = sizes.shard[name]
            self.at[name] = (total, rows, blocks)
            total += rows * blocks
        self.gains = None
        if gains:
            self.gains = total
            total += 16
        self.total = total


class Chunk:
    def __init__(self, layout, pieces, ids):
        self.layout, self.pieces, self.ids, self.mine = layout, pieces, ids, pieces[0]


class Env:
    def __init__(self):
        self.refs = {}
        self.pending = {}
        self.later = []

    def __getitem__(self, name):
        return self.refs[name]

    def w(self, name):
        if name in self.pending:
            sem = self.pending.pop(name)
            ref = self.refs[N.w(name)]
            pltpu.make_async_copy(ref, ref, sem).wait()
            if name == self.hold:
                for copy in self.later:
                    copy.start()
                self.later = []
        return self.refs[N.w(name)]


def run_kernel(sizes, name, stages, ins, outs, scratch=(), weights=(), smem=(), micros=0, hold=None, early=()):
    early = dict(early)
    chunks = []
    for _, chunk in weights:
        if chunk not in chunks:
            chunks.append(chunk)
    smem = dict(smem)
    for number, chunk in enumerate(chunks):
        smem[N.ids(number)] = chunk.ids
    scratch = dict(scratch)
    names_in = list(ins)
    names_smem = list(smem)
    pieces = [piece for chunk in chunks for piece in chunk.pieces]
    names_out = list(outs)
    names_scratch = list(scratch)
    shapes = []
    for wname, chunk in weights:
        if wname == N.gains:
            shapes.append(((sizes.slots, 16, LANES), BF))
        else:
            _, rows, blocks = chunk.layout.at[wname]
            shapes.append(((blocks, rows * sizes.slots, LANES), BF))

    def kernel(*refs):
        env = Env()
        env.hold, held = hold, False
        position = 0
        for key in names_smem + names_in:
            env.refs[key] = refs[position]
            position += 1
        piece_refs = refs[position : position + len(pieces)]
        position += len(pieces)
        for key in names_out + names_scratch:
            env.refs[key] = refs[position]
            position += 1
        whole = {}
        for key in early:
            whole[key] = env.refs[key]
            env.refs[key] = refs[len(refs) - 2 * len(early) + list(early).index(key)]
        of_chunk = {}
        start = 0
        for number, chunk in enumerate(chunks):
            of_chunk[number] = piece_refs[start : start + len(chunk.pieces)]
            start += len(chunk.pieces)
        for number, (wname, chunk) in enumerate(weights):
            buffer = refs[position]
            position += 1
            env.refs[N.w(wname)] = buffer
        for number, (wname, chunk) in enumerate(weights):
            sem = refs[position]
            position += 1
            buffer = env.refs[N.w(wname)]
            which = chunks.index(chunk)
            for slot in range(sizes.slots):
                piece = of_chunk[which][0 if len(chunk.pieces) == 1 else slot]
                offset = slot * chunk.layout.total if len(chunk.pieces) == 1 else 0
                if wname == N.gains:
                    source = piece.at[pl.ds(offset + chunk.layout.gains, 16), :]
                    target = buffer.at[slot]
                else:
                    first, rows, blocks = chunk.layout.at[wname]
                    first = offset + first
                    source = piece.at[pl.ds(first, blocks * rows), :].reshape(blocks, rows, LANES)
                    if sizes.slots == 1:
                        target = buffer
                    else:
                        row = pl.multiple_of(env[N.ids(which)][slot] * rows, 16)
                        target = buffer.at[:, pl.ds(row, rows), :]
                copy = pltpu.make_async_copy(source, target, sem)
                if held:
                    env.later.append(copy)
                else:
                    copy.start()
            env.pending[wname] = sem
            held = held or wname == hold
        env.ids = lambda chunk: env[N.ids(chunks.index(chunk))]
        going = []
        early_sems = dict(zip(early, refs[len(refs) - len(early) :]))
        for number, stage in enumerate(stages):
            stage(env)
            for key, last in early.items():
                if last == number:
                    going.append(pltpu.make_async_copy(env[key], whole[key], early_sems[key]))
                    going[-1].start()
        for wname, _ in weights:
            env.w(wname)
        for copy in going:
            copy.wait()

    any_space = pl.BlockSpec(memory_space=pl.ANY)
    vmem = pl.BlockSpec(memory_space=pltpu.VMEM)
    nbytes = sum(math.prod(a.shape) * a.dtype.itemsize for a in list(ins.values()) + pieces)
    nbytes += sum(math.prod(s) * jnp.dtype(d).itemsize for s, d in outs.values())
    results = pl.pallas_call(
        kernel,
        name=name,
        out_shape=[jax.ShapeDtypeStruct(*outs[key]) for key in names_out],
        in_specs=[pl.BlockSpec(memory_space=pltpu.SMEM)] * len(names_smem)
        + [vmem] * len(names_in)
        + [any_space] * len(pieces),
        out_specs=[any_space if key in early else vmem for key in names_out],
        scratch_shapes=[pltpu.VMEM(*scratch[key]) for key in names_scratch]
        + [pltpu.VMEM(*shape) for shape in shapes]
        + [pltpu.SemaphoreType.DMA] * len(weights)
        + [pltpu.VMEM(*outs[key]) for key in early]
        + [pltpu.SemaphoreType.DMA] * len(early),
        compiler_params=pltpu.CompilerParams(vmem_limit_bytes=VMEM_LIMIT),
        cost_estimate=pl.CostEstimate(flops=int(micros * PEAK), bytes_accessed=0, transcendentals=0),
    )(*smem.values(), *ins.values(), *pieces)
    return dict(zip(names_out, results))


def columns(weight, first, count, rows=None):
    if rows is None:
        return side_by_side([weight[first + i] for i in range(count)])
    return side_by_side([weight[first + i, rows] for i in range(count)])


def root(values):
    return lax.rsqrt(jnp.mean(values * values, axis=-1, keepdims=True) + EPS)


def rms_back(values, gain, grad):
    r = root(values)
    scaled = grad * gain
    back = r * scaled - values * (r * r * r * jnp.mean(values * scaled, axis=-1, keepdims=True))
    return back, jnp.sum(values * r * grad, axis=0, keepdims=True)


def rotate(values, cos, sin):
    half = values.shape[-1] // 2
    p, q = values[:, :half], values[:, half:]
    return jnp.concatenate([p * cos - q * sin, q * cos + p * sin], axis=1)


def rotate_back(grad, cos, sin):
    half = grad.shape[-1] // 2
    a, b = grad[:, :half], grad[:, half:]
    return jnp.concatenate([a * cos + b * sin, b * cos - a * sin], axis=1)


GELU_A = math.sqrt(2.0 / math.pi)
GELU_B = 0.044715


def gelu_parts(v):
    t = jnp.tanh(GELU_A * (v + GELU_B * v * v * v))
    return 0.5 * v * (1.0 + t), t


def gelu_slope(v, t):
    return 0.5 * (1.0 + t) + 0.5 * v * (1.0 - t * t) * (GELU_A * (1.0 + 3.0 * GELU_B * v * v))


def stage_gains(sizes, chunk):
    def stage(env):
        blocks = env.w(N.gains)
        ids = env.ids(chunk)
        norm = jnp.zeros((16, sizes.D), F32)
        heads = jnp.zeros((16, sizes.HD), F32)
        width, head_width = sizes.D // sizes.slots, sizes.HD // sizes.slots

        def pick(total, each, index):
            a = lax.broadcasted_iota(jnp.int32, (LANES, total), 0)
            b = lax.broadcasted_iota(jnp.int32, (LANES, total), 1)
            return jnp.where((b == a + index * each) & (a < each), 1.0, 0.0).astype(BF)

        for m in range(sizes.slots):
            norm = norm + dot(blocks[m], pick(sizes.D, width, ids[m]))
            heads = heads + dot(blocks[m], pick(sizes.HD, head_width, ids[m]))
        env[N.norm][...] = norm
        env[N.qkg][...] = heads

    return stage


def stage_qkv(sizes, l, stream):
    def stage(env):
        x = env[stream][...]
        attn_in = (x * root(x) * env[N.norm][0:1, :]).astype(BF)
        env[N.attn_in(l)][...] = attn_in
        first = env.w(N.aqkv)
        mids = []
        for j in range(3):
            mid = dot(attn_in, columns(first, sizes.RB * j, sizes.RB)).astype(BF)
            env[N.mid(l)][j] = mid
            mids.append(mid)
        qkv, hb = env.w(N.qkv), sizes.HB
        cos, sin = env[N.cos][...], env[N.sin][...]
        gq, gk = env[N.qkg][4:5, :], env[N.qkg][5:6, :]
        bk, bv, bq = env.w(N.bk), env.w(N.bv), env.w(N.bq)
        raw = dot(attn_in, columns(qkv, hb * sizes.H, hb)) + dot(mids[1], columns(bk, 0, hb))
        env[N.raw(l)][sizes.H] = raw
        env[N.kv(l)][:, : sizes.HD] = rotate(raw * root(raw) * gk, cos, sin).astype(BF)
        raw = dot(attn_in, columns(qkv, hb * (sizes.H + 1), hb)) + dot(mids[2], columns(bv, 0, hb))
        env[N.kv(l)][:, sizes.HD :] = raw.astype(BF)
        for h in range(sizes.H):
            raw = dot(attn_in, columns(qkv, hb * h, hb)) + dot(mids[0], columns(bq, hb * h, hb))
            env[N.raw(l)][h] = raw
            env[N.q(l)][h] = rotate(raw * root(raw) * gq, cos, sin).astype(BF)

    return stage


def key_block(sizes, pieces, b, value):
    lanes = slice(sizes.HD, 2 * sizes.HD) if value else slice(0, sizes.HD)
    rows = pl.ds(pl.multiple_of(b * sizes.IB, 16), sizes.IB)
    parts = []
    for piece in pieces:
        if len(piece.shape) == 3:
            parts += [piece[g, rows, lanes] for g in range(piece.shape[0])]
        else:
            parts.append(piece[rows, lanes])
    return stacked(parts)


def query_limits(sizes, env, qb):
    rows = slice(qb * sizes.QB, (qb + 1) * sizes.QB)
    slot = jnp.concatenate([env[N.qslot][rows, :]] * sizes.H, axis=0)
    low = jnp.concatenate([env[N.qstart][rows, :]] * sizes.H, axis=0)
    last = -(-(qb + 1) * sizes.QB // sizes.IB)
    return rows, slot, low, last


def stage_attend(sizes, l):
    scale = sizes.HD ** (-0.5) * LOG2E
    M = sizes.H * sizes.QB

    def stage(env):
        pieces = [env[N.kvp(l, i)] for i in range(sizes.kv_pieces)]
        for qb in range(sizes.T // sizes.QB):
            rows, slot, low, last = query_limits(sizes, env, qb)
            query = env[N.q(l)][:, rows, :].reshape(M, sizes.HD)
            env[N.o_acc][...] = jnp.zeros((M, sizes.HD), F32)
            env[N.l_acc][...] = jnp.zeros((M, LANES), F32)

            def body(b, carry):
                keys = env[N.kslot][b]
                scores = dot_nt(query, key_block(sizes, pieces, b, False))
                allowed = (keys <= slot) & (keys >= low)
                probs = jnp.where(allowed, jnp.exp2(scores * scale), 0.0)
                part = probs[:, :LANES]
                for i in range(1, probs.shape[1] // LANES):
                    part = part + probs[:, i * LANES : (i + 1) * LANES]
                env[N.l_acc][...] += part
                env[N.o_acc][...] += dot(probs.astype(BF), key_block(sizes, pieces, b, True))
                return carry

            lax.fori_loop(env[N.first_block][qb], last, body, 0)
            total = jnp.sum(env[N.l_acc][...], axis=1, keepdims=True)
            env[N.att(l)][:, rows, :] = (env[N.o_acc][...] / total).reshape(sizes.H, sizes.QB, sizes.HD)
            env[N.lse(l)][:, rows, :] = jnp.broadcast_to(jnp.log2(total), (M, LANES)).reshape(
                sizes.H, sizes.QB, LANES
            )

    return stage


def stage_out(sizes, l, stream):
    def stage(env):
        outa, outw, outb = env.w(N.outa), env.w(N.outw), env.w(N.outb)
        mid = jnp.zeros((sizes.T, sizes.R), F32)
        branch = jnp.zeros((sizes.T, sizes.D), F32)
        for h in range(sizes.H):
            heads = env[N.att(l)][h].astype(BF)
            env[N.ho(l)][h] = heads
            rows = slice(h * sizes.HD, (h + 1) * sizes.HD)
            mid = mid + dot(heads, columns(outa, 0, sizes.RB, rows))
            branch = branch + dot(heads, columns(outw, 0, sizes.DB, rows))
        mid = mid.astype(BF)
        env[N.omid(l)][...] = mid
        branch = branch + dot(mid, columns(outb, 0, sizes.DB))
        env[N.branch(l)][...] = branch
        middle = env[stream][...] + branch * root(branch) * env[N.norm][1:2, :]
        env[N.middle(l)][...] = middle
        env[N.ffn_in(l)][...] = (middle * root(middle) * env[N.norm][2:3, :]).astype(BF)

    return stage


def stage_ffn(sizes, l):
    def stage(env):
        x = env[N.ffn_in(l)][...]
        agu = env.w(N.agu)
        mids = []
        for j in range(2):
            mid = dot(x, columns(agu, sizes.RB * j, sizes.RB)).astype(BF)
            env[N.gmid(l)][j] = mid
            mids.append(mid)
        bg, bu, gu = env.w(N.bg), env.w(N.bu), env.w(N.gu)
        blocks = sizes.F // 256
        out = jnp.zeros((sizes.T, sizes.D), F32)
        down = jnp.zeros((sizes.T, sizes.R), F32)
        for b in range(blocks):
            gate = dot(x, columns(gu, 2 * b, 2)) + dot(mids[0], columns(bg, 2 * b, 2))
            up = dot(x, columns(gu, 2 * (blocks + b), 2)) + dot(mids[1], columns(bu, 2 * b, 2))
            env[N.gu(l)][b, :, :256] = gate.astype(env[N.gu(l)].dtype)
            env[N.gu(l)][b, :, 256:] = up.astype(env[N.gu(l)].dtype)
            hidden = (gelu_parts(gate)[0] * up).astype(BF)
            env[N.hidden(l)][b] = hidden
            rows = slice(b * 256, (b + 1) * 256)
            dnw, dna = env.w(N.dnw), env.w(N.dna)
            out = out + dot(hidden, columns(dnw, 0, sizes.DB, rows))
            down = down + dot(hidden, columns(dna, 0, sizes.RB, rows))
        down = down.astype(BF)
        env[N.dmid(l)][...] = down
        out = out + dot(down, columns(env.w(N.dnb), 0, sizes.DB))
        env[N.ffn_out(l)][...] = out
        env[N.stream(l + 1)][...] = env[N.middle(l)][...] + out * root(out) * env[N.norm][3:4, :]

    return stage


def stage_ffn_back(sizes, l, grad):
    def stage(env):
        out_grad = env[grad][...]
        back, gain = rms_back(env[N.ffn_out(l)][...], env[N.norm][3:4, :], out_grad)
        env[N.dnorm(l, 3)][...] = gain
        low = back.astype(BF)
        env[N.ffn_low(l)][...] = low
        dmg = dot_nt(low, columns(env.w(N.dnb), 0, sizes.DB)).astype(BF)
        env[N.dmg(l)][...] = dmg
        dnw, dna = env.w(N.dnw), env.w(N.dna)
        blocks = sizes.F // 256
        gate_mid = jnp.zeros((sizes.T, sizes.R), F32)
        up_mid = jnp.zeros((sizes.T, sizes.R), F32)
        total = jnp.zeros((sizes.T, sizes.D), F32)
        for b in range(blocks):
            rows = slice(b * 256, (b + 1) * 256)
            hidden_grad = dot_nt(low, columns(dnw, 0, sizes.DB, rows)) + dot_nt(
                dmg, columns(dna, 0, sizes.RB, rows)
            )
            gate, up = env[N.gu(l)][b, :, :256].astype(F32), env[N.gu(l)][b, :, 256:].astype(F32)
            value, t = gelu_parts(gate)
            gate_grad = (hidden_grad * up * gelu_slope(gate, t)).astype(BF)
            up_grad = (hidden_grad * value).astype(BF)
            env[N.gug(l)][b] = gate_grad
            env[N.gug(l)][blocks + b] = up_grad
            bg, bu, gu = env.w(N.bg), env.w(N.bu), env.w(N.gu)
            gate_mid = gate_mid + dot_nt(gate_grad, columns(bg, 2 * b, 2))
            up_mid = up_mid + dot_nt(up_grad, columns(bu, 2 * b, 2))
            total = total + dot_nt(gate_grad, columns(gu, 2 * b, 2))
            total = total + dot_nt(up_grad, columns(gu, 2 * (blocks + b), 2))
        agu = env.w(N.agu)
        for j, mid in enumerate((gate_mid, up_mid)):
            mid = mid.astype(BF)
            env[N.gmg(l)][j] = mid
            total = total + dot_nt(mid, columns(agu, sizes.RB * j, sizes.RB))
        back, gain = rms_back(env[N.middle(l)][...], env[N.norm][2:3, :], total)
        env[N.dnorm(l, 2)][...] = gain
        env[N.mgrad(l)][...] = out_grad + back

    return stage


def stage_out_back(sizes, l):
    def stage(env):
        back, gain = rms_back(env[N.branch(l)][...], env[N.norm][1:2, :], env[N.mgrad(l)][...])
        env[N.dnorm(l, 1)][...] = gain
        low = back.astype(BF)
        env[N.blow(l)][...] = low
        omg = dot_nt(low, columns(env.w(N.outb), 0, sizes.DB)).astype(BF)
        env[N.omg(l)][...] = omg
        outw, outa = env.w(N.outw), env.w(N.outa)
        for h in range(sizes.H):
            rows = slice(h * sizes.HD, (h + 1) * sizes.HD)
            grad = dot_nt(low, columns(outw, 0, sizes.DB, rows)) + dot_nt(omg, columns(outa, 0, sizes.RB, rows))
            env[N.hgrad(l)][h] = grad.astype(BF)

    return stage


def stage_attend_back(sizes, l):
    factor = sizes.HD ** (-0.5)
    scale = factor * LOG2E
    M = sizes.H * sizes.QB
    HD = sizes.HD

    def stage(env):
        pieces = [env[N.kvp(l, i)] for i in range(sizes.kv_pieces)]
        total_blocks = sizes.T // sizes.IB
        for b in range(total_blocks):
            env[N.dkv_acc][b] = jnp.zeros((sizes.n * sizes.IB, 2 * HD), F32)
        for qb in range(sizes.T // sizes.QB):
            rows, slot, low, last = query_limits(sizes, env, qb)
            query = env[N.q(l)][:, rows, :].reshape(M, HD)
            grad = env[N.hgrad(l)][:, rows, :].reshape(M, HD)
            attended = env[N.att(l)][:, rows, :].reshape(M, HD)
            row_dot = jnp.sum(grad.astype(F32) * attended, axis=1, keepdims=True)
            lse = env[N.lse(l)][:, rows, :].reshape(M, LANES)[:, 0:1]
            env[N.o_acc][...] = jnp.zeros((M, HD), F32)

            def body(b, carry):
                keys = env[N.kslot][b]
                k = key_block(sizes, pieces, b, False)
                v = key_block(sizes, pieces, b, True)
                allowed = (keys <= slot) & (keys >= low)
                probs = jnp.where(allowed, jnp.exp2(dot_nt(query, k) * scale - lse), 0.0)
                scores_grad = (probs * (dot_nt(grad, v) - row_dot)).astype(BF)
                env[N.o_acc][...] += dot(scores_grad, k)
                env[N.dkv_acc][b, :, :HD] += dot_tn(scores_grad, query)
                env[N.dkv_acc][b, :, HD:] += dot_tn(probs.astype(BF), grad)
                return carry

            lax.fori_loop(env[N.first_block][qb], last, body, 0)
            env[N.dq(l)][:, rows, :] = (env[N.o_acc][...] * factor).reshape(sizes.H, sizes.QB, HD)
        IB = sizes.IB
        for m in range(sizes.n):
            if sizes.slots > 1:
                where = (N.dkvkeep if m < sizes.n // 2 else N.dkvsend, m % (sizes.n // 2))
            else:
                where = (N.dkvkeep, m)
            for b in range(total_blocks):
                for j, by in enumerate((factor, 1.0)):
                    lanes = slice(j * HD, (j + 1) * HD)
                    part = env[N.dkv_acc][b, m * IB : (m + 1) * IB, lanes]
                    env[where[0](l)][where[1], b * IB : (b + 1) * IB, lanes] = (part * by).astype(BF)

    return stage


def stage_q_back(sizes, l):
    def stage(env):
        cos, sin = env[N.cos][...], env[N.sin][...]
        gq = env[N.qkg][4:5, :]
        hb = sizes.HB
        qkv, bq, aqkv = env.w(N.qkv), env.w(N.bq), env.w(N.aqkv)
        gains = jnp.zeros((1, sizes.HD), F32)
        mid = jnp.zeros((sizes.T, sizes.R), F32)
        total = jnp.zeros((sizes.T, sizes.D), F32)
        for h in range(sizes.H):
            turned = rotate_back(env[N.dq(l)][h], cos, sin)
            back, gain = rms_back(env[N.raw(l)][h], gq, turned)
            gains = gains + gain
            low = back.astype(BF)
            env[N.rawq_low(l)][h] = low
            mid = mid + dot_nt(low, columns(bq, hb * h, hb))
            total = total + dot_nt(low, columns(qkv, hb * h, hb))
        mid = mid.astype(BF)
        env[N.midgq(l)][...] = mid
        total = total + dot_nt(mid, columns(aqkv, 0, sizes.RB))
        env[N.agrad(l)][...] = total
        env[N.dqg(l)][...] = gains

    return stage


def stage_kv_back(sizes, l, stream, result):
    def stage(env):
        cos, sin = env[N.cos][...], env[N.sin][...]
        hb = sizes.HB
        qkv, aqkv = env.w(N.qkv), env.w(N.aqkv)
        turned = rotate_back(env[N.dkv][:, : sizes.HD].astype(F32), cos, sin)
        back, gain = rms_back(env[N.raw(l)][sizes.H], env[N.qkg][5:6, :], turned)
        env[N.dkg(l)][...] = gain
        total = env[N.agrad(l)][...]
        for j, (low, second) in enumerate(((back.astype(BF), N.bk), (env[N.dkv][:, sizes.HD :], N.bv))):
            env[N.rawkv_low(l)][j] = low
            mid = dot_nt(low, columns(env.w(second), 0, hb)).astype(BF)
            env[N.midgkv(l)][j] = mid
            total = total + dot_nt(low, columns(qkv, hb * (sizes.H + j), hb))
            total = total + dot_nt(mid, columns(aqkv, sizes.RB * (j + 1), sizes.RB))
        back, gain = rms_back(env[stream][...], env[N.norm][0:1, :], total)
        env[N.dnorm(l, 0)][...] = gain
        env[result][...] = env[N.mgrad(l)][...] + back

    return stage


def put(sizes, env, layout, prefix, name, block, value, first_row=0):
    first, rows, _ = layout.at[name]
    count = value.shape[1] // LANES
    keep = env[N.keep(prefix)]
    if sizes.slots == 1:
        value = value.astype(BF)
        for i in range(count):
            at = first + (block + i) * rows + first_row
            keep[0, at : at + value.shape[0], :] = value[:, i * LANES : (i + 1) * LANES]
        return
    send = env[N.send(prefix)]
    core, chip = env[N.place][0], env[N.place][1]
    even_stays = core == 0
    for pair in range(value.shape[0] // (2 * rows)):
        a = value[2 * pair * rows : (2 * pair + 1) * rows]
        b = value[(2 * pair + 1) * rows : (2 * pair + 2) * rows]
        stays = jnp.where(even_stays, a, b).astype(BF)
        goes = jnp.where(even_stays, b, a).astype(BF)
        slot = jnp.bitwise_xor(first_row // (2 * rows) + pair, chip)
        for i in range(count):
            at = first + (block + i) * rows
            keep[slot, at : at + rows, :] = stays[:, i * LANES : (i + 1) * LANES]
            send[slot, at : at + rows, :] = goes[:, i * LANES : (i + 1) * LANES]


def grad_product(sizes, env, layout, prefix, name, lefts, rights, first_block=0, first_row=0):
    left = stacked([a.T if len(lefts) == 1 else a.T for a in lefts]) if len(lefts) == 1 else side_by_side(
        [a.T for a in lefts]
    )
    for block, right in rights:
        value = dot(left, stacked(right))
        put(sizes, env, layout, prefix, name, first_block + block, value, first_row)


def wide(ref, width, step=256):
    out = []
    at = 0
    while at < width:
        size = min(step, width - at)
        out.append((at // LANES, slice(at, at + size)))
        at += size
    return out


def grads_ffn_wide(sizes, env, layout, prefix, names, loops, pl_l):
    blocks = sizes.F // 256
    for j, name in enumerate((N.gug, N.guu)):
        if name in names:
            left = [env[N.ffn_in(l)][...] for l in loops]
            rights = [(2 * b, [env[N.gug(l)][j * blocks + b] for l in loops]) for b in range(blocks)]
            grad_product(sizes, env, layout, prefix, name, left, rights)
    if N.agu in names:
        rights = [(sizes.RB * j, [env[N.gmg(pl_l)][j]]) for j in range(2)]
        grad_product(sizes, env, layout, prefix, N.agu, [env[N.ffn_in(pl_l)][...]], rights)
    for j, name in enumerate((N.bg, N.bu)):
        if name in names:
            rights = [(2 * b, [env[N.gug(pl_l)][j * blocks + b]]) for b in range(blocks)]
            grad_product(sizes, env, layout, prefix, name, [env[N.gmid(pl_l)][j]], rights)


def grads_ffn_down(sizes, env, layout, prefix, names, loops, pl_l):
    blocks = sizes.F // 256
    step = 512
    for b in range(0, blocks, 2):
        row = b * 256
        if N.dnw in names:
            left = [side_by_side([env[N.hidden(l)][b], env[N.hidden(l)][b + 1]]) for l in loops]
            rights = [(i, [env[N.ffn_low(l)][:, s] for l in loops]) for i, s in wide(None, sizes.D, 640)]
            grad_product(sizes, env, layout, prefix, N.dnw, left, rights, 0, row)
        if N.dna in names:
            left = [side_by_side([env[N.hidden(pl_l)][b], env[N.hidden(pl_l)][b + 1]])]
            grad_product(sizes, env, layout, prefix, N.dna, left, [(0, [env[N.dmg(pl_l)][...]])], 0, row)
    if N.dnb in names:
        grad_product(
            sizes, env, layout, prefix, N.dnb, [env[N.dmid(pl_l)][...]], [(0, [env[N.ffn_low(pl_l)][...]])]
        )


def grads_out(sizes, env, layout, prefix, names, loops, pl_l):
    for h in range(0, sizes.H, 2):
        row = h * sizes.HD
        if N.outw in names:
            left = [side_by_side([env[N.ho(l)][h], env[N.ho(l)][h + 1]]) for l in loops]
            grad_product(
                sizes, env, layout, prefix, N.outw, left, [(0, [env[N.blow(l)][...] for l in loops])], 0, row
            )
        if N.outa in names:
            left = [side_by_side([env[N.ho(pl_l)][h], env[N.ho(pl_l)][h + 1]])]
            grad_product(sizes, env, layout, prefix, N.outa, left, [(0, [env[N.omg(pl_l)][...]])], 0, row)
    if N.outb in names:
        grad_product(
            sizes, env, layout, prefix, N.outb, [env[N.omid(pl_l)][...]], [(0, [env[N.blow(pl_l)][...]])]
        )


def grads_qkv(sizes, env, layout, prefix, names, loops, pl_l):
    hb = sizes.HB
    left = [env[N.attn_in(l)][...] for l in loops] if {N.qkvq, N.qkvkv} & set(names) else None
    if N.qkvq in names:
        rights = [(hb * h, [env[N.rawq_low(l)][h] for l in loops]) for h in range(sizes.H)]
        grad_product(sizes, env, layout, prefix, N.qkvq, left, rights)
    if N.qkvkv in names:
        rights = [(hb * j, [env[N.rawkv_low(l)][j] for l in loops]) for j in range(2)]
        grad_product(sizes, env, layout, prefix, N.qkvkv, left, rights)
    first = ([(0, N.midgq(pl_l), None)] if {N.aqkv, N.aqkvq} & set(names) else []) + (
        [(sizes.RB * j, N.midgkv(pl_l), j) for j in range(2)] if {N.aqkv, N.aqkvkv} & set(names) else []
    )
    for name in (N.aqkv, N.aqkvq, N.aqkvkv):
        if name in names:
            rights = [
                (at + (sizes.RB if name == N.aqkv and j is not None else 0), [env[ref][...] if j is None else env[ref][j]])
                for at, ref, j in first
            ]
            grad_product(sizes, env, layout, prefix, name, [env[N.attn_in(pl_l)][...]], rights)
    if N.bq in names:
        rights = [(hb * h, [env[N.rawq_low(pl_l)][h]]) for h in range(sizes.H)]
        grad_product(sizes, env, layout, prefix, N.bq, [env[N.mid(pl_l)][0]], rights)
    for j, name in enumerate((N.bk, N.bv)):
        if name in names:
            grad_product(
                sizes, env, layout, prefix, name, [env[N.mid(pl_l)][j + 1]], [(0, [env[N.rawkv_low(pl_l)][j]])]
            )


def stage_grads(sizes, parts):
    def stage(env):
        for prefix, layout, names, loops, pl_l in parts:
            for build in (grads_ffn_wide, grads_ffn_down, grads_out, grads_qkv):
                build(sizes, env, layout, prefix, names, loops, pl_l)

    return stage


def stage_gain_grads(sizes, prefix, layout):
    def stage(env):
        norm = stacked(
            [env[N.dnorm(0, i)][...] + env[N.dnorm(1, i)][...] for i in range(4)] + [jnp.zeros((12, sizes.D), F32)]
        )
        heads = stacked(
            [jnp.zeros((4, sizes.HD), F32)]
            + [env[kind(0)][...] + env[kind(1)][...] for kind in (N.dqg, N.dkg)]
            + [jnp.zeros((10, sizes.HD), F32)]
        )
        if sizes.slots == 1:
            env[N.gain_norm][...] = norm
            env[N.gain_heads][...] = heads
            return
        norm, heads = norm.astype(BF), heads.astype(BF)
        width, head_width = sizes.D // sizes.slots, sizes.HD // sizes.slots

        def pick(total, each, index):
            a = lax.broadcasted_iota(jnp.int32, (total, LANES), 0)
            b = lax.broadcasted_iota(jnp.int32, (total, LANES), 1)
            return jnp.where((a == b + index * each) & (b < each), 1.0, 0.0).astype(BF)

        at = layout.gains
        chip, core = env[N.place][1], env[N.place][0]
        for k in range(sizes.slots // 2):
            for name, flip in ((N.keep, core), (N.send, 1 - core)):
                index = 2 * jnp.bitwise_xor(k, chip) + flip
                block = dot(norm, pick(sizes.D, width, index)) + dot(heads, pick(sizes.HD, head_width, index))
                env[name(prefix)][k, at : at + 16, :] = block.astype(BF)

    return stage


def pack(sizes, layout, arrays, gains=None):
    names = list(layout.at)
    unique = []
    for name in names:
        if not any(arrays[name][0] is u for u in unique):
            unique.append(arrays[name][0])
    extra = [] if layout.gains is None else [gains]

    def kernel(*refs):
        out = refs[-1]
        for name in names:
            array, lead = arrays[name]
            source = refs[[array is u for u in unique].index(True)]
            first, rows, blocks = layout.at[name]
            for b in range(blocks):
                out[first + b * rows : first + (b + 1) * rows, :] = source[
                    lead + (slice(None), slice(b * LANES, (b + 1) * LANES))
                ]
        if layout.gains is not None:
            out[layout.gains : layout.gains + 16, :] = refs[len(unique)][...]

    return pl.pallas_call(
        kernel,
        name=N.pack,
        out_shape=jax.ShapeDtypeStruct((layout.total, LANES), BF),
        compiler_params=pltpu.CompilerParams(vmem_limit_bytes=VMEM_LIMIT),
        cost_estimate=pl.CostEstimate(flops=0, bytes_accessed=4 * layout.total * LANES, transcendentals=0),
    )(*unique, *extra)


def sort_rows(sizes, rank, *arrays):
    def kernel(rank_ref, *refs):
        count = len(refs) // 2
        place = lax.broadcasted_iota(jnp.int32, (sizes.T, sizes.T), 0)
        matrix = jnp.where(place == rank_ref[...], 1.0, 0.0).astype(BF)
        for source, target in zip(refs[:count], refs[count:]):
            target[...] = dot(matrix, source[...])

    return pl.pallas_call(
        kernel,
        name=N.sort_rows,
        out_shape=[jax.ShapeDtypeStruct(a.shape, F32) for a in arrays],
        compiler_params=pltpu.CompilerParams(vmem_limit_bytes=VMEM_LIMIT),
        cost_estimate=pl.CostEstimate(flops=0, bytes_accessed=2**21, transcendentals=0),
    )(rank, *arrays)


def unsort_rows(sizes, rank, value):
    def kernel(rank_ref, source, target):
        place = lax.broadcasted_iota(jnp.int32, (sizes.T, sizes.T), 0)
        matrix = jnp.where(place == rank_ref[...], 1.0, 0.0).astype(BF)
        target[...] = dot_tn(matrix, source[...].astype(BF)).astype(BF)

    return pl.pallas_call(
        kernel,
        name=N.unsort_rows,
        out_shape=jax.ShapeDtypeStruct(value.shape, BF),
        compiler_params=pltpu.CompilerParams(vmem_limit_bytes=VMEM_LIMIT),
        cost_estimate=pl.CostEstimate(flops=0, bytes_accessed=2**20, transcendentals=0),
    )(rank, value)


def unpack(sizes, targets, sources):
    names = list(sources)
    shapes = [jax.ShapeDtypeStruct(shape, F32) for shape, _ in targets]

    def kernel(*refs):
        ins = {name: refs[2 * i : 2 * i + 2] for i, name in enumerate(names)}
        outs = refs[2 * len(names) :]

        def rows_of(prefix, first, count):
            low, high = ins[prefix]
            first = first + sources[prefix][3]
            half = low.shape[0]
            if first + count <= half:
                return low[first : first + count, :].astype(F32)
            if first >= half:
                return high[first - half : first + count - half, :].astype(F32)
            return jnp.concatenate(
                [low[first:half, :].astype(F32), high[: first + count - half, :].astype(F32)], axis=0
            )

        for out, (_, parts) in zip(outs, targets):
            for lead, prefix, name, column in parts:
                layout = sources[prefix][2]
                if name == N.norm:
                    first, count = lead
                    out[...] = rows_of(prefix, layout.gains, 16)[first : first + count, : out.shape[1]]
                    continue
                first, rows, blocks = layout.at[name]
                for b in range(blocks):
                    out[lead + (slice(None), slice((column + b) * LANES, (column + b + 1) * LANES))] = rows_of(
                        prefix, first + b * rows, rows
                    )

    return pl.pallas_call(
        kernel,
        name=N.unpack,
        out_shape=shapes,
        compiler_params=pltpu.CompilerParams(vmem_limit_bytes=VMEM_LIMIT),
        cost_estimate=pl.CostEstimate(flops=0, bytes_accessed=2**22, transcendentals=0),
    )(*[half for name in names for half in sources[name][:2]])


def swap(sizes, value, bit):
    return lax.ppermute(value, "own", [(i, i ^ bit) for i in range(sizes.n)])


def along(value, pairs):
    return lax.ppermute(value, "dp", pairs)


def after_all(values, others):
    others = [o for o in others if not any(o is value for value in values)]
    count = len(values)

    def kernel(*refs):
        pass

    space = pl.BlockSpec(memory_space=pl.ANY)
    return pl.pallas_call(
        kernel,
        name=N.after,
        out_shape=[jax.ShapeDtypeStruct(value.shape, value.dtype) for value in values],
        in_specs=[space] * (count + len(others)),
        out_specs=[space] * count,
        input_output_aliases={i: i for i in range(count)},
        cost_estimate=pl.CostEstimate(flops=0, bytes_accessed=0, transcendentals=0),
    )(*values, *others)


def after(value, *others):
    return after_all([value], others)[0]


def gather_plain(sizes, mine, x_first, others=()):
    px, py = swap(sizes, mine, XBIT), swap(sizes, mine, YBIT)
    px = after(px, *others) if others else px
    pd = swap(sizes, px, YBIT) if x_first else swap(sizes, py, XBIT)
    here = [mine, px, py, pd]
    return here + [swap(sizes, piece, CORE) for piece in here]


def gather_direct(sizes, mine):
    here = [mine] + [swap(sizes, mine, bit) for bit in (XBIT, YBIT, XBIT | YBIT)]
    return here + [swap(sizes, piece, CORE) for piece in here]


PIECES = (0, XBIT, YBIT, XBIT | YBIT, CORE, CORE | XBIT, CORE | YBIT, CORE | XBIT | YBIT)


def gather_paired(sizes, mine, odd, others=()):
    px = swap(sizes, mine, XBIT)
    chosen = jnp.where(odd, px, mine)
    py = swap(sizes, after(chosen, *others) if others else chosen, YBIT)
    pz = along(py, [(0, 1), (1, 0), (2, 3), (3, 2)])
    here = [mine, px, py, pz]
    return here + [swap(sizes, piece, CORE) for piece in here]


def add(first, *others):
    total = first.astype(F32)
    for other in others:
        total = total + other.astype(F32)
    return total.astype(BF)


class Sum:
    def __init__(self, sizes, keep, send, mode, odd=None):
        self.sizes, self.keep, self.mode, self.odd = sizes, keep, mode, odd
        self.payload, self.done = [send], []
        self.steps = [self.core] + ([self.direct] if mode == N.direct else [self.near, self.far])
        self.steps += [self.trade, self.level, self.back]

    def step(self):
        now = self.steps.pop(0)
        now(self.payload)

    def swap(self, value, bit):
        return swap(self.sizes, value, bit)

    def core(self, sent):
        here, come = self.keep, self.swap(sent[0], CORE)
        if self.mode == N.direct:
            self.keep, *self.payload = [add(here[k], come[k]) for k in range(4)]
            return
        if self.mode == N.x:
            here, come = [a.reshape((2, 2) + a.shape[1:]) for a in (here, come)]
            pairs = [(here[:, i], come[:, i]) for i in range(2)]
        else:
            pairs = [(here[i : i + 2], come[i : i + 2]) for i in (0, 2)]
        self.keep, self.payload = add(*pairs[0]), [add(*pairs[1])]

    def direct(self, sent):
        come = [self.swap(value, bit) for value, bit in zip(sent, (XBIT, YBIT, XBIT | YBIT))]
        self.level_in(add(self.keep, *come))

    def near(self, sent):
        come = self.swap(sent[0], XBIT if self.mode == N.x else YBIT)
        self.keep, self.payload = add(self.keep[0], come[0]), [add(self.keep[1], come[1])]

    def far(self, sent):
        self.level_in(add(self.keep, self.swap(sent[0], YBIT if self.mode == N.x else XBIT)))

    def level_in(self, total):
        self.plane_total = total
        if self.odd is None:
            self.payload = [total]
            return
        rows = total.shape[0] // 2
        low, high = total[:rows], total[rows:]
        self.keep, self.payload = jnp.where(self.odd, high, low), [jnp.where(self.odd, low, high)]

    @staticmethod
    def joined(a, b):
        both = Sum(a.sizes, None, None, N.direct, a.odd)
        both.steps = both.steps[-3:]
        both.level_in(jnp.concatenate([a.plane_total, b.plane_total], axis=0))
        return both

    def trade(self, sent):
        self.payload = [add(self.keep, along(sent[0], [(0, 1), (1, 0), (2, 3), (3, 2)]))]

    def level(self, sent):
        self.payload = [add(sent[0], along(sent[0], [(0, 2), (2, 0), (1, 3), (3, 1)]))]

    def back(self, sent):
        come = along(sent[0], [(0, 1), (1, 0), (2, 3), (3, 2)])
        self.halves = (jnp.where(self.odd, come, sent[0]), jnp.where(self.odd, sent[0], come))
        self.payload = list(self.halves)


def make_shards(mesh):
    n, planes = mesh.shape["own"], mesh.shape["dp"]
    fast = n == 8 and planes == 4

    def shards(
        tokens,
        cotangent,
        lengths,
        row_packed_slot,
        shared_attention_matrix,
        shared_output_matrix,
        shared_gate_up_matrix,
        shared_down_matrix,
        norm_gain_table,
        query_key_gains,
        adapter_attention_first,
        adapter_query_second,
        adapter_key_value_second,
        adapter_output_first,
        adapter_output_second,
        adapter_gate_first,
        adapter_gate_second,
        adapter_down_first,
        adapter_down_second,
    ):
        s = Sizes()
        s.n, s.slots = n, (8 if fast else 1)
        s.T, s.D = tokens.shape
        s.HD = adapter_key_value_second.shape[3]
        s.H = adapter_query_second.shape[2] // s.HD
        s.R = adapter_query_second.shape[1] * n
        s.F = shared_down_matrix.shape[0] * n
        s.DB, s.RB, s.HB = s.D // LANES, s.R // LANES, s.HD // LANES
        s.IB = max(16, 1024 // n)
        s.QB = s.T // 4
        s.kv_pieces = 8 if fast else 1
        QW, k = s.H * s.HD, s.slots
        s.shard = {
            N.qkv: (s.D // k, (QW + 2 * s.HD) // LANES),
            N.aqkv: (s.D // k, 3 * s.RB),
            N.gug: (s.D // k, s.F // LANES),
            N.guu: (s.D // k, s.F // LANES),
            N.qkvq: (s.D // k, QW // LANES),
            N.qkvkv: (s.D // k, 2 * s.HB),
            N.aqkvq: (s.D // k, s.RB),
            N.aqkvkv: (s.D // k, 2 * s.RB),
            N.bq: (s.R // k, QW // LANES),
            N.bk: (s.R // k, s.HB),
            N.bv: (s.R // k, s.HB),
            N.outw: (QW // k, s.DB),
            N.outa: (QW // k, s.RB),
            N.outb: (s.R // k, s.DB),
            N.gu: (s.D // k, 2 * s.F // LANES),
            N.agu: (s.D // k, 2 * s.RB),
            N.bg: (s.R // k, s.F // LANES),
            N.bu: (s.R // k, s.F // LANES),
            N.dnw: (s.F // k, s.DB),
            N.dna: (s.F // k, s.RB),
            N.dnb: (s.R // k, s.DB),
        }
        own, plane = lax.axis_index("own"), lax.axis_index("dp")

        plain_ids = jnp.stack([own ^ m for m in PIECES]).astype(jnp.int32) if fast else jnp.zeros((1,), jnp.int32)
        slots = row_packed_slot[0]
        seq = lengths[0]
        my_slots = lax.dynamic_slice_in_dim(slots, own * s.T, s.T)
        rank = (my_slots // n).reshape(1, s.T)
        rest = slots.reshape(n, s.T)[:, 0] % n
        my_rest = my_slots[0] % n
        counts = jnp.arange(seq.shape[0])
        ends = jnp.sum(jnp.where(counts[None, :] <= counts[:, None], seq[None, :], 0), axis=1)
        sorted_slots = n * jnp.arange(s.T, dtype=jnp.int32) + my_rest
        past = sorted_slots[:, None] >= ends[None, :]
        starts = jnp.sum(jnp.where(past, seq[None, :], 0), axis=1)
        position = sorted_slots - starts
        inverse = THETA ** (-jnp.arange(s.HD // 2, dtype=F32) * 2.0 / s.HD)
        angles = position.astype(F32)[:, None] * inverse[None, :]
        block_slots = s.IB * n
        first_block = starts.reshape(4, s.QB)[:, 0] // block_slots
        key_rest = rest
        if fast:
            key_rest = jnp.sum(
                jnp.where(plain_ids[:, None] == jnp.arange(n)[None, :], rest[None, :], 0), axis=1
            )
        along_rows = jnp.arange(s.T, dtype=jnp.int32).reshape(s.T // s.IB, 1, 1, s.IB) * n
        kslot = (along_rows + key_rest.reshape(1, 1, n, 1)).reshape(s.T // s.IB, 1, n * s.IB).astype(jnp.int32)
        stream0, cot = sort_rows(s, rank, tokens, cotangent)

        v = {
            N.cos: jnp.cos(angles),
            N.sin: jnp.sin(angles),
            N.qslot: sorted_slots.reshape(s.T, 1),
            N.qstart: starts.reshape(s.T, 1).astype(jnp.int32),
            N.kslot: kslot,
            N.stream0: stream0,
            N.cot: cot,
        }
        def full(array, axis):
            return array if fast else lax.all_gather(array, "own", axis=axis, tiled=True)

        w_att, w_out = full(shared_attention_matrix, 0), full(shared_output_matrix, 0)
        w_gu, w_dn = full(shared_gate_up_matrix, 0), full(shared_down_matrix, 0)
        a_att, b_q = full(adapter_attention_first, 1), full(adapter_query_second, 1)
        b_kv, a_out = full(adapter_key_value_second, 2), full(adapter_output_first, 1)
        b_out, a_gu = full(adapter_output_second, 1), full(adapter_gate_first, 1)
        b_gu, a_dn = full(adapter_gate_second, 2), full(adapter_down_first, 1)
        b_dn = full(adapter_down_second, 1)

        def arrays_of(l):
            return {
                N.qkv: (w_att, ()),
                N.aqkv: (a_att, (l,)),
                N.bq: (b_q, (l,)),
                N.bk: (b_kv, (l, 0)),
                N.bv: (b_kv, (l, 1)),
                N.outw: (w_out, ()),
                N.outa: (a_out, (l,)),
                N.outb: (b_out, (l,)),
                N.gu: (w_gu, ()),
                N.agu: (a_gu, (l,)),
                N.bg: (b_gu, (l, 0)),
                N.bu: (b_gu, (l, 1)),
                N.dnw: (w_dn, ()),
                N.dna: (a_dn, (l,)),
                N.dnb: (b_dn, (l,)),
            }

        q_names, o_names = (N.qkv, N.aqkv, N.bq, N.bk, N.bv), (N.outw, N.outa, N.outb)
        g_names, d_names = (N.gu, N.agu, N.bg, N.bu), (N.dnw, N.dna, N.dnb)
        lq_names, lr_names = (N.aqkv, N.bq, N.bk, N.bv), (N.outa, N.outb, N.agu, N.bg, N.bu, N.dna, N.dnb)
        odd = (plane & 1) == 1
        inner = (plane == 1) | (plane == 2)
        paired_ids = plain_ids
        if fast:
            over_y = jnp.where(odd, XBIT | YBIT, YBIT)
            over_z = jnp.where(odd, YBIT, XBIT | YBIT)
            order = [0, XBIT, over_y, over_z]
            paired_ids = jnp.stack([own ^ m for m in order] + [own ^ m ^ CORE for m in order]).astype(jnp.int32)
        gain_block = None
        if fast:
            gain_block = jnp.concatenate(
                [
                    jnp.pad(norm_gain_table, ((0, 0), (0, LANES - norm_gain_table.shape[1]))),
                    jnp.pad(query_key_gains, ((0, 0), (0, LANES - query_key_gains.shape[1]))),
                    jnp.zeros((10, LANES), BF),
                ],
                axis=0,
            )

        def packed(names, l, gains=False, of=()):
            layout = Layout(s, names, gains)
            arrays = {m: arrays_of(k)[m] for m, k in of} if of else arrays_of(l)
            return layout, pack(s, layout, arrays, gain_block)

        def fetch(made, scheme, start=None, turn=()):
            layout, mine = made
            if not fast:
                return Chunk(layout, [mine], plain_ids)
            if scheme == N.y:
                over = [after(mine, start.pieces[1]), after(mine, start.pieces[3])]
                px, py = swap(s, over[0], XBIT), swap(s, over[1], YBIT)
                here = [mine, px, py, swap(s, py, XBIT)]
                chunk = Chunk(layout, here + [swap(s, piece, CORE) for piece in here], plain_ids)
                chunk.gates = over
                return chunk
            if start is not None:
                mine = after(mine, *start)
            if scheme == N.whole:
                whole = Chunk(layout, [lax.all_gather(mine, "own", axis=0, tiled=True)], jnp.arange(n, dtype=jnp.int32))
                whole.mine = mine
                return whole
            if scheme == N.direct:
                return Chunk(layout, gather_direct(s, mine), plain_ids)
            if scheme == N.paired:
                return Chunk(layout, gather_paired(s, mine, odd, turn), paired_ids)
            return Chunk(layout, gather_plain(s, mine, scheme == N.x, turn), plain_ids)

        pack_g, pack_q = packed(g_names + d_names, 0), packed(q_names, 0, gains=fast)
        pack_lr = packed(lr_names, 1)
        first = [(m, 0) for m in o_names] + [(m, 1) for m in lq_names]
        pack_o = packed(o_names + lq_names, None, of=first)
        chunk_g = fetch(pack_g, N.whole)
        chunk_q = fetch(pack_q, N.x, None, (stream0, v[N.cos], pack_g[1], pack_o[1], pack_lr[1]))
        chunk_o = fetch(pack_o, N.y, chunk_q)
        chunk_lq = chunk_o
        if fast:
            v[N.stream0] = after(v[N.stream0], *chunk_o.gates)
        loop0 = {**{m: chunk_q for m in q_names}, **{m: chunk_o for m in o_names}}
        loop0 |= {m: chunk_g for m in g_names + d_names}
        of_loop = [loop0]

        def wts(names, l):
            return [(m, of_loop[l][m]) for m in names]

        T, D, HD, H, R, F = s.T, s.D, s.HD, s.H, s.R, s.F
        blocks = F // 256
        half = n // 2 if fast else n
        shapes = {
            N.norm: ((16, D), F32),
            N.qkg: ((16, HD), F32),
            N.stream1: ((T, D), F32),
            N.stream2: ((T, D), F32),
            N.o_acc: ((H * s.QB, HD), F32),
            N.l_acc: ((H * s.QB, LANES), F32),
            N.dkv_acc: ((T // s.IB, n * s.IB, 2 * HD), F32),
            N.sgrad1: ((T, D), F32),
            N.sgrad0: ((T, D), F32),
            N.gain_norm: ((16, D), F32),
            N.gain_heads: ((16, HD), F32),
        }
        for l in (0, 1):
            shapes |= {
                N.attn_in(l): ((T, D), BF),
                N.mid(l): ((3, T, R), BF),
                N.raw(l): ((H + 1, T, HD), F32),
                N.q(l): ((H, T, HD), BF),
                N.kv(l): ((T, 2 * HD), BF),
                N.att(l): ((H, T, HD), F32),
                N.lse(l): ((H, T, LANES), F32),
                N.ho(l): ((H, T, HD), BF),
                N.omid(l): ((T, R), BF),
                N.branch(l): ((T, D), F32),
                N.middle(l): ((T, D), F32),
                N.ffn_in(l): ((T, D), BF),
                N.gmid(l): ((2, T, R), BF),
                N.gu(l): ((blocks, T, 512), BF if l == 0 else F32),
                N.hidden(l): ((blocks, T, 256), BF),
                N.dmid(l): ((T, R), BF),
                N.ffn_out(l): ((T, D), F32),
                N.ffn_low(l): ((T, D), BF),
                N.dmg(l): ((T, R), BF),
                N.gug(l): ((2 * blocks, T, 256), BF),
                N.gmg(l): ((2, T, R), BF),
                N.mgrad(l): ((T, D), F32),
                N.blow(l): ((T, D), BF),
                N.omg(l): ((T, R), BF),
                N.hgrad(l): ((H, T, HD), BF),
                N.dq(l): ((H, T, HD), F32),
                N.dkvkeep(l): ((half, T, 2 * HD), BF),
                N.dkvsend(l): ((half, T, 2 * HD), BF),
                N.rawq_low(l): ((H, T, HD), BF),
                N.rawkv_low(l): ((2, T, HD), BF),
                N.midgq(l): ((T, R), BF),
                N.midgkv(l): ((2, T, R), BF),
                N.agrad(l): ((T, D), F32),
                N.dqg(l): ((1, HD), F32),
                N.dkg(l): ((1, HD), F32),
            }
            for i in range(4):
                shapes[N.dnorm(l, i)] = ((1, D), F32)

        def call(name, stages, ins, outs, scratch=(), weights=(), smem=(), micros=0, hold=None, early=()):
            made = run_kernel(
                s,
                name,
                stages,
                {m: v[m] for m in ins},
                {m: shapes[m] for m in outs},
                {m: shapes[m] for m in scratch},
                weights,
                {m: v[m] for m in smem},
                micros,
                hold,
                early,
            )
            v.update(made)

        v[N.first_block] = first_block.astype(jnp.int32)
        v[N.place] = jnp.stack([own & 1, own >> 1]).astype(jnp.int32)

        def share_kv(l):
            if fast:
                pieces = gather_direct(s, v[N.kv(l)])
            else:
                gathered = lax.all_gather(v[N.kv(l)], "own", axis=0, tiled=False)
                pieces = [gathered]
            for i, piece in enumerate(pieces):
                v[N.kvp(l, i)] = piece

        def kv_names(l):
            return [N.kvp(l, i) for i in range(s.kv_pieces)]

        qkv_outs = [N.attn_in, N.mid, N.raw, N.q, N.kv]

        def fill(names, l):
            return [m(l) for m in names]

        if fast:
            call(
                N.qkv0,
                [stage_gains(s, chunk_q), stage_qkv(s, 0, N.stream0)],
                [N.stream0, N.cos, N.sin],
                [N.norm, N.qkg] + fill(qkv_outs, 0),
                weights=[(N.gains, chunk_q)] + wts(q_names, 0),
                micros=6.5,
            )
        else:
            norm = lax.all_gather(norm_gain_table, "own", axis=1, tiled=True).astype(F32)
            heads = lax.all_gather(query_key_gains, "own", axis=1, tiled=True).astype(F32)
            v[N.norm] = jnp.pad(norm, ((0, 12), (0, 0)))
            v[N.qkg] = jnp.pad(heads, ((4, 10), (0, 0)))
            call(
                N.qkv0,
                [stage_qkv(s, 0, N.stream0)],
                [N.stream0, N.cos, N.sin, N.norm, N.qkg],
                fill(qkv_outs, 0),
                weights=wts(q_names, 0),
                micros=6.5,
            )
        share_kv(0)
        if fast:
            mine = after(pack_lr[1], v[N.kvp(0, 3)])
            here = [mine] + [swap(s, mine, bit) for bit in (XBIT, YBIT, XBIT | YBIT)]
        of_loop.append({**loop0, **{m: chunk_lq for m in lq_names}})
        att_ins = [N.qslot, N.qstart, N.kslot]
        out_outs = [N.att, N.lse, N.ho, N.omid, N.branch, N.middle, N.ffn_in]
        ffn_outs = [N.gmid, N.gu, N.hidden, N.dmid, N.ffn_out]
        call(
            N.loop0,
            [stage_attend(s, 0), stage_out(s, 0, N.stream0), stage_ffn(s, 0), stage_qkv(s, 1, N.stream1)],
            [N.stream0, N.q0, N.norm, N.qkg, N.cos, N.sin] + att_ins + kv_names(0),
            fill(out_outs + ffn_outs, 0) + [N.stream1] + fill(qkv_outs, 1),
            scratch=[N.o_acc, N.l_acc],
            weights=wts(o_names + (N.agu, N.gu, N.bg, N.bu) + d_names, 0)
            + wts((N.aqkv, N.qkv, N.bk, N.bv, N.bq), 1),
            smem=[N.first_block],
            micros=20,
            early={N.att0: 0, N.lse0: 0, N.ho0: 1, N.branch0: 1, N.middle0: 1, N.gu0: 2, N.hidden0: 2, N.ffn_out0: 2}
            if fast
            else (),
        )
        chunk_lr = Chunk(*pack_lr[:1], [pack_lr[1]], plain_ids)
        if fast:
            here = list(after_all(here, [v[N.stream1]]))
            chunk_lr.pieces = here + [swap(s, piece, CORE) for piece in here]
        of_loop[1] |= {m: chunk_lr for m in lr_names}
        share_kv(1)
        loop1 = [
            stage_attend(s, 1),
            stage_out(s, 1, N.stream1),
            stage_ffn(s, 1),
            stage_ffn_back(s, 1, N.cot),
            stage_out_back(s, 1),
        ]
        loop1_outs = (
            [N.stream2, N.mgrad1]
            + fill([N.ho, N.omid, N.ffn_in, N.gmid, N.hidden, N.dmid], 1)
            + fill([N.ffn_low, N.dmg, N.gug, N.gmg, N.blow, N.omg], 1)
            + [N.dnorm(1, 1), N.dnorm(1, 2), N.dnorm(1, 3)]
        )
        loop1_scratch = [N.o_acc, N.l_acc, N.branch1, N.middle1, N.gu1, N.ffn_out1]
        back_outs = [N.dq, N.dkvkeep] + ([N.dkvsend] if fast else [])
        kept = [N.att1, N.lse1, N.hgrad1]
        call(
            N.loop1,
            loop1 + ([stage_attend_back(s, 1)] if fast else []),
            [N.stream1, N.q1, N.norm, N.cot] + att_ins + kv_names(1),
            loop1_outs + (fill(back_outs, 1) if fast else kept),
            scratch=loop1_scratch + ([N.dkv_acc] + kept if fast else []),
            weights=wts(o_names + g_names + d_names, 1),
            smem=[N.first_block],
            micros=35,
            early={N.ho1: 1, N.hidden1: 2, N.stream2: 2, N.gug1: 3, N.mgrad1: 3} if fast else (),
        )
        if not fast:
            call(
                N.attend_back1,
                [stage_attend_back(s, 1)],
                [N.q1] + kept + att_ins + kv_names(1),
                fill(back_outs, 1),
                scratch=[N.o_acc, N.dkv_acc],
                smem=[N.first_block],
                micros=10,
            )

        plans = {
            N.la: [((N.bg, N.bu, N.agu, N.dna, N.dnb, N.outa, N.outb), 1)],
            N.g1: [((N.gug,), 0), ((N.aqkv,), 1)],
            N.g2: [((N.guu,), 0), ((N.bq, N.bk, N.bv), 1)],
            N.g3: [((N.dnw, N.agu), 0)],
            N.g4: [((N.bg, N.bu, N.dna, N.dnb), 0)],
            N.rb: [((N.outw, N.outa, N.outb, N.bq, N.qkvq, N.aqkvq), 0)],
            N.ra: [((N.qkvkv, N.aqkvkv, N.bk, N.bv), 0)],
        }
        modes = {N.la: N.direct, N.g1: N.x, N.g2: N.y, N.g3: N.x, N.g4: N.y, N.rb: N.direct, N.ra: N.direct}
        layouts = {}
        where = {}
        for m, parts in plans.items():
            layouts[m] = Layout(s, [name for names, _ in parts for name in names], gains=(m == N.ra and fast))
            shapes[N.keep(m)] = ((half if fast else 1, layouts[m].total, LANES), BF)
            shapes[N.send(m)] = shapes[N.keep(m)]
            where |= {(name, l): m for names, l in parts for name in names}

        def grads(names, ins, micros, extra=(), extra_outs=()):
            parts = []
            for m in names:
                parts += [(m, layouts[m], group, [0, 1], l) for group, l in plans[m]]
            outs = [end(m) for m in names for end in ((N.keep, N.send) if fast else (N.keep,))]
            call(
                N.grads(names[0]),
                [stage_grads(s, parts)] + list(extra),
                ins,
                outs + list(extra_outs),
                smem=[N.place] if fast else [],
                micros=micros,
            )

        sums = {}

        def open_sum(*names):
            for m in names:
                if fast:
                    sums[m] = Sum(s, v[N.keep(m)], v[N.send(m)], modes[m], odd)

        def join(m, a, b):
            if fast:
                sums[m] = Sum.joined(sums[a], sums[b])

        def open_kv(l):
            if fast:
                sums[N.dkv(l)] = Sum(s, v[N.dkvkeep(l)], v[N.dkvsend(l)], N.direct)
            else:
                keep = v[N.dkvkeep(l)].reshape(n * T, 2 * HD)
                v[N.dkv] = lax.psum_scatter(keep, "own", scatter_dimension=0, tiled=True)

        def close_kv(l):
            if fast:
                v[N.dkv] = sums[N.dkv(l)].payload[0]

        def phase(starts, inputs=(), need=()):
            if not fast:
                return
            starts, inputs = [sums[m] for m in starts], list(inputs)
            others = []
            for m in need:
                others += sums[m].payload if m in sums else [v[m]]
            values = after_all([p for r in starts for p in r.payload] + [v[m] for m in inputs], others)
            for r in starts:
                count = len(r.payload)
                r.payload, values = values[:count], values[count:]
            for m, value in zip(inputs, values):
                v[m] = value
            for r in starts:
                r.step()

        gain_ins = [N.dnorm(l, i) for l in (0, 1) for i in range(4)] + [N.dqg0, N.dqg1, N.dkg0, N.dkg1]
        qkv_l = [N.attn_in, N.mid, N.rawq_low, N.rawkv_low, N.midgq, N.midgkv]

        open_kv(1)
        phase([N.dkv1], [N.gmg1])
        grads(
            [N.la],
            [N.ffn_in1, N.gmid1, N.gug1, N.gmg1, N.hidden1, N.dmid1, N.ffn_low1, N.dmg1, N.ho1, N.omid1, N.blow1, N.omg1],
            8.6,
        )
        open_sum(N.la)
        phase([N.dkv1, N.la], [N.dq1])
        call(
            N.q_back1,
            [stage_q_back(s, 1)],
            [N.cos, N.sin, N.qkg, N.dq1, N.raw1],
            [N.rawq_low1, N.midgq1, N.agrad1, N.dqg1],
            weights=wts((N.qkv, N.bq, N.aqkv), 1),
            micros=5.8,
        )
        phase([N.la], [N.agrad1], [N.dkv1])
        close_kv(1)
        call(
            N.kv_back1,
            [stage_kv_back(s, 1, N.stream1, N.sgrad1), stage_ffn_back(s, 0, N.sgrad1)],
            [N.cos, N.sin, N.qkg, N.norm, N.dkv, N.raw1, N.agrad1, N.stream1, N.mgrad1]
            + [N.ffn_out0, N.gu0, N.middle0],
            [N.dkg1, N.rawkv_low1, N.midgkv1, N.dnorm(1, 0), N.dnorm(0, 3), N.dnorm(0, 2)]
            + fill([N.ffn_low, N.dmg, N.gug, N.gmg, N.mgrad], 0),
            scratch=[N.sgrad1],
            weights=wts((N.qkv, N.aqkv, N.bk, N.bv), 1) + wts((N.dnb, N.dnw, N.dna, N.bg, N.bu, N.gu, N.agu), 0),
            micros=17,
        )
        grads([N.g1, N.g2], fill([N.ffn_in, N.gug], 0) + [N.ffn_in1, N.gug1] + fill(qkv_l, 1), 9.7)
        open_sum(N.g1, N.g2)
        phase([N.g1, N.g2], [N.mgrad0], [N.la])
        call(
            N.out_back0,
            [stage_out_back(s, 0)],
            [N.branch0, N.norm, N.mgrad0],
            [N.dnorm(0, 1), N.blow0, N.omg0, N.hgrad0],
            weights=wts(o_names, 0),
            micros=4.5,
        )
        phase([N.g1, N.g2, N.la], [N.dmg0, N.hgrad0], [N.blow0])
        grads(
            [N.g3, N.g4],
            fill([N.ffn_in, N.gmid, N.gug, N.gmg, N.hidden, N.dmid, N.ffn_low, N.dmg], 0) + [N.hidden1, N.ffn_low1],
            8.5,
        )
        open_sum(N.g3, N.g4)
        if fast:
            v[N.hgrad0] = after(v[N.hgrad0], v[N.keep(N.g3)])
        call(
            N.attend_back0,
            [stage_attend_back(s, 0)],
            [N.hgrad0, N.q0, N.att0, N.lse0] + att_ins + kv_names(0),
            fill(back_outs, 0),
            scratch=[N.o_acc, N.dkv_acc],
            smem=[N.first_block],
            micros=13,
        )
        open_kv(0)
        phase([N.dkv0, N.g1, N.g2, N.la], [N.dq0])
        call(
            N.q_back0,
            [stage_q_back(s, 0)],
            [N.cos, N.sin, N.qkg, N.dq0, N.raw0],
            [N.rawq_low0, N.midgq0, N.agrad0, N.dqg0],
            weights=wts((N.qkv, N.bq, N.aqkv), 0),
            micros=5.8,
        )
        join(N.g12, N.g1, N.g2)
        phase([N.dkv0, N.g3, N.g4], [N.rawq_low0], [N.g12])
        grads(
            [N.rb],
            fill([N.ho, N.omid, N.blow, N.omg, N.mid, N.rawq_low, N.attn_in, N.midgq], 0)
            + [N.ho1, N.blow1, N.attn_in1, N.rawq_low1],
            7,
        )
        open_sum(N.rb)
        phase([N.g3, N.g4, N.rb, N.g12], [N.agrad0, N.stream2], [N.dkv0])
        close_kv(0)
        mixed = unsort_rows(s, rank, v[N.stream2])
        v[N.mixed] = mixed
        call(
            N.kv_back0,
            [stage_kv_back(s, 0, N.stream0, N.sgrad0)],
            [N.cos, N.sin, N.qkg, N.norm, N.dkv, N.raw0, N.agrad0, N.stream0, N.mgrad0],
            [N.dkg0, N.rawkv_low0, N.midgkv0, N.dnorm(0, 0), N.sgrad0],
            weights=wts((N.qkv, N.aqkv, N.bk, N.bv), 0),
            micros=6.2,
        )
        grads(
            [N.ra],
            fill([N.attn_in, N.mid, N.rawkv_low, N.midgkv], 0) + [N.attn_in1, N.rawkv_low1] + gain_ins,
            3,
            [stage_gain_grads(s, N.ra, layouts[N.ra])],
            [] if fast else [N.gain_norm, N.gain_heads],
        )
        open_sum(N.ra)
        tokens_grad = unsort_rows(s, rank, v[N.sgrad0])
        v[N.tokens_grad] = tokens_grad
        phase([N.g3, N.g4, N.ra, N.la], [], [N.mixed, N.tokens_grad, N.g12])
        join(N.g34, N.g3, N.g4)
        phase([N.rb, N.g12], [], [N.g34, N.ra])
        phase([N.ra, N.g34], [], [N.rb, N.g12])
        phase([N.ra, N.rb, N.g34, N.g12])
        phase([N.ra, N.rb, N.g34])
        phase([N.ra, N.rb])
        finished = {}
        for m in plans if fast else ():
            pair, first = {N.g1: (N.g12, 0), N.g2: (N.g12, N.g1), N.g3: (N.g34, 0), N.g4: (N.g34, N.g3)}.get(m, (m, 0))
            finished[m] = (*sums[pair].payload, layouts[m], layouts[first].total if first else 0)

        HB, RB = s.HB, s.RB
        two = (0, 1)
        targets = [
            (shared_attention_matrix.shape, [((), N.qkvq, 0, 0), ((), N.qkvkv, 0, H * HB)]),
            (shared_output_matrix.shape, [((), N.outw, 0, 0)]),
            (shared_gate_up_matrix.shape, [((), N.gug, 0, 0), ((), N.guu, 0, F // LANES)]),
            (shared_down_matrix.shape, [((), N.dnw, 0, 0)]),
            (
                adapter_attention_first.shape,
                [((0,), N.aqkvq, 0, 0), ((0,), N.aqkvkv, 0, RB), ((1,), N.aqkv, 1, 0)],
            ),
            (adapter_query_second.shape, [((l,), N.bq, l, 0) for l in two]),
            (
                adapter_key_value_second.shape,
                [((l, j), m, l, 0) for l in two for j, m in enumerate((N.bk, N.bv))],
            ),
            (adapter_output_first.shape, [((l,), N.outa, l, 0) for l in two]),
            (adapter_output_second.shape, [((l,), N.outb, l, 0) for l in two]),
            (adapter_gate_first.shape, [((l,), N.agu, l, 0) for l in two]),
            (adapter_gate_second.shape, [((l, j), m, l, 0) for l in two for j, m in enumerate((N.bg, N.bu))]),
            (adapter_down_first.shape, [((l,), N.dna, l, 0) for l in two]),
            (adapter_down_second.shape, [((l,), N.dnb, l, 0) for l in two]),
        ]
        if fast:
            plan = [(shape, [(lead, where[m, l], m, col) for lead, m, l, col in parts]) for shape, parts in targets]
            made = [None] * len(plan)
            early = [i for i, (_, parts) in enumerate(plan) if all(part[1][0] in N.lg for part in parts)]
            late = [i for i in range(len(plan)) if i not in early]
            ends = [
                (norm_gain_table.shape, [((0, 4), N.ra, N.norm, 0)]),
                (query_key_gains.shape, [((4, 2), N.ra, N.norm, 0)]),
            ]
            for which, last in ((early, []), (late, ends)):
                chosen = [plan[i] for i in which] + last
                used = sorted({part[1] for _, parts in chosen for part in parts})
                results = unpack(s, chosen, {m: finished[m] for m in used})
                for i, value in zip(which, results):
                    made[i] = value
            grads, (norm_grad, heads_grad) = made, results[-2:]
        else:

            def natural(name, l):
                layout = layouts[where[name, l]]
                first, rows, count = layout.at[name]
                block = v[N.keep(where[name, l])][0, first : first + rows * count]
                return block.reshape(count, rows, LANES).transpose(1, 0, 2).reshape(rows, count * LANES)

            def reduced(value, axis):
                part = lax.psum_scatter(value.astype(BF), "own", scatter_dimension=axis, tiled=True)
                return lax.psum(part, "dp").astype(F32)

            grads = []
            for shape, parts in targets:
                of_lead = {}
                for lead, m, l, _ in parts:
                    of_lead.setdefault(lead, []).append(natural(m, l))
                value = jnp.stack([side_by_side(columns_of) for columns_of in of_lead.values()])
                value = value.reshape(shape[:-2] + value.shape[1:])
                grads.append(reduced(value, len(shape) - 2))
            norm_grad = reduced(v[N.gain_norm][:4], 1)
            heads_grad = reduced(v[N.gain_heads][4:6], 1)
        return (mixed, tokens_grad) + tuple(grads[:4]) + (norm_grad, heads_grad) + tuple(grads[4:])

    return shards


def solution(mesh):
    both, rows = P(("dp", "own"), None), P("own", None)
    second, third = P(None, "own", None), P(None, None, "own", None)
    wide_gain = P(None, "own")
    in_specs = (
        (both, both, P("dp", None), P("dp", None), rows, rows, rows, rows, wide_gain, wide_gain)
        + (second, second, third, second, second, second, third, second, second)
    )
    out_specs = (
        (both, both, rows, rows, rows, rows, wide_gain, wide_gain)
        + (second, second, third, second, second, second, third, second, second)
    )
    return jax.shard_map(make_shards(mesh), mesh=mesh, in_specs=in_specs, out_specs=out_specs, check_vma=False)
```
